32 devices in a mesh: dp: 4 (over y, x), tensor: 8 (over z, core).
Axes of the slice: x: 2, y: 2, z: 4, core: 2. Of those that a mesh axis runs over, the one named last changes fastest.
Arguments:
- tokens: bfloat16 [2048, 2048], P(('dp', 'tensor')), may hold values from -40 to 40
- attn_gain: bfloat16 [2048], replicated, may hold values from 0.099609375 to 1.8984375
- moe_gain: bfloat16 [2048], replicated, may hold values from 0.099609375 to 1.8984375
- q_gain: bfloat16 [128], replicated, may hold values from 0.099609375 to 1.8984375
- k_gain: bfloat16 [128], replicated, may hold values from 0.099609375 to 1.8984375
- query_weight: bfloat16 [2048, 4096], P(None, 'tensor'), may hold values from -0.125 to 0.125
- w_kv: bfloat16 [256, 4, 2048], P('tensor'), may hold values from -0.125 to 0.125
- w_o: bfloat16 [4096, 2048], P('tensor'), may hold values from -0.5 to 0.5
- w_gate: bfloat16 [64, 768, 2048], P('tensor'), may hold values from -0.125 to 0.125
- w_up: bfloat16 [64, 768, 2048], P('tensor'), may hold values from -0.125 to 0.125
- w_down: bfloat16 [64, 768, 2048], P('tensor'), may hold values from -0.21875 to 0.21875
- shrink_qkv: bfloat16 [16, 48, 2048], P('dp'), may hold values from -0.125 to 0.125
- shrink_o: bfloat16 [16, 16, 4096], P(None, None, 'tensor'), may hold values from -0.5 to 0.5
- query_up_factors: bfloat16 [16, 16, 4096], P(None, None, 'tensor'), may hold values from -1.5 to 1.5
- key_value_up_factors: bfloat16 [16, 16, 1024], replicated, may hold values from -1.5 to 1.5
- expand_o: bfloat16 [16, 16, 2048], replicated, may hold values from -1.5 to 1.5
- lengths: int32 [4, 32], P('dp'), may hold values from 1 to 256, 512 in all within a row
- groups: int32 [4, 32], P('dp'), may hold values from 0 to 3, never falling along the last dimension, each value on 1 to 16 neighbouring positions
- adapter_of_request: int32 [4, 32], P('dp'), may hold values from 0 to 15
- adapter_slot: int32 [16], replicated, may hold values from 0 to 15, each once
- page_table: int32 [4, 64], P('dp'), may hold values from 0 to 63, each once within a row
- expert_ids: int32 [2048, 8], P('dp'), may hold values from 0 to 63, all different within a row; in each aligned block of 64 rows (0 to 63, 64 to 127, ...) at most 16 rows name the same one
- expert_gates: float32 [2048, 8], P('dp'), may hold values from 0.05 to 1
Outputs:
- attn_out: bfloat16 [2048, 2048], P(('dp', 'tensor'))
- moe_out: bfloat16 [2048, 2048], P(('dp', 'tensor'))
- kv_pages: bfloat16 [256, 1024, 128], P('dp', 'tensor')
The draws below stay inside these ranges and needn't reach their ends.
Inputs may be any that keep to these rules, and one draw needn't show every extreme that they name: `lengths`: each row sums to 512; its largest entry is exactly 256. `groups`: never falling along a row; each group holds 1 to 16 consecutive requests, one exactly 16. `adapter_slot`: A permutation; the factors of slots k * 16 / 4 to (k + 1) * 16 / 4 - 1 are held at dp index k. `page_table`: each row is a permutation of the pages of that token group's pool. `expert_ids`: A token's 8 experts are distinct; within each aligned block of 64 rows (the rows of one device) no expert is chosen by more than 16 tokens, a bound that some block reaches.
All inputs are finite; a program needn't handle non-finite values.
Results may differ from the reference program's by a relative error of at most 0.025.
Values may be sent and summed in bfloat16 or wider, within the bound.
No kernel may reach another device: no remote copies, remote signals or barrier semaphores. Data moves between devices by JAX's collectives and lax.ppermute only.
A program may use at most 192 MiB of HBM per device.

```python
import math
import jax
import jax.numpy as jnp
import numpy as np
from jax import lax

D = 2048
QUERY_HEADS = 32
KEY_VALUE_HEADS = 4
HEAD_DIM = 128
EXPERTS = 64
FF = 768
TOPK = 8
FACTOR_RANK = 16
ADAPTER_COUNT = 16
REQ = 32
GROUPS = 4
GMAX = 16
PAGE = 128
TOK_DEV = 64
CAP_DEV = 16
GROUP_TOKENS = 512
TOKENS = 2048
QUERY_WIDTH = 4096
KVW = 1024
LMAX = 256
PAGES_DP = 64
PAGES = 256
CAP = 128
N_DP = 4
N_TENSOR = 8


def draw_tokens(key, part):
    key_rows, key_cols, key_base = jax.random.split(key, 3)
    row_scale = jnp.exp(jax.random.uniform(key_rows, (TOKENS, 1), jnp.float32, math.log(0.3), math.log(3.0)))
    col_scale = jnp.exp(jax.random.uniform(key_cols, (1, D), jnp.float32, math.log(0.3), math.log(3.0)))
    base = jax.random.normal(key_base, (TOKENS, D), jnp.float32)
    return jnp.clip(base * row_scale * col_scale, -40.0, 40.0).astype(jnp.bfloat16)


def touch_ends(drawn, rng, low, largest):
    longest = drawn.shape.index(max(drawn.shape))
    spots = []
    for shift in (0, 1):
        where = [jax.random.randint(jax.random.fold_in(rng, axis), (), 0, length) for axis, length in enumerate(drawn.shape)]
        where[longest] = (where[longest] + shift) % drawn.shape[longest]
        spots.append(tuple(where))
    return drawn.at[spots[0]].set(low).at[spots[1]].set(largest)


def block_scale(rng, dims, cuts, low, largest):
    def one(dim, blocks):
        heights = jax.random.uniform(jax.random.fold_in(jax.random.fold_in(rng, 6), dim), (blocks,), jnp.float32, low / len(cuts), largest / len(cuts))
        return jnp.repeat(jnp.exp(heights), dims[dim] // blocks).reshape((-1,) + (1,) * (len(dims) - dim - 1))

    level = one(*cuts[0])
    for cut in cuts[1:]:
        level = level * one(*cut)
    return level


def split_up(number_of, total, limit, skew):
    weights = [(1 << 20) // math.isqrt(rank ** skew) + 1 for rank in range(2, number_of + 1)]
    surplus, given = total - limit - (number_of - 1), [1] * (number_of - 1)
    while surplus > 0:
        free = [i for i in range(number_of - 1) if given[i] < limit]
        whole, budget = sum([weights[i] for i in free]), surplus
        for i in free:
            addition = min(limit - given[i], max(1, budget * weights[i] // whole), surplus)
            given[i] = given[i] + addition
            surplus = surplus - addition
    return np.array([limit] + given)


def ragged(key, number_of, total, bound, lean):
    if number_of == 2:
        one = jax.random.randint(key, (), max(1, total - bound), min(bound, total - 1) + 1)
        return jnp.stack([one, total - one])
    tallies = jnp.asarray(split_up(number_of, total, bound, lean), jnp.int32)
    pairs = (number_of - 1) // 2
    source_of, receiver = tallies[1:1 + 2 * pairs:2], tallies[2:2 + 2 * pairs:2]
    room = jnp.minimum(source_of - 1, bound - receiver)
    moved = jax.random.randint(jax.random.fold_in(key, 1), (pairs,), 0, 1 << 20) % (room + 1)
    tallies = tallies.at[1:1 + 2 * pairs:2].set(source_of - moved).at[2:2 + 2 * pairs:2].set(receiver + moved)
    return tallies[jax.random.permutation(jax.random.fold_in(key, 2), number_of)]


def routed_block(stream_key, own, number, rows, number_of, top, reach, skew):
    ranking = jax.random.permutation(stream_key, number_of)
    packed, common = portions_of(number_of, rows * top, reach, skew, True), portions_of(number_of, rows * top, reach, skew, False)
    places = jnp.arange(number_of)

    def named(sizes, rotation):
        used = int((sizes > 0).sum())
        fixed = max(1, used // 4)
        shifted = fixed + (places - fixed + rotation * (used - fixed)) % max(1, number_of - fixed)
        return jnp.zeros((number_of,), jnp.int32).at[ranking[jnp.where(places < fixed, places, shifted)]].set(jnp.asarray(sizes, jnp.int32))

    sizes = jnp.where(number % 4 == 0, named(packed, number // 4), named(common, number - number // 4 - 1))
    mixed = jax.random.permutation(jax.random.fold_in(own, 3), number_of)
    source_of, sink = mixed[0:number_of // 2 * 2:2], mixed[1:number_of // 2 * 2:2]
    room = jnp.minimum(sizes[source_of] - 1, reach - sizes[sink]) // 2
    room = jnp.where((source_of == ranking[0]) | (sink == ranking[0]) | (sizes[sink] == 0), 0, jnp.maximum(room, 0))
    shifted = jax.random.randint(jax.random.fold_in(own, 4), (number_of // 2,), 0, 1 << 20) % (room + 1)
    sizes = sizes.at[source_of].add(-shifted).at[sink].add(shifted)
    items = jnp.searchsorted(jnp.cumsum(sizes), jnp.arange(rows * top), side="right").astype(jnp.int32)
    table = items.reshape(top, rows).T
    table = table[jax.random.permutation(jax.random.fold_in(own, 1), rows)]
    rotation = jax.random.randint(jax.random.fold_in(own, 2), (rows, 1), 0, top)
    return jnp.take_along_axis(table, (jnp.arange(top)[None, :] + rotation) % top, axis=1)


def portions_of(number_of, total, bound, slope, full):
    portions = [(1 << 20) // math.isqrt(rank ** slope) + 1 for rank in range(1, number_of + 1)]
    largest = bound if full else min(bound, max(-(-total // number_of), total * portions[0] // sum(portions)))
    least = 1 if total - largest >= number_of - 1 else 0
    given, rest = [largest] + [least] * (number_of - 1), total - largest - least * (number_of - 1)
    while rest > 0:
        movable = [i for i in range(1, number_of) if given[i] < largest] or [i for i in range(1, number_of) if given[i] < bound]
        whole, left = sum([portions[i] for i in movable]), rest
        for i in movable:
            extra = min(bound - given[i], max(1, left * portions[i] // whole), rest)
            given[i] = given[i] + extra
            rest = rest - extra
    return np.array(given)


def bell_draw(rng, extent, width, bound, cuts=(), held_as=jnp.bfloat16):
    values = width * jax.random.normal(rng, extent, jnp.float32)
    if cuts:
        values = values * block_scale(rng, extent, cuts, -0.22, 0.18)
    return jnp.clip(values, -bound, bound).astype(held_as)


def setup_inputs(seed: int = 0) -> dict:
    key_list = jax.random.split(jax.random.key(seed), 24)
    tokens = draw_tokens(jax.random.fold_in(key_list[23], 71), 0)
    attn_gain = jnp.clip(1.0 + 0.18 * jax.random.normal(key_list[1], (D,), jnp.float32), 0.099609375, 1.8984375).astype(jnp.bfloat16)
    moe_gain = jnp.clip(1.0 + 0.18 * jax.random.normal(key_list[2], (D,), jnp.float32), 0.099609375, 1.8984375).astype(jnp.bfloat16)
    q_gain = jnp.clip(1.0 + 0.18 * jax.random.normal(key_list[3], (HEAD_DIM,), jnp.float32), 0.099609375, 1.8984375).astype(jnp.bfloat16)
    k_gain = jnp.clip(1.0 + 0.18 * jax.random.normal(key_list[4], (HEAD_DIM,), jnp.float32), 0.099609375, 1.8984375).astype(jnp.bfloat16)
    query_weight = bell_draw(key_list[5], (D, QUERY_WIDTH), D ** -0.5, 0.125, ((1, 8),))
    w_kv = bell_draw(key_list[6], (2 * HEAD_DIM, KEY_VALUE_HEADS, D), D ** -0.5, 0.125, ((0, 8),))
    w_o = bell_draw(key_list[7], (QUERY_WIDTH, D), HEAD_DIM ** -0.5, 0.5, ((0, 8),))
    w_gate = bell_draw(key_list[8], (EXPERTS, FF, D), D ** -0.5, 0.125, ((0, 8),))
    w_up = bell_draw(key_list[9], (EXPERTS, FF, D), D ** -0.5, 0.125, ((0, 8),))
    w_down = bell_draw(key_list[10], (EXPERTS, FF, D), FF ** -0.5, 0.21875, ((0, 8),))
    shrink_qkv = bell_draw(key_list[11], (ADAPTER_COUNT, 3 * FACTOR_RANK, D), D ** -0.5, 0.125, ((0, 4),))
    shrink_o = bell_draw(key_list[12], (ADAPTER_COUNT, FACTOR_RANK, QUERY_WIDTH), HEAD_DIM ** -0.5, 0.5, ((2, 8),))
    query_up_factors = bell_draw(key_list[13], (ADAPTER_COUNT, FACTOR_RANK, QUERY_WIDTH), FACTOR_RANK ** -0.5, 1.5, ((2, 8),))
    key_value_up_factors = bell_draw(key_list[14], (ADAPTER_COUNT, FACTOR_RANK, KVW), FACTOR_RANK ** -0.5, 1.5)
    expand_o = bell_draw(key_list[15], (ADAPTER_COUNT, FACTOR_RANK, D), FACTOR_RANK ** -0.5, 1.5)
    lengths = jax.vmap(lambda own: ragged(own, REQ, GROUP_TOKENS, LMAX, 2))(jax.random.split(key_list[16], N_DP)).reshape((N_DP, REQ)).astype(jnp.int32)
    groups = jax.vmap(lambda own: jnp.searchsorted(jnp.cumsum(ragged(own, GROUPS, REQ, GMAX, 2)), jnp.arange(REQ), side="right"))(jax.random.split(key_list[17], N_DP)).reshape((N_DP, REQ)).astype(jnp.int32)
    adapter_of_request = touch_ends(jax.random.randint(key_list[18], (N_DP, REQ), 0, ADAPTER_COUNT), jax.random.fold_in(key_list[18], 1), 0, ADAPTER_COUNT - 1).astype(jnp.int32)
    adapter_slot = jax.random.permutation(key_list[19], ADAPTER_COUNT).astype(jnp.int32)
    page_table = jax.vmap(lambda own: jax.random.permutation(own, PAGES_DP))(jax.random.split(key_list[20], N_DP)).reshape((N_DP, PAGES_DP)).astype(jnp.int32)
    expert_ids_keys = jax.random.split(jax.random.fold_in(key_list[21], 1), TOKENS // TOK_DEV)
    expert_ids_turns = jax.random.permutation(jax.random.fold_in(key_list[21], 3), TOKENS // TOK_DEV)
    expert_ids = jax.vmap(lambda own, number: routed_block(jax.random.fold_in(key_list[21], 2), own, number, TOK_DEV, EXPERTS, TOPK, CAP_DEV, 2))(expert_ids_keys, expert_ids_turns).reshape((TOKENS, TOPK))
    expert_gates = jnp.clip(jnp.exp(math.log(1.0) - 2.9957323 * jax.random.uniform(key_list[22], (TOKENS, TOPK), jnp.float32) ** block_scale(key_list[22], (TOKENS, TOPK), ((0, 4),), -0.2, 0.2)), 0.05, 1.0)
    return dict(tokens=tokens, attn_gain=attn_gain, moe_gain=moe_gain, q_gain=q_gain, k_gain=k_gain, query_weight=query_weight, w_kv=w_kv, w_o=w_o, w_gate=w_gate, w_up=w_up, w_down=w_down, shrink_qkv=shrink_qkv, shrink_o=shrink_o, query_up_factors=query_up_factors, key_value_up_factors=key_value_up_factors, expand_o=expand_o, lengths=lengths, groups=groups, adapter_of_request=adapter_of_request, adapter_slot=adapter_slot, page_table=page_table, expert_ids=expert_ids, expert_gates=expert_gates)


NORM_EPS = 1e-06
ROPE_BASE = 1000000.0
ADAPTER_FACTOR = 0.5

def normalize(values, gain):
    return values * lax.rsqrt(lax.optimization_barrier(jnp.mean(values * values, axis=-1, keepdims=True)) + NORM_EPS) * gain.astype(jnp.float32)

def rotate(values, position):
    half = values.shape[-1] // 2
    freq = jnp.exp(-jnp.arange(half, dtype=jnp.float32) * (2.0 * math.log(ROPE_BASE) / values.shape[-1]))
    angle = position.astype(jnp.float32)[:, None, None] * freq[None, None, :]
    cosine = jnp.cos(angle)
    sine = jnp.sin(angle)
    first = values[..., :half]
    second = values[..., half:]
    return jnp.concatenate([first * cosine - second * sine, second * cosine + first * sine], axis=-1)

def lookup(index_value, table):
    match = index_value[:, None] == jnp.arange(table.shape[0], dtype=jnp.int32)[None, :]
    return lax.optimization_barrier(jnp.sum(jnp.where(match, table[None, :], 0), axis=1)).astype(jnp.int32)

def token_layout(length_row, group_row, adapter_row, adapter_slot, page_row, grand_total):
    position = jnp.arange(grand_total, dtype=jnp.int32)
    ends = jnp.cumsum(length_row).astype(jnp.int32)
    starts = (ends - length_row).astype(jnp.int32)
    request = lax.optimization_barrier(jnp.sum((ends[None, :] <= position[:, None]).astype(jnp.int32), axis=1)).astype(jnp.int32)
    group = lookup(request, group_row)
    same = group_row[:, None] == group_row[None, :]
    group_first = lax.optimization_barrier(jnp.min(jnp.where(same, starts[None, :], grand_total), axis=1)).astype(jnp.int32)
    rope_pos = position - lookup(request, group_first)
    offset = position - lookup(request, starts)
    per_request = page_row.shape[0] // length_row.shape[0]
    page = lookup(request * per_request + offset // PAGE, page_row)
    cell = page * PAGE + offset % PAGE
    adapter_position = lookup(request, lookup(adapter_row, adapter_slot))
    return (group, rope_pos, cell, adapter_position)

def spread_rows(values, adapter_position, adapters):
    match = adapter_position[:, None] == jnp.arange(adapters, dtype=jnp.int32)[None, :]
    placed = jnp.where(match[:, :, None], values[:, None, :], jnp.zeros((), values.dtype))
    return placed.reshape(values.shape[0], -1)

def key_adapter_term(shrunken_rows, adapter_position, upward_columns, column_begin, head_length):
    adapters, rank, columns = upward_columns.shape
    table = upward_columns.reshape(adapters * rank, columns)
    key_part = jnp.dot(spread_rows(shrunken_rows[:, rank:2 * rank], adapter_position, adapters), table, preferred_element_type=jnp.float32)
    value_part = jnp.dot(spread_rows(shrunken_rows[:, 2 * rank:], adapter_position, adapters), table, preferred_element_type=jnp.float32)
    whether_key = (column_begin + jnp.arange(columns, dtype=jnp.int32)) % (2 * head_length) < head_length
    return jnp.where(whether_key[None, :], key_part, value_part)

def routing(chosen, gates, experts, capacity):
    token_count = chosen.shape[0]
    choose = chosen[:, :, None] == jnp.arange(experts, dtype=jnp.int32)[None, None, :]
    gates_f = gates.astype(jnp.float32)
    share = gates_f / lax.optimization_barrier(jnp.sum(gates_f, axis=1, keepdims=True))
    weight = lax.optimization_barrier(jnp.sum(jnp.where(choose, share[:, :, None], 0.0), axis=1))
    hit = jnp.any(choose, axis=1)
    place = (jnp.cumsum(hit.astype(jnp.int32), axis=0) - 1).astype(jnp.int32)
    column = jnp.where(hit, place, capacity)
    expert_grid = jnp.broadcast_to(jnp.arange(experts, dtype=jnp.int32)[None, :], hit.shape)
    token_grid = jnp.broadcast_to(jnp.arange(token_count, dtype=jnp.int32)[:, None], hit.shape)
    slot_token = jnp.zeros((experts, capacity + 1), jnp.int32).at[expert_grid, column].set(token_grid)[:, :capacity]
    slot_weight = jnp.zeros((experts, capacity + 1), jnp.float32).at[expert_grid, column].set(weight)[:, :capacity]
    return (slot_token, slot_weight)

def attend(query_rows_out, keys, values, group, scale):
    grand_total = query_rows_out.shape[0]
    block = min(512, grand_total)
    position = jnp.arange(grand_total, dtype=jnp.int32)

    def one_block(number):
        first = number * block
        query_block = lax.dynamic_slice_in_dim(query_rows_out, first, block, 0)
        rows_here = first + jnp.arange(block, dtype=jnp.int32)
        group_here = lax.dynamic_slice_in_dim(group, first, block, 0)
        allowed = (position[None, :] <= rows_here[:, None]) & (group[None, :] == group_here[:, None])
        scores = jnp.einsum('qhd,kd->hqk', query_block.astype(jnp.float32), keys.astype(jnp.float32)) * scale
        raised = jnp.where(allowed[None], jnp.exp(scores), 0.0)
        shares = (raised / lax.optimization_barrier(jnp.sum(raised, axis=-1, keepdims=True))).astype(jnp.bfloat16)
        mixed = jnp.einsum('hqk,kd->qhd', shares.astype(jnp.float32), values.astype(jnp.float32))
        return mixed.astype(jnp.bfloat16).reshape(block, -1)
    return lax.map(one_block, jnp.arange(grand_total // block, dtype=jnp.int32)).reshape(grand_total, -1)

def reference(tokens, attn_gain, moe_gain, q_gain, k_gain, query_weight, w_kv, w_o, w_gate, w_up, w_down, shrink_qkv, shrink_o, query_up_factors, key_value_up_factors, expand_o, lengths, groups, adapter_of_request, adapter_slot, page_table, expert_ids, expert_gates):
    heads_per_shard = QUERY_HEADS // N_TENSOR
    width_dev = heads_per_shard * HEAD_DIM
    kv_rows = w_kv.transpose(1, 0, 2).reshape(KVW, D)

    def one_group(items):
        x_rows, length_row, group_row, adapter_row, page_row, expert_row, gate_row = items
        group, rope_pos, cell, adapter_position = token_layout(length_row, group_row, adapter_row, adapter_slot, page_row, GROUP_TOKENS)
        normalized_input = normalize(x_rows.astype(jnp.float32), attn_gain).astype(jnp.bfloat16)
        projected = jnp.einsum('td,ard->tar', normalized_input.astype(jnp.float32), shrink_qkv.astype(jnp.float32))
        match = adapter_position[:, None] == jnp.arange(ADAPTER_COUNT, dtype=jnp.int32)[None, :]
        shrunken_rows = lax.optimization_barrier(jnp.sum(jnp.where(match[:, :, None], projected, 0.0), axis=1)).astype(jnp.bfloat16)
        query_rows_out = jnp.dot(normalized_input, query_weight, preferred_element_type=jnp.float32) + ADAPTER_FACTOR * jnp.dot(spread_rows(shrunken_rows[:, :FACTOR_RANK], adapter_position, ADAPTER_COUNT), query_up_factors.reshape(ADAPTER_COUNT * FACTOR_RANK, QUERY_WIDTH), preferred_element_type=jnp.float32)
        query_rows_out = rotate(normalize(query_rows_out.reshape(GROUP_TOKENS, QUERY_HEADS, HEAD_DIM), q_gain), rope_pos).astype(jnp.bfloat16)
        key_value_rows = lax.dot_general(normalized_input, kv_rows, (((1,), (1,)), ((), ())), preferred_element_type=jnp.float32)
        key_value_rows = (key_value_rows + ADAPTER_FACTOR * key_adapter_term(shrunken_rows, adapter_position, key_value_up_factors, 0, HEAD_DIM)).astype(jnp.bfloat16)
        divided_key_value = key_value_rows.reshape(GROUP_TOKENS, KEY_VALUE_HEADS, 2, HEAD_DIM)
        keys = rotate(normalize(divided_key_value[:, :, 0].astype(jnp.float32), k_gain), rope_pos).astype(jnp.bfloat16)
        values = divided_key_value[:, :, 1]
        entries = jnp.stack([keys, values], axis=2).reshape(GROUP_TOKENS, KVW)
        pages = jnp.zeros((PAGES_DP * PAGE, KVW), jnp.bfloat16).at[cell].set(entries)
        pages = pages.reshape(PAGES_DP, PAGE, KVW).transpose(0, 2, 1)
        retained_mask = jnp.repeat(match, FACTOR_RANK, axis=1)
        upward_wide_rows = expand_o.reshape(ADAPTER_COUNT * FACTOR_RANK, D).astype(jnp.float32)

        def head_group(carry, index_value):
            query_part = lax.dynamic_slice_in_dim(query_rows_out, index_value * heads_per_shard, heads_per_shard, 1)
            key_value_head = index_value * heads_per_shard // (QUERY_HEADS // KEY_VALUE_HEADS)
            key_part = lax.dynamic_index_in_dim(keys, key_value_head, 1, keepdims=False)
            value_part = lax.dynamic_index_in_dim(values, key_value_head, 1, keepdims=False)
            mixed = attend(query_part, key_part, value_part, group, HEAD_DIM ** (-0.5))
            out_rows = lax.dynamic_slice_in_dim(w_o, index_value * width_dev, width_dev, 0)
            shrink_part = lax.dynamic_slice_in_dim(shrink_o, index_value * width_dev, width_dev, 2).reshape(ADAPTER_COUNT * FACTOR_RANK, width_dev)
            lower_rank_rows = lax.dot_general(mixed, shrink_part, (((1,), (1,)), ((), ())), preferred_element_type=jnp.float32)
            adapter_contribution = jnp.dot(mixed, out_rows, preferred_element_type=jnp.float32)
            adapter_contribution = adapter_contribution + ADAPTER_FACTOR * jnp.dot(jnp.where(retained_mask, lower_rank_rows, 0.0), upward_wide_rows, precision=lax.Precision.HIGHEST)
            return (carry + lax.optimization_barrier(adapter_contribution.astype(jnp.bfloat16)).astype(jnp.float32), None)
        attn_total, unused = lax.scan(head_group, jnp.zeros((GROUP_TOKENS, D), jnp.float32), jnp.arange(N_TENSOR, dtype=jnp.int32))
        residual = x_rows.astype(jnp.float32) + attn_total
        moe_in = normalize(residual, moe_gain).astype(jnp.bfloat16)
        slot_token, slot_weight = routing(expert_row, gate_row, EXPERTS, CAP)

        def expert_step(carry, parts):
            token_list, weight_list, gate_rows, up_rows, down_rows = parts
            gathered = moe_in[token_list]
            gate_value = lax.dot_general(gathered, gate_rows, (((1,), (1,)), ((), ())), preferred_element_type=jnp.float32)
            up_value = lax.dot_general(gathered, up_rows, (((1,), (1,)), ((), ())), preferred_element_type=jnp.float32)
            hidden = (jax.nn.silu(gate_value) * up_value).astype(jnp.bfloat16)
            out = lax.optimization_barrier(jnp.dot(hidden, down_rows, preferred_element_type=jnp.float32).astype(jnp.bfloat16))
            return (carry.at[token_list].add(out.astype(jnp.float32) * weight_list[:, None]), None)
        moe_total, unused = lax.scan(expert_step, jnp.zeros((GROUP_TOKENS, D), jnp.float32), (slot_token, slot_weight, w_gate, w_up, w_down))
        return (attn_total.astype(jnp.bfloat16), moe_total.astype(jnp.bfloat16), pages)
    results = lax.map(one_group, (tokens.reshape(N_DP, GROUP_TOKENS, D), lengths, groups, adapter_of_request, page_table, expert_ids.reshape(N_DP, GROUP_TOKENS, TOPK), expert_gates.reshape(N_DP, GROUP_TOKENS, TOPK)))
    return (results[0].reshape(TOKENS, D), results[1].reshape(TOKENS, D), results[2].reshape(PAGES, KVW, PAGE))
```

```python
import functools
import math

import jax
import jax.numpy as jnp
from jax import lax
from jax.experimental import pallas as pl
from jax.experimental.pallas import tpu as pltpu
from jax.sharding import PartitionSpec as P

PAGE = 128
CAP_DEV = 16
NORM_EPS = 1e-06
ROPE_BASE = 1000000.0
ADAPTER_FACTOR = 0.5
MIB = 1 << 20
BF16 = jnp.bfloat16
F32 = jnp.float32
VMEM = pl.BlockSpec(memory_space=pltpu.VMEM)
SMEM = pl.BlockSpec(memory_space=pltpu.SMEM)
ANY = pl.BlockSpec(memory_space=pl.ANY)


def dot(a, b):
    return jnp.dot(a, b, preferred_element_type=F32)


def dot_nt(a, b):
    return lax.dot_general(a, b, (((1,), (1,)), ((), ())), preferred_element_type=F32)


def lookup(index_value, table):
    match = index_value[:, None] == jnp.arange(table.shape[0], dtype=jnp.int32)[None, :]
    return jnp.sum(jnp.where(match, table[None, :], 0), axis=1)


def loop(count, body, carry):
    if count <= 2:
        for i in range(count):
            carry = body(i, carry)
        return carry
    return lax.fori_loop(0, count, body, carry)


def rms(v, gain):
    return v * lax.rsqrt(jnp.mean(v * v, axis=-1, keepdims=True) + NORM_EPS) * gain


def norm_kernel(x_ref, gain_ref, out_ref):
    out_ref[...] = rms(x_ref[...].astype(F32), gain_ref[...].astype(F32)).astype(BF16)


def norm_rows(x, gain):
    return pl.pallas_call(
        norm_kernel,
        out_shape=jax.ShapeDtypeStruct(x.shape, BF16),
        in_specs=[VMEM, VMEM],
        out_specs=VMEM,
        name="norm_rows",
    )(x, gain.reshape(1, -1))


def residual_kernel(x_ref, gain_ref, *refs):
    parts, (attn_ref, out_ref) = refs[:-2], refs[-2:]
    total = parts[0][...].astype(F32)
    for part in parts[1:]:
        total = total + part[...].astype(F32)
    attn_ref[...] = total.astype(BF16)
    out_ref[...] = rms(x_ref[...].astype(F32) + total, gain_ref[...].astype(F32)).astype(BF16)


def residual_norm(x, gain, parts):
    shape = jax.ShapeDtypeStruct(x.shape, BF16)
    return pl.pallas_call(
        residual_kernel,
        out_shape=(shape, shape),
        in_specs=[VMEM] * (2 + len(parts)),
        out_specs=(VMEM, VMEM),
        name="residual_norm",
    )(x, gain.reshape(1, -1), *parts)


def pair_kernel(a_ref, b_ref, *outs):
    for i, out in enumerate(outs):
        out[...] = (a_ref[i].astype(F32) + b_ref[i].astype(F32)).astype(BF16)


def pair_sum(a, b):
    count = a.shape[0]
    shape = jax.ShapeDtypeStruct(a.shape[1:], BF16)
    return pl.pallas_call(
        pair_kernel,
        out_shape=(shape,) * count,
        in_specs=[VMEM, VMEM],
        out_specs=(VMEM,) * count,
        compiler_params=pltpu.CompilerParams(vmem_limit_bytes=40 * MIB),
        name="pair_sum",
    )(a, b)


def attention_kernel(
    factor_blocks,
    scal_ref,
    x_ref,
    wq_ref,
    wkv_ref,
    up_ref,
    wo_ref,
    sho_ref,
    exo_ref,
    meta_ref,
    row_ref,
    colslot_ref,
    oslot_ref,
    cos_ref,
    sin_ref,
    qg_ref,
    kg_ref,
    *refs,
):
    pieces, refs = refs[:factor_blocks], refs[factor_blocks:]
    own_ref, part_ref, kv_ref, s_ref, q_ref, o_ref, sems = refs
    rows, width = x_ref.shape
    query_cols = wq_ref.shape[1]
    head = qg_ref.shape[1]
    heads = query_cols // head
    block = min(256, rows)
    blocks = rows // block
    chips = own_ref.shape[0]
    own_rows = own_ref.shape[1]
    chip, core = scal_ref[0], scal_ref[1]
    copies = []
    for i, piece in enumerate(pieces):
        target = s_ref.at[pl.ds(scal_ref[2 + i], piece.shape[0])]
        copies.append(pltpu.make_async_copy(piece, target, sems.at[i]))
        copies[-1].start()
    for copy in copies:
        copy.wait()
    factors = s_ref.shape[0] * s_ref.shape[1]
    qg = qg_ref[...].astype(F32)
    kg = kg_ref[...].astype(F32)
    scale = head**-0.5

    def turned(v, gain, here):
        v = rms(v, gain)
        return v * cos_ref[here, :] + pltpu.roll(v, head // 2, 1) * sin_ref[here, :]

    def project(i, carry):
        here = pl.ds(pl.multiple_of(i * block, block), block)
        x = x_ref[here, :]
        low = dot_nt(x, s_ref[...].reshape(factors, width))
        slot = meta_ref[here, 0:1]
        low = jnp.where(slot == colslot_ref[...], low, 0.0).astype(BF16)
        delta = ADAPTER_FACTOR * dot(low, up_ref[...])
        q = dot(x, wq_ref[...]) + delta[:, :query_cols]
        kv = (dot_nt(x, wkv_ref[...]) + delta[:, query_cols:]).astype(BF16)
        for h in range(heads):
            cut = slice(h * head, (h + 1) * head)
            q_ref[here, cut] = turned(q[:, cut], qg, here).astype(BF16)
        kv_ref[here, :head] = turned(kv[:, :head].astype(F32), kg, here).astype(BF16)
        kv_ref[here, head:] = kv[:, head:]
        return carry

    loop(blocks, project, 0)

    def attend(i, carry):
        first = pl.multiple_of(i * block, block)
        here = pl.ds(first, block)
        group = meta_ref[here, 1:2]
        place = first + lax.broadcasted_iota(jnp.int32, (block, 1), 0)

        def keys(j, state):
            begin = pl.multiple_of(j * block, block)
            there = pl.ds(begin, block)
            spot = begin + lax.broadcasted_iota(jnp.int32, (1, block), 1)
            allowed = (spot <= place) & (row_ref[0:1, there] == group)
            k = kv_ref[there, :head]
            v = kv_ref[there, head:]
            new = []
            for h in range(heads):
                s = dot_nt(q_ref[here, h * head : (h + 1) * head], k) * scale
                raised = jnp.where(allowed, jnp.exp(s), 0.0)
                total, mixed = state[2 * h], state[2 * h + 1]
                new.append(total + jnp.sum(raised, axis=1, keepdims=True))
                new.append(mixed + dot(raised.astype(BF16), v))
            return tuple(new)

        state = (jnp.zeros((block, 1), F32), jnp.zeros((block, head), F32)) * heads
        if blocks <= 2:
            for j in range(i + 1):
                state = keys(j, state)
        else:
            state = lax.fori_loop(0, i + 1, keys, state)
        mixed = jnp.concatenate(
            [(state[2 * h + 1] / state[2 * h]).astype(BF16) for h in range(heads)], axis=1
        )
        low = dot_nt(mixed, sho_ref[...])
        low = jnp.where(meta_ref[here, 0:1] == oslot_ref[...], low, 0.0)
        high = low.astype(BF16)
        rest = (low - high.astype(F32)).astype(BF16)
        step = min(512, width)
        for c in range(0, width, step):
            cut = slice(c, c + step)
            expand = exo_ref[:, cut]
            term = dot(mixed, wo_ref[:, cut]) + ADAPTER_FACTOR * (
                dot(high, expand) + dot(rest, expand)
            )
            o_ref[:, cut] = term.astype(BF16)
        for b in range(block // own_rows):
            number = i * (block // own_rows) + b
            to = lax.rem(number // 2 - chip + chips, chips)

            @pl.when(core == b % 2)
            def _():
                own_ref[to] = o_ref[b * own_rows : (b + 1) * own_rows, :]

            @pl.when(core != b % 2)
            def _():
                part_ref[to] = o_ref[b * own_rows : (b + 1) * own_rows, :]

        return carry

    loop(blocks, attend, 0)


def attention(scal, x, weights, meta, pieces, adapters, chips, own_rows):
    rows, width = x.shape
    query_cols = weights[0].shape[1]
    head = weights[-1].shape[1]
    ranks = pieces[0].shape[1]
    block = min(256, rows)
    split = jax.ShapeDtypeStruct((chips, own_rows, width), BF16)
    flops = 2 * rows * (width * (adapters * ranks + query_cols + 2 * head) + 3 * query_cols * width)
    wq, wkv, up, wo, sho, exo, qg, kg = weights
    meta_col, meta_row, colslot, oslot, cos, sin = meta
    return pl.pallas_call(
        functools.partial(attention_kernel, len(pieces)),
        out_shape=(split, split, jax.ShapeDtypeStruct((rows, 2 * head), BF16)),
        in_specs=[SMEM] + [VMEM] * 15 + [ANY] * len(pieces),
        out_specs=(VMEM, VMEM, VMEM),
        scratch_shapes=[
            pltpu.VMEM((adapters, ranks, width), BF16),
            pltpu.VMEM((rows, query_cols), BF16),
            pltpu.VMEM((block, width), BF16),
            pltpu.SemaphoreType.DMA((len(pieces),)),
        ],
        compiler_params=pltpu.CompilerParams(vmem_limit_bytes=56 * MIB),
        cost_estimate=pl.CostEstimate(
            flops=flops, bytes_accessed=14 * MIB, transcendentals=rows * rows
        ),
        name="attention",
    )(scal, x, wq, wkv, up, wo, sho, exo, meta_col, meta_row, colslot, oslot, cos, sin, qg, kg, *pieces)


def pages_kernel(first_ref, length_ref, page_ref, entries_ref, out_ref):
    columns, extent = entries_ref.shape
    rows = extent - PAGE
    window = 2 * PAGE
    gap = lax.broadcasted_iota(jnp.int32, (window, PAGE), 0) - lax.broadcasted_iota(
        jnp.int32, (window, PAGE), 1
    )
    lane = lax.broadcasted_iota(jnp.int32, (columns, PAGE), 1)

    def one(n, carry):
        length = length_ref[n]
        page = page_ref[n]

        @pl.when(length > 0)
        def _():
            first = jnp.minimum(first_ref[n], rows - 1)
            base = pl.multiple_of(first // PAGE * PAGE, PAGE)
            pick = (gap == first - base).astype(F32).astype(BF16)
            moved = dot(entries_ref[:, pl.ds(base, window)], pick)
            out_ref[page] = jnp.where(lane < length, moved, 0.0).astype(BF16)

        @pl.when(length <= 0)
        def _():
            out_ref[page] = jnp.zeros((columns, PAGE), BF16)

        return carry

    lax.fori_loop(0, page_ref.shape[0], one, 0)


def fill_pages(first, length, page, entries):
    rows, columns = entries.shape
    count = page.shape[0]
    turned = jnp.pad(entries.T, ((0, 0), (0, PAGE)))
    return pl.pallas_call(
        pages_kernel,
        out_shape=jax.ShapeDtypeStruct((count, columns, PAGE), BF16),
        in_specs=[SMEM, SMEM, SMEM, VMEM],
        out_specs=VMEM,
        compiler_params=pltpu.CompilerParams(vmem_limit_bytes=32 * MIB),
        cost_estimate=pl.CostEstimate(
            flops=count * columns * PAGE * PAGE * 16, bytes_accessed=4 * MIB, transcendentals=0
        ),
        name="fill_pages",
    )(first, length, page, turned)


def experts_kernel(blocks, scal_ref, slot_ref, slot_t_ref, weight_ref, *refs):
    pieces, refs = refs[:blocks], refs[blocks:]
    gate_ref, up_ref, down_ref, out_ref, x_ref, rows_ref, y_ref, acc_ref, sems = refs
    e, f = pl.program_id(0), pl.program_id(1)
    count, parts = pl.num_programs(0), pl.num_programs(1)
    total, width = x_ref.shape
    experts = slot_ref.shape[1]
    capacity = rows_ref.shape[0] // experts
    tile = min(512, total)

    @pl.when((e == 0) & (f == 0))
    def _():
        copies = []
        for i, piece in enumerate(pieces):
            begin = pl.multiple_of(scal_ref[i], piece.shape[0])
            target = x_ref.at[pl.ds(begin, piece.shape[0])]
            copies.append(pltpu.make_async_copy(piece, target, sems.at[i]))
            copies[-1].start()
        for copy in copies:
            copy.wait()
        line = lax.broadcasted_iota(jnp.int32, (capacity, total), 0)
        for n in range(experts):
            pick = (slot_t_ref[n : n + 1, :] == line).astype(F32).astype(BF16)
            rows_ref[n * capacity : (n + 1) * capacity, :] = dot(pick, x_ref[...]).astype(BF16)

    here = pl.ds(pl.multiple_of(e * capacity, capacity), capacity)
    x = rows_ref[here, :]
    gate = dot_nt(x, gate_ref[0])
    up = dot_nt(x, up_ref[0])
    hidden = (gate / (1.0 + jnp.exp(-gate)) * up).astype(BF16)
    out = dot(hidden, down_ref[0])

    @pl.when(f == 0)
    def _():
        acc_ref[...] = out

    @pl.when(f > 0)
    def _():
        acc_ref[...] += out

    @pl.when(f == parts - 1)
    def _():
        y_ref[here, :] = acc_ref[...].astype(BF16)

    @pl.when((e == count - 1) & (f == parts - 1))
    def _():
        line = lax.broadcasted_iota(jnp.int32, (tile, capacity), 1)

        def mix(i, carry):
            these = pl.ds(pl.multiple_of(i * tile, tile), tile)
            spread = jnp.concatenate(
                [
                    jnp.where(
                        slot_ref[these, n : n + 1] == line, weight_ref[these, n : n + 1], 0.0
                    ).astype(BF16)
                    for n in range(experts)
                ],
                axis=1,
            )
            step = min(512, width)
            for c in range(0, width, step):
                out_ref[these, c : c + step] = dot(spread, y_ref[:, c : c + step]).astype(BF16)
            return carry

        loop(total // tile, mix, 0)


def expert_layer(scal, slot, slot_t, weight, pieces, gate, up, down, capacity):
    experts, hidden, width = gate.shape
    total = slot.shape[0]
    parts = 2
    part = hidden // parts
    whole = lambda e, f: (0, 0)
    streamed = pl.BlockSpec((1, part, width), lambda e, f: (e, f, 0))
    return pl.pallas_call(
        functools.partial(experts_kernel, len(pieces)),
        grid=(experts, parts),
        out_shape=jax.ShapeDtypeStruct((total, width), BF16),
        in_specs=[
            SMEM,
            pl.BlockSpec(slot.shape, whole),
            pl.BlockSpec(slot_t.shape, whole),
            pl.BlockSpec(weight.shape, whole),
        ]
        + [ANY] * len(pieces)
        + [streamed] * 3,
        out_specs=pl.BlockSpec((total, width), whole),
        scratch_shapes=[
            pltpu.VMEM((total, width), BF16),
            pltpu.VMEM((experts * capacity, width), BF16),
            pltpu.VMEM((experts * capacity, width), BF16),
            pltpu.VMEM((capacity, width), F32),
            pltpu.SemaphoreType.DMA((len(pieces),)),
        ],
        compiler_params=pltpu.CompilerParams(
            vmem_limit_bytes=60 * MIB, dimension_semantics=("arbitrary", "arbitrary")
        ),
        cost_estimate=pl.CostEstimate(
            flops=6 * experts * capacity * hidden * width,
            bytes_accessed=6 * experts * hidden * width,
            transcendentals=experts * capacity * hidden,
        ),
        name="experts",
    )(scal, slot, slot_t, weight, *pieces, gate, up, down)


def other_core(value, parts):
    return lax.ppermute(value, "tensor", [(i, i ^ 1) for i in range(parts)])


def turn_chips(value, parts, by):
    return lax.ppermute(value, "tensor", [(i, (i + 2 * by) % parts) for i in range(parts)])


def local(
    tokens,
    attn_gain,
    moe_gain,
    q_gain,
    k_gain,
    query_weight,
    w_kv,
    w_o,
    w_gate,
    w_up,
    w_down,
    shrink_qkv,
    shrink_o,
    query_up_factors,
    key_value_up_factors,
    expand_o,
    lengths,
    groups,
    adapter_of_request,
    adapter_slot,
    page_table,
    expert_ids,
    expert_gates,
):
    parts = lax.axis_size("tensor")
    place = lax.axis_index("tensor")
    holders = lax.axis_size("dp")
    holder = lax.axis_index("dp")
    chips, chip, core = parts // 2, place // 2, place % 2
    own_rows, width = tokens.shape
    total = own_rows * parts
    head_length = q_gain.shape[0]
    adapters, rank, kv_width = key_value_up_factors.shape
    kv_heads = kv_width // (2 * head_length)
    ranks = shrink_qkv.shape[1]
    held = shrink_qkv.shape[0]
    head = place * kv_heads // parts
    query_cols = query_weight.shape[1]

    normed_own = norm_rows(tokens, attn_gain)
    normed = lax.all_gather(normed_own, "tensor", axis=0, tiled=True)

    half = held // 2
    half_own = lax.dynamic_slice_in_dim(shrink_qkv, core * half, half, 0)
    pieces, spots = [shrink_qkv], [holder * held]
    for r in range(1, holders):
        got = lax.ppermute(half_own, "dp", [(i, i ^ r) for i in range(holders)])
        pieces += [got, other_core(got, parts)]
        begin = (holder ^ r) * held
        spots += [begin + core * half, begin + (1 - core) * half]

    cols = w_kv.shape[0]

    def head_rows(turn):
        to = (2 * ((chip + turn) % chips)) * kv_heads // parts
        return lax.dynamic_index_in_dim(w_kv, to, 1, keepdims=False)

    mine = [head_rows(0)] + [turn_chips(head_rows(r), parts, r) for r in range(1, chips)]
    mine = jnp.stack(mine[:1] + mine[:0:-1])
    theirs = other_core(mine, parts)
    pair = jnp.where(core == 0, jnp.stack([mine, theirs], 1), jnp.stack([theirs, mine], 1))
    pair = lax.dynamic_slice_in_dim(jnp.concatenate([pair, pair]), (chips - chip) % chips, chips, 0)
    wkv_head = pair.reshape(2 * head_length, width)

    position = jnp.arange(total, dtype=jnp.int32)
    length_row, group_row, adapter_row = lengths[0], groups[0], adapter_of_request[0]
    ends = jnp.cumsum(length_row)
    starts = ends - length_row
    request = jnp.sum((ends[None, :] <= position[:, None]).astype(jnp.int32), axis=1)
    same = group_row[:, None] == group_row[None, :]
    group_first = jnp.min(jnp.where(same, starts[None, :], total), axis=1)
    slot_of_request = lookup(adapter_row, adapter_slot)
    group = lookup(request, group_row)
    rope_pos = position - lookup(request, group_first)
    slot = lookup(request, slot_of_request)
    meta_col = jnp.stack([slot, group], axis=1)
    meta_row = group[None, :]
    freq = jnp.exp(
        -jnp.arange(head_length // 2, dtype=F32) * (2.0 * math.log(ROPE_BASE) / head_length)
    )
    angle = rope_pos.astype(F32)[:, None] * freq[None, :]
    cosine, sine = jnp.cos(angle), jnp.sin(angle)
    cosine = jnp.concatenate([cosine, cosine], axis=1)
    sine = jnp.concatenate([-sine, sine], axis=1)
    colslot = (jnp.arange(adapters * ranks, dtype=jnp.int32) // ranks)[None, :]
    oslot = (jnp.arange(adapters * rank, dtype=jnp.int32) // rank)[None, :]

    up_kv = lax.dynamic_index_in_dim(
        key_value_up_factors.reshape(adapters, rank, kv_heads, 2, head_length), head, 2, keepdims=False
    )
    up = jnp.concatenate(
        [
            jnp.pad(query_up_factors, ((0, 0), (0, 2 * rank), (0, 0))),
            jnp.pad(up_kv[:, :, 0], ((0, 0), (rank, rank), (0, 0))),
            jnp.pad(up_kv[:, :, 1], ((0, 0), (2 * rank, 0), (0, 0))),
        ],
        axis=2,
    ).reshape(adapters * ranks, query_cols + 2 * head_length)

    scal = jnp.stack([chip, core] + spots).astype(jnp.int32)
    weights = (
        query_weight,
        wkv_head,
        up,
        w_o,
        shrink_o.reshape(adapters * rank, query_cols),
        expand_o.reshape(adapters * rank, width),
        q_gain.reshape(1, -1),
        k_gain.reshape(1, -1),
    )
    meta = (meta_col, meta_row, colslot, oslot, cosine, sine)
    own_terms, part_terms, entries = attention(
        scal, normed, weights, meta, pieces, adapters, chips, own_rows
    )

    sums = pair_sum(own_terms, other_core(part_terms, parts))
    arrived = [sums[0]] + [turn_chips(sums[r], parts, r) for r in range(1, chips)]
    attn_own, moe_own = residual_norm(tokens, moe_gain, arrived)

    local_cols = kv_width // parts
    kept = lax.dynamic_slice_in_dim(
        entries, place * local_cols - head * 2 * head_length, local_cols, 1
    )
    page_row = page_table[0]
    per_request = page_row.shape[0] // length_row.shape[0]
    offset = PAGE * jnp.arange(per_request, dtype=jnp.int32)[None, :]
    page_first = (starts[:, None] + offset).reshape(-1)
    page_length = jnp.clip(length_row[:, None] - offset, 0, PAGE).reshape(-1)
    kv_pages = fill_pages(page_first, page_length, page_row, kept)

    experts = w_gate.shape[0]
    capacity = CAP_DEV * parts
    share = expert_gates / jnp.sum(expert_gates, axis=1, keepdims=True)
    own_experts = place * experts + jnp.arange(experts, dtype=jnp.int32)
    chosen = expert_ids[:, :, None] == own_experts[None, None, :]
    hit = jnp.any(chosen, axis=1)
    weight = jnp.sum(jnp.where(chosen, share[:, :, None], 0.0), axis=1)
    before = dot(
        (position[:, None] > position[None, :]).astype(BF16), hit.astype(BF16)
    ).astype(jnp.int32)
    slot_in = jnp.where(hit, before, -1)

    blocks, places = [moe_own], [chip * 2 + core]
    for r in range(1, chips):
        blocks.append(turn_chips(moe_own, parts, r))
        places.append((chip - r + chips) % chips * 2 + core)
    blocks += [other_core(b, parts) for b in blocks]
    places += [p - core + (1 - core) for p in places]
    spots = (jnp.stack(places) * own_rows).astype(jnp.int32)
    moe_terms = expert_layer(
        spots, slot_in, slot_in.T, weight, blocks, w_gate, w_up, w_down, capacity
    )
    moe_total = lax.psum_scatter(moe_terms, "tensor", scatter_dimension=0, tiled=True)
    return (attn_own, moe_total, kv_pages)


def solution(mesh):
    placed = (
        P(("dp", "tensor"), None),
        P(),
        P(),
        P(),
        P(),
        P(None, "tensor"),
        P("tensor", None, None),
        P("tensor", None),
        P("tensor", None, None),
        P("tensor", None, None),
        P("tensor", None, None),
        P("dp", None, None),
        P(None, None, "tensor"),
        P(None, None, "tensor"),
        P(),
        P(),
        P("dp", None),
        P("dp", None),
        P("dp", None),
        P(),
        P("dp", None),
        P("dp", None),
        P("dp", None),
    )
    return jax.shard_map(
        local,
        mesh=mesh,
        in_specs=placed,
        out_specs=(P(("dp", "tensor"), None), P(("dp", "tensor"), None), P("dp", "tensor", None)),
        check_vma=False,
    )
```

```python
import functools
import math

import jax
import jax.numpy as jnp
from jax import lax
from jax.experimental import pallas as pl
from jax.experimental.pallas import tpu as pltpu
from jax.sharding import PartitionSpec as P

PAGE = 128
CAP_DEV = 16
NORM_EPS = 1e-06
ROPE_BASE = 1000000.0
ADAPTER_FACTOR = 0.5
MIB = 1 << 20
BF16 = jnp.bfloat16
F32 = jnp.float32
VMEM = pl.BlockSpec(memory_space=pltpu.VMEM)
SMEM = pl.BlockSpec(memory_space=pltpu.SMEM)
ANY = pl.BlockSpec(memory_space=pl.ANY)


def dot(a, b):
    return jnp.dot(a, b, preferred_element_type=F32)


def dot_nt(a, b):
    return lax.dot_general(a, b, (((1,), (1,)), ((), ())), preferred_element_type=F32)


def lookup(index_value, table):
    match = index_value[:, None] == jnp.arange(table.shape[0], dtype=jnp.int32)[None, :]
    return jnp.sum(jnp.where(match, table[None, :], 0), axis=1)


def loop(count, body, carry):
    if count <= 2:
        for i in range(count):
            carry = body(i, carry)
        return carry
    return lax.fori_loop(0, count, body, carry)


def rms(v, gain):
    return v * lax.rsqrt(jnp.mean(v * v, axis=-1, keepdims=True) + NORM_EPS) * gain


def residual_kernel(x_ref, gain_ref, *refs):
    parts, (attn_ref, out_ref) = refs[:-2], refs[-2:]
    total = parts[0][...].astype(F32)
    for part in parts[1:]:
        total = total + part[...].astype(F32)
    attn_ref[...] = total.astype(BF16)
    out_ref[...] = rms(x_ref[...].astype(F32) + total, gain_ref[...].astype(F32)).astype(BF16)


def residual_norm(x, gain, parts):
    shape = jax.ShapeDtypeStruct(x.shape, BF16)
    return pl.pallas_call(
        residual_kernel,
        out_shape=(shape, shape),
        in_specs=[VMEM] * (2 + len(parts)),
        out_specs=(VMEM, VMEM),
        name="residual_norm",
    )(x, gain.reshape(1, -1), *parts)


def pair_kernel(a_ref, b_ref, *outs):
    rows = outs[0].shape[0]
    for i, out in enumerate(outs):
        here = slice(i * rows, (i + 1) * rows)
        out[...] = (a_ref[here, :].astype(F32) + b_ref[here, :].astype(F32)).astype(BF16)


def pair_sum(a, b, count):
    shape = jax.ShapeDtypeStruct((a.shape[0] // count, a.shape[1]), BF16)
    return pl.pallas_call(
        pair_kernel,
        out_shape=(shape,) * count,
        in_specs=[VMEM, VMEM],
        out_specs=(VMEM,) * count,
        compiler_params=pltpu.CompilerParams(vmem_limit_bytes=24 * MIB),
        name="pair_sum",
    )(a, b)


def attention_kernel(
    token_blocks,
    factor_blocks,
    spot_ref,
    gain_ref,
    wq_ref,
    wkv_ref,
    up_ref,
    meta_ref,
    row_ref,
    colslot_ref,
    cos_ref,
    sin_ref,
    qg_ref,
    kg_ref,
    *refs,
):
    tokens, refs = refs[:token_blocks], refs[token_blocks:]
    pieces, refs = refs[:factor_blocks], refs[factor_blocks:]
    own_ref, part_ref, kv_ref, x_ref, s_ref, qf_ref, kvf_ref, q_ref, x_sems, s_sems = refs
    rows, width = x_ref.shape
    query_cols = wq_ref.shape[1]
    head = qg_ref.shape[1]
    heads = query_cols // head
    block = min(256, rows // 2)
    blocks = rows // block
    scale = head**-0.5
    own_rows = rows // token_blocks
    token_copies, factor_copies = [], []
    for i, piece in enumerate(tokens):
        target = x_ref.at[pl.ds(i * own_rows, own_rows)]
        token_copies.append(pltpu.make_async_copy(piece, target, x_sems.at[i]))
        token_copies[-1].start()
    for i, piece in enumerate(pieces):
        target = s_ref.at[pl.ds(spot_ref[i], piece.shape[0])]
        factor_copies.append(pltpu.make_async_copy(piece, target, s_sems.at[i]))
        factor_copies[-1].start()
    factors = s_ref.shape[0] * s_ref.shape[1]
    gain = gain_ref[...].astype(F32)
    qg = qg_ref[...].astype(F32)
    kg = kg_ref[...].astype(F32)

    for copy in token_copies:
        copy.wait()

    def project(i, carry):
        here = pl.ds(pl.multiple_of(i * block, block), block)
        x = rms(x_ref[here, :].astype(F32), gain).astype(BF16)
        x_ref[here, :] = x
        qf_ref[here, :] = dot(x, wq_ref[...])
        kvf_ref[here, :] = dot_nt(x, wkv_ref[...])
        return carry

    loop(blocks, project, 0)

    for copy in factor_copies:
        copy.wait()

    def turned(v, gain, here):
        v = rms(v, gain)
        return v * cos_ref[here, :] + pltpu.roll(v, head // 2, 1) * sin_ref[here, :]

    def adapt(i, carry):
        here = pl.ds(pl.multiple_of(i * block, block), block)
        low = dot_nt(x_ref[here, :], s_ref[...].reshape(factors, width))
        low = jnp.where(meta_ref[here, 0:1] == colslot_ref[...], low, 0.0).astype(BF16)
        delta = ADAPTER_FACTOR * dot(low, up_ref[...])
        q = qf_ref[here, :] + delta[:, :query_cols]
        kv = (kvf_ref[here, :] + delta[:, query_cols:]).astype(BF16)
        for h in range(heads):
            cut = slice(h * head, (h + 1) * head)
            q_ref[here, cut] = turned(q[:, cut], qg, here).astype(BF16)
        kv_ref[here, :head] = turned(kv[:, :head].astype(F32), kg, here).astype(BF16)
        kv_ref[here, head:] = kv[:, head:]
        return carry

    loop(blocks, adapt, 0)

    def attend(target, offset):
        def one(i, carry):
            there = pl.ds(pl.multiple_of(i * block, block), block)
            here = pl.ds(pl.multiple_of(offset + i * block, block), block)
            allowed = (row_ref[1:2, :] <= meta_ref[here, 2:3]) & (
                row_ref[0:1, :] == meta_ref[here, 1:2]
            )
            for h in range(heads):
                cut = slice(h * head, (h + 1) * head)
                s = dot_nt(q_ref[here, cut], kv_ref[:, :head]) * scale
                raised = jnp.where(allowed, jnp.exp(s), 0.0)
                mixed = dot(raised.astype(BF16), kv_ref[:, head:])
                mixed = mixed / jnp.sum(raised, axis=1, keepdims=True)
                target[there, cut] = mixed.astype(BF16)
            return carry

        loop(blocks // 2, one, 0)

    attend(part_ref, rows // 2)
    attend(own_ref, 0)


def attention(spots, tokens, weights, meta, pieces, adapters):
    gain, wq, wkv, up, qg, kg = weights
    own_rows, width = tokens[0].shape
    rows = own_rows * len(tokens)
    query_cols = wq.shape[1]
    head = qg.shape[1]
    ranks = pieces[0].shape[1]
    half = jax.ShapeDtypeStruct((rows // 2, query_cols), BF16)
    flops = 2 * rows * (width * (adapters * ranks + query_cols + 2 * head) + rows * query_cols)
    return pl.pallas_call(
        functools.partial(attention_kernel, len(tokens), len(pieces)),
        out_shape=(half, half, jax.ShapeDtypeStruct((rows, 2 * head), BF16)),
        in_specs=[SMEM] + [VMEM] * 11 + [ANY] * (len(tokens) + len(pieces)),
        out_specs=(VMEM, VMEM, VMEM),
        scratch_shapes=[
            pltpu.VMEM((rows, width), BF16),
            pltpu.VMEM((adapters, ranks, width), BF16),
            pltpu.VMEM((rows, query_cols), F32),
            pltpu.VMEM((rows, 2 * head), F32),
            pltpu.VMEM((rows, query_cols), BF16),
            pltpu.SemaphoreType.DMA((len(tokens),)),
            pltpu.SemaphoreType.DMA((len(pieces),)),
        ],
        compiler_params=pltpu.CompilerParams(vmem_limit_bytes=40 * MIB),
        cost_estimate=pl.CostEstimate(
            flops=flops, bytes_accessed=14 * MIB, transcendentals=rows * rows
        ),
        name="attention",
    )(spots, gain, wq, wkv, up, *meta, qg, kg, *tokens, *pieces)


def output_kernel(
    own_ref, got_ref, wo_ref, wo2_ref, sho_ref, sho2_ref, exo_ref, slot_ref, oslot_ref, *outs
):
    rows = own_ref.shape[0]
    own_rows, width = outs[0].shape
    block = min(256, rows)
    per = block // own_rows
    step = min(512, width)
    for i in range(rows // block):
        here = slice(i * block, (i + 1) * block)
        own, got = own_ref[here, :], got_ref[here, :]
        low = dot_nt(own, sho_ref[...]) + dot_nt(got, sho2_ref[...])
        low = jnp.where(slot_ref[here, :] == oslot_ref[...], low, 0.0)
        high = low.astype(BF16)
        rest = (low - high.astype(F32)).astype(BF16)
        for c in range(0, width, step):
            cut = slice(c, c + step)
            expand = exo_ref[:, cut]
            term = dot(own, wo_ref[:, cut]) + dot(got, wo2_ref[:, cut])
            term = term + ADAPTER_FACTOR * (dot(high, expand) + dot(rest, expand))
            term = term.astype(BF16)
            for b in range(per):
                outs[i * per + b][:, cut] = term[b * own_rows : (b + 1) * own_rows, :]


def output_terms(own, got, weights, slot, oslot, chips):
    rows, query_cols = own.shape
    width = weights[0].shape[1]
    shape = jax.ShapeDtypeStruct((rows // chips, width), BF16)
    return pl.pallas_call(
        output_kernel,
        out_shape=(shape,) * chips,
        in_specs=[VMEM] * 9,
        out_specs=(VMEM,) * chips,
        compiler_params=pltpu.CompilerParams(vmem_limit_bytes=32 * MIB),
        cost_estimate=pl.CostEstimate(
            flops=4 * rows * query_cols * width, bytes_accessed=8 * MIB, transcendentals=0
        ),
        name="output_terms",
    )(own, got, *weights, slot, oslot)


def pages_kernel(first_ref, length_ref, page_ref, entries_ref, out_ref):
    columns, extent = entries_ref.shape
    rows = extent - PAGE
    window = 2 * PAGE
    gap = lax.broadcasted_iota(jnp.int32, (window, PAGE), 0) - lax.broadcasted_iota(
        jnp.int32, (window, PAGE), 1
    )
    lane = lax.broadcasted_iota(jnp.int32, (columns, PAGE), 1)

    def one(n, carry):
        length = length_ref[n]
        page = page_ref[n]

        @pl.when(length > 0)
        def _():
            first = jnp.minimum(first_ref[n], rows - 1)
            base = pl.multiple_of(first // PAGE * PAGE, PAGE)
            pick = (gap == first - base).astype(F32).astype(BF16)
            moved = dot(entries_ref[:, pl.ds(base, window)], pick)
            out_ref[page] = jnp.where(lane < length, moved, 0.0).astype(BF16)

        @pl.when(length <= 0)
        def _():
            out_ref[page] = jnp.zeros((columns, PAGE), BF16)

        return carry

    lax.fori_loop(0, page_ref.shape[0], one, 0)


def fill_pages(first, length, page, entries):
    rows, columns = entries.shape
    count = page.shape[0]
    turned = jnp.pad(entries.T, ((0, 0), (0, PAGE)))
    return pl.pallas_call(
        pages_kernel,
        out_shape=jax.ShapeDtypeStruct((count, columns, PAGE), BF16),
        in_specs=[SMEM, SMEM, SMEM, VMEM],
        out_specs=VMEM,
        compiler_params=pltpu.CompilerParams(vmem_limit_bytes=32 * MIB),
        cost_estimate=pl.CostEstimate(
            flops=count * columns * PAGE * PAGE * 16, bytes_accessed=4 * MIB, transcendentals=0
        ),
        name="fill_pages",
    )(first, length, page, turned)


def experts_kernel(blocks, slot_ref, slot_t_ref, weight_ref, *refs):
    pieces, refs = refs[:blocks], refs[blocks:]
    (gate_ref, up_ref, down_ref, own_ref, part_ref) = refs[:5]
    (x_ref, rows_ref, y_ref, gate_buf, up_buf, down_buf, x_sems, w_sems) = refs[5:]
    total, width = x_ref.shape
    own_rows = total // blocks
    experts = slot_ref.shape[1]
    capacity = rows_ref.shape[0] // experts
    slots = gate_buf.shape[0]
    streams = ((gate_ref, gate_buf), (up_ref, up_buf), (down_ref, down_buf))

    def copy(k, e, s):
        source, buffer = streams[k]
        return pltpu.make_async_copy(source.at[e], buffer.at[s], w_sems.at[k, s])

    copies = []
    for i, piece in enumerate(pieces):
        target = x_ref.at[pl.ds(i * own_rows, own_rows)]
        copies.append(pltpu.make_async_copy(piece, target, x_sems.at[i]))
        copies[-1].start()
    for e in range(min(slots, experts)):
        for k in range(3):
            copy(k, e, e).start()
    for item in copies:
        item.wait()
    line = lax.broadcasted_iota(jnp.int32, (capacity, total), 0)
    pick = jnp.concatenate(
        [(slot_t_ref[n : n + 1, :] == line).astype(F32).astype(BF16) for n in range(experts)], axis=0
    )
    step = min(512, width)
    for c in range(0, width, step):
        rows_ref[:, c : c + step] = dot(pick, x_ref[:, c : c + step]).astype(BF16)

    def one(e, carry):
        s = lax.rem(e, slots)
        here = pl.ds(pl.multiple_of(e * capacity, capacity), capacity)
        x = rows_ref[here, :]
        copy(0, e, s).wait()
        gate = dot_nt(gate_buf[s], x)
        copy(1, e, s).wait()
        up = dot_nt(up_buf[s], x)
        hidden = (gate / (1.0 + jnp.exp(-gate)) * up).T.astype(BF16)
        copy(2, e, s).wait()
        y_ref[here, :] = dot(hidden, down_buf[s]).astype(BF16)

        @pl.when(e + slots < experts)
        def _():
            for k in range(3):
                copy(k, e + slots, s).start()

        return carry

    lax.fori_loop(0, experts, one, 0)

    tile = min(256, total // 2)
    line = lax.broadcasted_iota(jnp.int32, (tile, capacity), 1)

    def combine(target, offset):
        def mix(i, carry):
            there = pl.ds(pl.multiple_of(i * tile, tile), tile)
            here = pl.ds(pl.multiple_of(offset + i * tile, tile), tile)
            spread = jnp.concatenate(
                [
                    jnp.where(
                        slot_ref[here, n : n + 1] == line, weight_ref[here, n : n + 1], 0.0
                    ).astype(BF16)
                    for n in range(experts)
                ],
                axis=1,
            )
            for c in range(0, width, step):
                target[there, c : c + step] = dot(spread, y_ref[:, c : c + step]).astype(BF16)
            return carry

        loop(total // 2 // tile, mix, 0)

    combine(part_ref, total // 2)
    combine(own_ref, 0)


def expert_layer(slot, slot_t, weight, pieces, gate, up, down, capacity):
    experts, hidden, width = gate.shape
    total = slot.shape[0]
    slots = min(3 if total <= 512 else 2, experts)
    half = jax.ShapeDtypeStruct((total // 2, width), BF16)
    return pl.pallas_call(
        functools.partial(experts_kernel, len(pieces)),
        out_shape=(half, half),
        in_specs=[VMEM] * 3 + [ANY] * (len(pieces) + 3),
        out_specs=(VMEM, VMEM),
        scratch_shapes=[
            pltpu.VMEM((total, width), BF16),
            pltpu.VMEM((experts * capacity, width), BF16),
            pltpu.VMEM((experts * capacity, width), BF16),
            pltpu.VMEM((slots, hidden, width), BF16),
            pltpu.VMEM((slots, hidden, width), BF16),
            pltpu.VMEM((slots, hidden, width), BF16),
            pltpu.SemaphoreType.DMA((len(pieces),)),
            pltpu.SemaphoreType.DMA((3, slots)),
        ],
        compiler_params=pltpu.CompilerParams(vmem_limit_bytes=60 * MIB),
        cost_estimate=pl.CostEstimate(
            flops=6 * experts * capacity * hidden * width,
            bytes_accessed=6 * experts * hidden * width,
            transcendentals=experts * capacity * hidden,
        ),
        name="experts",
    )(slot, slot_t, weight, *pieces, gate, up, down)


def other_core(value, parts):
    return lax.ppermute(value, "tensor", [(i, i ^ 1) for i in range(parts)])


def turn_chips(value, parts, by):
    return lax.ppermute(value, "tensor", [(i, (i + 2 * by) % parts) for i in range(parts)])


def swap_holder(value, holders, by):
    return lax.ppermute(value, "dp", [(i, i ^ by) for i in range(holders)])


def gather_blocks(own, parts):
    chips = parts // 2
    mine = [own] + [turn_chips(own, parts, r) for r in range(chips - 1, 0, -1)]
    return mine + [other_core(block, parts) for block in mine]


def from_here(rows, chip, core, chips):
    split = rows.reshape((chips, 2, -1) + rows.shape[1:])
    split = jnp.where(core == 0, split, split[:, ::-1])
    split = lax.dynamic_slice_in_dim(jnp.concatenate([split, split]), chip, chips, 0)
    return jnp.swapaxes(split, 0, 1).reshape(rows.shape)


def to_group(rows, chip, core, chips):
    split = jnp.swapaxes(rows.reshape((2, chips, -1) + rows.shape[1:]), 0, 1)
    split = lax.dynamic_slice_in_dim(
        jnp.concatenate([split, split]), (chips - chip) % chips, chips, 0
    )
    return jnp.where(core == 0, split, split[:, ::-1]).reshape(rows.shape)


def head_weights(w_kv, head_of_chip, chip, core, holder, parts, holders):
    chips = parts // 2
    cols, _, width = w_kv.shape
    piece = width // holders

    def cut(turn):
        to = head_of_chip((chip + turn) % chips)
        return lax.dynamic_slice(w_kv, (0, to, holder * piece), (cols, 1, piece))[:, 0]

    mine = [cut(0)] + [turn_chips(cut(r), parts, r) for r in range(chips - 1, 0, -1)]
    mine = jnp.stack(mine)
    full = [mine] + [swap_holder(mine, holders, r) for r in range(1, holders)]
    bit = 1
    while bit < holders:
        full = [
            jnp.where((holder & bit) == 0, full[i], full[i ^ bit]) for i in range(holders)
        ]
        bit *= 2
    full = jnp.concatenate(full, axis=2)
    theirs = other_core(full, parts)
    pair = jnp.where(core == 0, jnp.stack([full, theirs], 1), jnp.stack([theirs, full], 1))
    pair = lax.dynamic_slice_in_dim(jnp.concatenate([pair, pair]), (chips - chip) % chips, chips, 0)
    return pair.reshape(parts * cols, width)


def local(
    tokens,
    attn_gain,
    moe_gain,
    q_gain,
    k_gain,
    query_weight,
    w_kv,
    w_o,
    w_gate,
    w_up,
    w_down,
    shrink_qkv,
    shrink_o,
    query_up_factors,
    key_value_up_factors,
    expand_o,
    lengths,
    groups,
    adapter_of_request,
    adapter_slot,
    page_table,
    expert_ids,
    expert_gates,
):
    parts = lax.axis_size("tensor")
    place = lax.axis_index("tensor")
    holders = lax.axis_size("dp")
    holder = lax.axis_index("dp")
    chips, chip, core = parts // 2, place // 2, place % 2
    own_rows, width = tokens.shape
    total = own_rows * parts
    head_length = q_gain.shape[0]
    adapters, rank, kv_width = key_value_up_factors.shape
    kv_heads = kv_width // (2 * head_length)
    held, ranks = shrink_qkv.shape[:2]
    head = place * kv_heads // parts
    query_cols = query_weight.shape[1]

    wkv_head = head_weights(
        w_kv, lambda c: 2 * c * kv_heads // parts, chip, core, holder, parts, holders
    )
    gathered = gather_blocks(tokens, parts)
    half = held // 2
    half_own = lax.dynamic_slice_in_dim(shrink_qkv, core * half, half, 0)
    pieces, spots = [shrink_qkv], [holder * held]
    for r in range(1, holders):
        got = swap_holder(half_own, holders, r)
        pieces += [got, other_core(got, parts)]
        begin = (holder ^ r) * held
        spots += [begin + core * half, begin + (1 - core) * half]
    shrink_rows = shrink_o.reshape(adapters * rank, query_cols)
    w_o_other = other_core(w_o, parts)
    shrink_other = other_core(shrink_rows, parts)

    line = jnp.arange(total, dtype=jnp.int32)
    side, number = line // (total // 2), line // own_rows % chips
    position = ((number + chip) % chips * 2 + (side ^ core)) * own_rows + line % own_rows
    length_row, group_row, adapter_row = lengths[0], groups[0], adapter_of_request[0]
    ends = jnp.cumsum(length_row)
    starts = ends - length_row
    request = jnp.sum((ends[None, :] <= position[:, None]).astype(jnp.int32), axis=1)
    same = group_row[:, None] == group_row[None, :]
    group_first = jnp.min(jnp.where(same, starts[None, :], total), axis=1)
    slot_of_request = lookup(adapter_row, adapter_slot)
    group = lookup(request, group_row)
    rope_pos = position - lookup(request, group_first)
    slot = lookup(request, slot_of_request)
    meta_col = jnp.stack([slot, group, position], axis=1)
    meta_row = jnp.stack([group, position], axis=0)
    freq = jnp.exp(
        -jnp.arange(head_length // 2, dtype=F32) * (2.0 * math.log(ROPE_BASE) / head_length)
    )
    angle = rope_pos.astype(F32)[:, None] * freq[None, :]
    cosine, sine = jnp.cos(angle), jnp.sin(angle)
    cosine = jnp.concatenate([cosine, cosine], axis=1)
    sine = jnp.concatenate([-sine, sine], axis=1)
    colslot = (jnp.arange(adapters * ranks, dtype=jnp.int32) // ranks)[None, :]
    oslot = (jnp.arange(adapters * rank, dtype=jnp.int32) // rank)[None, :]

    up_kv = lax.dynamic_index_in_dim(
        key_value_up_factors.reshape(adapters, rank, kv_heads, 2, head_length), head, 2, keepdims=False
    )
    up = jnp.concatenate(
        [
            jnp.pad(query_up_factors, ((0, 0), (0, 2 * rank), (0, 0))),
            jnp.pad(up_kv[:, :, 0], ((0, 0), (rank, rank), (0, 0))),
            jnp.pad(up_kv[:, :, 1], ((0, 0), (2 * rank, 0), (0, 0))),
        ],
        axis=2,
    ).reshape(adapters * ranks, query_cols + 2 * head_length)

    weights = (
        attn_gain.reshape(1, -1),
        query_weight,
        wkv_head,
        up,
        q_gain.reshape(1, -1),
        k_gain.reshape(1, -1),
    )
    meta = (meta_col, meta_row, colslot, cosine, sine)
    mixed, mixed_part, entries = attention(
        jnp.stack(spots).astype(jnp.int32), gathered, weights, meta, pieces, adapters
    )

    out_weights = (
        w_o,
        w_o_other,
        shrink_rows,
        shrink_other,
        expand_o.reshape(adapters * rank, width),
    )
    sums = output_terms(
        mixed, other_core(mixed_part, parts), out_weights, slot[: total // 2, None], oslot, chips
    )
    arrived = [sums[0]] + [turn_chips(sums[r], parts, r) for r in range(1, chips)]
    attn_own, moe_own = residual_norm(tokens, moe_gain, arrived)

    local_cols = kv_width // parts
    kept = lax.dynamic_slice_in_dim(
        entries, place * local_cols - head * 2 * head_length, local_cols, 1
    )
    page_row = page_table[0]
    per_request = page_row.shape[0] // length_row.shape[0]
    offset = PAGE * jnp.arange(per_request, dtype=jnp.int32)[None, :]
    page_first = (starts[:, None] + offset).reshape(-1)
    page_length = jnp.clip(length_row[:, None] - offset, 0, PAGE).reshape(-1)
    kv_pages = fill_pages(page_first, page_length, page_row, to_group(kept, chip, core, chips))

    experts = w_gate.shape[0]
    capacity = CAP_DEV * parts
    ids = from_here(expert_ids, chip, core, chips)
    gates = from_here(expert_gates, chip, core, chips)
    share = gates / jnp.sum(gates, axis=1, keepdims=True)
    own_experts = place * experts + jnp.arange(experts, dtype=jnp.int32)
    chosen = ids[:, :, None] == own_experts[None, None, :]
    hit = jnp.any(chosen, axis=1)
    weight = jnp.sum(jnp.where(chosen, share[:, :, None], 0.0), axis=1)
    before = dot((line[:, None] > line[None, :]).astype(BF16), hit.astype(BF16)).astype(jnp.int32)
    slot_in = jnp.where(hit, before, -1)

    own_terms, part_terms = expert_layer(
        slot_in,
        slot_in.T,
        weight,
        gather_blocks(moe_own, parts),
        w_gate,
        w_up,
        w_down,
        capacity,
    )
    sums = pair_sum(own_terms, other_core(part_terms, parts), chips)
    arrived = [sums[0]] + [turn_chips(sums[r], parts, r) for r in range(1, chips)]
    moe_total = sum(part.astype(F32) for part in arrived).astype(BF16)
    return (attn_own, moe_total, kv_pages)


def solution(mesh):
    placed = (
        P(("dp", "tensor"), None),
        P(),
        P(),
        P(),
        P(),
        P(None, "tensor"),
        P("tensor", None, None),
        P("tensor", None),
        P("tensor", None, None),
        P("tensor", None, None),
        P("tensor", None, None),
        P("dp", None, None),
        P(None, None, "tensor"),
        P(None, None, "tensor"),
        P(),
        P(),
        P("dp", None),
        P("dp", None),
        P("dp", None),
        P(),
        P("dp", None),
        P("dp", None),
        P("dp", None),
    )
    return jax.shard_map(
        local,
        mesh=mesh,
        in_specs=placed,
        out_specs=(P(("dp", "tensor"), None), P(("dp", "tensor"), None), P("dp", "tensor", None)),
        check_vma=False,
    )
```

```python
import functools
import math

import jax
import jax.numpy as jnp
from jax import lax
from jax.experimental import pallas as pl
from jax.experimental.pallas import tpu as pltpu
from jax.sharding import PartitionSpec as P

PAGE = 128
CAP_DEV = 16
NORM_EPS = 1e-06
ROPE_BASE = 1000000.0
ADAPTER_FACTOR = 0.5
MIB = 1 << 20
BF16 = jnp.bfloat16
F32 = jnp.float32
VMEM = pl.BlockSpec(memory_space=pltpu.VMEM)
SMEM = pl.BlockSpec(memory_space=pltpu.SMEM)
ANY = pl.BlockSpec(memory_space=pl.ANY)


def dot(a, b):
    return jnp.dot(a, b, preferred_element_type=F32)


def dot_nt(a, b):
    return lax.dot_general(a, b, (((1,), (1,)), ((), ())), preferred_element_type=F32)


def lookup(index_value, table):
    match = index_value[:, None] == jnp.arange(table.shape[0], dtype=jnp.int32)[None, :]
    return jnp.sum(jnp.where(match, table[None, :], 0), axis=1)


def loop(count, body, carry):
    if count <= 2:
        for i in range(count):
            carry = body(i, carry)
        return carry
    return lax.fori_loop(0, count, body, carry)


def rms(v, gain):
    return v * lax.rsqrt(jnp.mean(v * v, axis=-1, keepdims=True) + NORM_EPS) * gain


def residual_kernel(x_ref, gain_ref, *refs):
    parts, (attn_ref, out_ref) = refs[:-2], refs[-2:]
    total = parts[0][...].astype(F32)
    for part in parts[1:]:
        total = total + part[...].astype(F32)
    attn_ref[...] = total.astype(BF16)
    out_ref[...] = rms(x_ref[...].astype(F32) + total, gain_ref[...].astype(F32)).astype(BF16)


def residual_norm(x, gain, parts):
    shape = jax.ShapeDtypeStruct(x.shape, BF16)
    return pl.pallas_call(
        residual_kernel,
        out_shape=(shape, shape),
        in_specs=[VMEM] * (2 + len(parts)),
        out_specs=(VMEM, VMEM),
        name="residual_norm",
    )(x, gain.reshape(1, -1), *parts)


def pair_kernel(a_ref, b_ref, *outs):
    rows = outs[0].shape[0]
    for i, out in enumerate(outs):
        here = slice(i * rows, (i + 1) * rows)
        out[...] = (a_ref[here, :].astype(F32) + b_ref[here, :].astype(F32)).astype(BF16)


def pair_sum(a, b, count):
    shape = jax.ShapeDtypeStruct((a.shape[0] // count, a.shape[1]), BF16)
    return pl.pallas_call(
        pair_kernel,
        out_shape=(shape,) * count,
        in_specs=[VMEM, VMEM],
        out_specs=(VMEM,) * count,
        compiler_params=pltpu.CompilerParams(vmem_limit_bytes=24 * MIB),
        name="pair_sum",
    )(a, b)


def attention_kernel(
    factor_blocks,
    head_blocks,
    spot_ref,
    gain_ref,
    wq_ref,
    up_ref,
    meta_ref,
    row_ref,
    colslot_ref,
    cos_ref,
    sin_ref,
    qg_ref,
    kg_ref,
    *refs,
):
    tokens_ref, refs = refs[0], refs[1:]
    pieces, refs = refs[:factor_blocks], refs[factor_blocks:]
    parts, refs = refs[:head_blocks], refs[head_blocks:]
    own_ref, part_ref, kv_ref = refs[:3]
    x_ref, s_ref, w_ref, qf_ref, kvf_ref, q_ref, x_sems, s_sems, w_sems = refs[3:]
    rows, width = x_ref.shape
    query_cols = wq_ref.shape[1]
    head = qg_ref.shape[1]
    heads = query_cols // head
    block = min(256, rows // 2)
    blocks = rows // block
    scale = head**-0.5
    devices, holders, cols, piece_width = w_ref.shape
    chips = devices // 2
    own_rows = rows // devices
    chip, core, holder = spot_ref[0], spot_ref[1], spot_ref[2]
    token_copies, factor_copies, head_copies = [], [], []
    for q in range(2):
        for j in range(chips):
            i = q * chips + j
            device = lax.rem(chip + j, chips) * 2 + (core ^ q)
            source = tokens_ref.at[pl.ds(pl.multiple_of(device * own_rows, own_rows), own_rows)]
            target = x_ref.at[pl.ds(i * own_rows, own_rows)]
            token_copies.append(pltpu.make_async_copy(source, target, x_sems.at[i]))
            token_copies[-1].start()
    for q in range(2):
        for r in range(holders):
            for j in range(chips):
                device = lax.rem(chip + j, chips) * 2 + (core ^ q)
                target = w_ref.at[device, holder ^ r]
                head_copies.append(
                    pltpu.make_async_copy(
                        parts[q * holders + r].at[j],
                        target,
                        w_sems.at[(q * holders + r) * chips + j],
                    )
                )
                head_copies[-1].start()
    for i, piece in enumerate(pieces):
        target = s_ref.at[pl.ds(spot_ref[3 + i], piece.shape[0])]
        factor_copies.append(pltpu.make_async_copy(piece, target, s_sems.at[i]))
        factor_copies[-1].start()
    factors = s_ref.shape[0] * s_ref.shape[1]
    gain = gain_ref[...].astype(F32)
    qg = qg_ref[...].astype(F32)
    kg = kg_ref[...].astype(F32)

    for copy in token_copies + head_copies:
        copy.wait()

    def project(i, carry):
        here = pl.ds(pl.multiple_of(i * block, block), block)
        x = rms(x_ref[here, :].astype(F32), gain).astype(BF16)
        x_ref[here, :] = x
        qf_ref[here, :] = dot(x, wq_ref[...])
        kv = 0.0
        for r in range(holders):
            w = w_ref[:, r].reshape(devices * cols, piece_width)
            kv = kv + dot_nt(x[:, r * piece_width : (r + 1) * piece_width], w)
        kvf_ref[here, :] = kv
        return carry

    loop(blocks, project, 0)

    for copy in factor_copies:
        copy.wait()

    def turned(v, gain, here):
        v = rms(v, gain)
        return v * cos_ref[here, :] + pltpu.roll(v, head // 2, 1) * sin_ref[here, :]

    def adapt(i, carry):
        here = pl.ds(pl.multiple_of(i * block, block), block)
        low = dot_nt(x_ref[here, :], s_ref[...].reshape(factors, width))
        low = jnp.where(meta_ref[here, 0:1] == colslot_ref[...], low, 0.0).astype(BF16)
        delta = ADAPTER_FACTOR * dot(low, up_ref[...])
        q = qf_ref[here, :] + delta[:, :query_cols]
        kv = (kvf_ref[here, :] + delta[:, query_cols:]).astype(BF16)
        for h in range(heads):
            cut = slice(h * head, (h + 1) * head)
            q_ref[here, cut] = turned(q[:, cut], qg, here).astype(BF16)
        kv_ref[here, :head] = turned(kv[:, :head].astype(F32), kg, here).astype(BF16)
        kv_ref[here, head:] = kv[:, head:]
        return carry

    loop(blocks, adapt, 0)

    def attend(target, offset):
        def one(i, carry):
            there = pl.ds(pl.multiple_of(i * block, block), block)
            here = pl.ds(pl.multiple_of(offset + i * block, block), block)
            allowed = (row_ref[1:2, :] <= meta_ref[here, 2:3]) & (
                row_ref[0:1, :] == meta_ref[here, 1:2]
            )
            for h in range(heads):
                cut = slice(h * head, (h + 1) * head)
                s = dot_nt(q_ref[here, cut], kv_ref[:, :head]) * scale
                raised = jnp.where(allowed, jnp.exp(s), 0.0)
                mixed = dot(raised.astype(BF16), kv_ref[:, head:])
                mixed = mixed / jnp.sum(raised, axis=1, keepdims=True)
                target[there, cut] = mixed.astype(BF16)
            return carry

        loop(blocks // 2, one, 0)

    attend(part_ref, rows // 2)
    attend(own_ref, 0)


def attention(spots, tokens, weights, meta, pieces, parts, adapters, holders):
    gain, wq, up, qg, kg = weights
    rows, width = tokens.shape
    chips, cols, piece_width = parts[0].shape
    query_cols = wq.shape[1]
    head = qg.shape[1]
    ranks = pieces[0].shape[1]
    half = jax.ShapeDtypeStruct((rows // 2, query_cols), BF16)
    flops = 2 * rows * (width * (adapters * ranks + query_cols + 2 * head) + rows * query_cols)
    return pl.pallas_call(
        functools.partial(attention_kernel, len(pieces), len(parts)),
        out_shape=(half, half, jax.ShapeDtypeStruct((rows, 2 * head), BF16)),
        in_specs=[SMEM] + [VMEM] * 10 + [ANY] * (1 + len(pieces) + len(parts)),
        out_specs=(VMEM, VMEM, VMEM),
        scratch_shapes=[
            pltpu.VMEM((rows, width), BF16),
            pltpu.VMEM((adapters, ranks, width), BF16),
            pltpu.VMEM((2 * chips, holders, cols, piece_width), BF16),
            pltpu.VMEM((rows, query_cols), F32),
            pltpu.VMEM((rows, 2 * head), F32),
            pltpu.VMEM((rows, query_cols), BF16),
            pltpu.SemaphoreType.DMA((2 * chips,)),
            pltpu.SemaphoreType.DMA((len(pieces),)),
            pltpu.SemaphoreType.DMA((2 * chips * holders,)),
        ],
        compiler_params=pltpu.CompilerParams(vmem_limit_bytes=40 * MIB),
        cost_estimate=pl.CostEstimate(
            flops=flops, bytes_accessed=14 * MIB, transcendentals=rows * rows
        ),
        name="attention",
    )(spots, gain, wq, up, *meta, qg, kg, tokens, *pieces, *parts)


def output_kernel(
    own_ref, got_ref, wo_ref, wo2_ref, sho_ref, sho2_ref, exo_ref, slot_ref, oslot_ref, *outs
):
    rows = own_ref.shape[0]
    own_rows, width = outs[0].shape
    block = min(256, rows)
    per = block // own_rows
    step = min(512, width)
    for i in range(rows // block):
        here = slice(i * block, (i + 1) * block)
        own, got = own_ref[here, :], got_ref[here, :]
        low = dot_nt(own, sho_ref[...]) + dot_nt(got, sho2_ref[...])
        low = jnp.where(slot_ref[here, :] == oslot_ref[...], low, 0.0)
        high = low.astype(BF16)
        rest = (low - high.astype(F32)).astype(BF16)
        for c in range(0, width, step):
            cut = slice(c, c + step)
            expand = exo_ref[:, cut]
            term = dot(own, wo_ref[:, cut]) + dot(got, wo2_ref[:, cut])
            term = term + ADAPTER_FACTOR * (dot(high, expand) + dot(rest, expand))
            term = term.astype(BF16)
            for b in range(per):
                outs[i * per + b][:, cut] = term[b * own_rows : (b + 1) * own_rows, :]


def output_terms(own, got, weights, slot, oslot, chips):
    rows, query_cols = own.shape
    width = weights[0].shape[1]
    shape = jax.ShapeDtypeStruct((rows // chips, width), BF16)
    return pl.pallas_call(
        output_kernel,
        out_shape=(shape,) * chips,
        in_specs=[VMEM] * 9,
        out_specs=(VMEM,) * chips,
        compiler_params=pltpu.CompilerParams(vmem_limit_bytes=32 * MIB),
        cost_estimate=pl.CostEstimate(
            flops=4 * rows * query_cols * width, bytes_accessed=8 * MIB, transcendentals=0
        ),
        name="output_terms",
    )(own, got, *weights, slot, oslot)


def pages_kernel(first_ref, length_ref, page_ref, entries_ref, out_ref):
    columns, extent = entries_ref.shape
    rows = extent - PAGE
    window = 2 * PAGE
    gap = lax.broadcasted_iota(jnp.int32, (window, PAGE), 0) - lax.broadcasted_iota(
        jnp.int32, (window, PAGE), 1
    )
    lane = lax.broadcasted_iota(jnp.int32, (columns, PAGE), 1)

    def one(n, carry):
        length = length_ref[n]
        page = page_ref[n]

        @pl.when(length > 0)
        def _():
            first = jnp.minimum(first_ref[n], rows - 1)
            base = pl.multiple_of(first // PAGE * PAGE, PAGE)
            pick = (gap == first - base).astype(F32).astype(BF16)
            moved = dot(entries_ref[:, pl.ds(base, window)], pick)
            out_ref[page] = jnp.where(lane < length, moved, 0.0).astype(BF16)

        @pl.when(length <= 0)
        def _():
            out_ref[page] = jnp.zeros((columns, PAGE), BF16)

        return carry

    lax.fori_loop(0, page_ref.shape[0], one, 0)


def fill_pages(first, length, page, entries):
    rows, columns = entries.shape
    count = page.shape[0]
    turned = jnp.pad(entries.T, ((0, 0), (0, PAGE)))
    return pl.pallas_call(
        pages_kernel,
        out_shape=jax.ShapeDtypeStruct((count, columns, PAGE), BF16),
        in_specs=[SMEM, SMEM, SMEM, VMEM],
        out_specs=VMEM,
        compiler_params=pltpu.CompilerParams(vmem_limit_bytes=32 * MIB),
        cost_estimate=pl.CostEstimate(
            flops=count * columns * PAGE * PAGE * 16, bytes_accessed=4 * MIB, transcendentals=0
        ),
        name="fill_pages",
    )(first, length, page, turned)


def experts_kernel(spot_ref, slot_ref, weight_ref, tokens_ref, *refs):
    (gate_ref, up_ref, down_ref, own_ref, part_ref) = refs[:5]
    (x_ref, rows_ref, y_ref, gate_buf, up_buf, down_buf, x_sems, w_sems) = refs[5:]
    total, width = x_ref.shape
    devices = x_sems.shape[0]
    chips = devices // 2
    own_rows = total // devices
    experts = slot_ref.shape[1]
    capacity = rows_ref.shape[1] // experts
    chip, core = spot_ref[0], spot_ref[1]
    slots = gate_buf.shape[0]
    streams = ((gate_ref, gate_buf), (up_ref, up_buf), (down_ref, down_buf))

    def copy(k, e, s):
        source, buffer = streams[k]
        return pltpu.make_async_copy(source.at[e], buffer.at[s], w_sems.at[k, s])

    copies = []
    for q in range(2):
        for j in range(chips):
            i = q * chips + j
            device = lax.rem(chip + j, chips) * 2 + (core ^ q)
            source = tokens_ref.at[pl.ds(pl.multiple_of(device * own_rows, own_rows), own_rows)]
            target = x_ref.at[pl.ds(i * own_rows, own_rows)]
            copies.append(pltpu.make_async_copy(source, target, x_sems.at[i]))
            copies[-1].start()
    for e in range(min(slots, experts)):
        for k in range(3):
            copy(k, e, e).start()
    for item in copies:
        item.wait()
    step = min(512, width)
    line = lax.broadcasted_iota(jnp.int32, (total, capacity), 1)
    pick = jnp.concatenate(
        [(slot_ref[:, n : n + 1] == line).astype(F32).astype(BF16) for n in range(experts)], axis=1
    )
    for c in range(0, width, step):
        rows_ref[c : c + step, :] = dot(x_ref[:, c : c + step].T, pick).astype(BF16)

    def one(e, carry):
        s = lax.rem(e, slots)
        here = pl.ds(pl.multiple_of(e * capacity, capacity), capacity)
        x = rows_ref[:, here]
        copy(0, e, s).wait()
        gate = dot(gate_buf[s], x)
        copy(1, e, s).wait()
        up = dot(up_buf[s], x)
        hidden = (gate / (1.0 + jnp.exp(-gate)) * up).T.astype(BF16)
        copy(2, e, s).wait()
        y_ref[here, :] = dot(hidden, down_buf[s]).astype(BF16)

        @pl.when(e + slots < experts)
        def _():
            for k in range(3):
                copy(k, e + slots, s).start()

        return carry

    lax.fori_loop(0, experts, one, 0)

    tile = min(256, total // 2)
    line = lax.broadcasted_iota(jnp.int32, (tile, capacity), 1)

    def combine(target, offset):
        def mix(i, carry):
            there = pl.ds(pl.multiple_of(i * tile, tile), tile)
            here = pl.ds(pl.multiple_of(offset + i * tile, tile), tile)
            spread = jnp.concatenate(
                [
                    jnp.where(
                        slot_ref[here, n : n + 1] == line, weight_ref[here, n : n + 1], 0.0
                    ).astype(BF16)
                    for n in range(experts)
                ],
                axis=1,
            )
            for c in range(0, width, step):
                target[there, c : c + step] = dot(spread, y_ref[:, c : c + step]).astype(BF16)
            return carry

        loop(total // 2 // tile, mix, 0)

    combine(part_ref, total // 2)
    combine(own_ref, 0)


def expert_layer(spots, slot, weight, tokens, gate, up, down, capacity, devices):
    experts, hidden, width = gate.shape
    total = slot.shape[0]
    slots = min(3 if total <= 512 else 2, experts)
    half = jax.ShapeDtypeStruct((total // 2, width), BF16)
    return pl.pallas_call(
        experts_kernel,
        out_shape=(half, half),
        in_specs=[SMEM, VMEM, VMEM] + [ANY] * 4,
        out_specs=(VMEM, VMEM),
        scratch_shapes=[
            pltpu.VMEM((total, width), BF16),
            pltpu.VMEM((width, experts * capacity), BF16),
            pltpu.VMEM((experts * capacity, width), BF16),
            pltpu.VMEM((slots, hidden, width), BF16),
            pltpu.VMEM((slots, hidden, width), BF16),
            pltpu.VMEM((slots, hidden, width), BF16),
            pltpu.SemaphoreType.DMA((devices,)),
            pltpu.SemaphoreType.DMA((3, slots)),
        ],
        compiler_params=pltpu.CompilerParams(vmem_limit_bytes=60 * MIB),
        cost_estimate=pl.CostEstimate(
            flops=6 * experts * capacity * hidden * width,
            bytes_accessed=6 * experts * hidden * width,
            transcendentals=experts * capacity * hidden,
        ),
        name="experts",
    )(spots, slot, weight, tokens, gate, up, down)


def other_core(value, parts):
    return lax.ppermute(value, "tensor", [(i, i ^ 1) for i in range(parts)])


def turn_chips(value, parts, by):
    return lax.ppermute(value, "tensor", [(i, (i + 2 * by) % parts) for i in range(parts)])


def swap_holder(value, holders, by):
    return lax.ppermute(value, "dp", [(i, i ^ by) for i in range(holders)])


def from_here(rows, chip, core, chips):
    split = rows.reshape((chips, 2, -1) + rows.shape[1:])
    split = jnp.where(core == 0, split, split[:, ::-1])
    split = lax.dynamic_slice_in_dim(jnp.concatenate([split, split]), chip, chips, 0)
    return jnp.swapaxes(split, 0, 1).reshape(rows.shape)


def to_group(rows, chip, core, chips):
    split = jnp.swapaxes(rows.reshape((2, chips, -1) + rows.shape[1:]), 0, 1)
    split = lax.dynamic_slice_in_dim(
        jnp.concatenate([split, split]), (chips - chip) % chips, chips, 0
    )
    return jnp.where(core == 0, split, split[:, ::-1]).reshape(rows.shape)


def head_weights(w_kv, head_of_chip, chip, holder, parts, holders):
    chips = parts // 2
    cols, _, width = w_kv.shape
    piece = width // holders

    def cut(turn):
        to = head_of_chip((chip + turn) % chips)
        return lax.dynamic_slice(w_kv, (0, to, holder * piece), (cols, 1, piece))[:, 0]

    mine = [cut(0)] + [turn_chips(cut(r), parts, r) for r in range(chips - 1, 0, -1)]
    mine = jnp.stack(mine)
    full = [mine] + [swap_holder(mine, holders, r) for r in range(1, holders)]
    return full + [other_core(piece, parts) for piece in full]


def local(
    tokens,
    attn_gain,
    moe_gain,
    q_gain,
    k_gain,
    query_weight,
    w_kv,
    w_o,
    w_gate,
    w_up,
    w_down,
    shrink_qkv,
    shrink_o,
    query_up_factors,
    key_value_up_factors,
    expand_o,
    lengths,
    groups,
    adapter_of_request,
    adapter_slot,
    page_table,
    expert_ids,
    expert_gates,
):
    parts = lax.axis_size("tensor")
    place = lax.axis_index("tensor")
    holders = lax.axis_size("dp")
    holder = lax.axis_index("dp")
    chips, chip, core = parts // 2, place // 2, place % 2
    own_rows, width = tokens.shape
    total = own_rows * parts
    head_length = q_gain.shape[0]
    adapters, rank, kv_width = key_value_up_factors.shape
    kv_heads = kv_width // (2 * head_length)
    held, ranks = shrink_qkv.shape[:2]
    head = place * kv_heads // parts
    query_cols = query_weight.shape[1]

    gathered = lax.all_gather(tokens, "tensor", axis=0, tiled=True)
    head_parts = head_weights(
        w_kv, lambda c: 2 * c * kv_heads // parts, chip, holder, parts, holders
    )
    half = held // 2
    half_own = lax.dynamic_slice_in_dim(shrink_qkv, core * half, half, 0)
    pieces, spots = [shrink_qkv], [chip, core, holder, holder * held]
    for r in range(1, holders):
        got = swap_holder(half_own, holders, r)
        pieces += [got, other_core(got, parts)]
        begin = (holder ^ r) * held
        spots += [begin + core * half, begin + (1 - core) * half]
    shrink_rows = shrink_o.reshape(adapters * rank, query_cols)
    w_o_other = other_core(w_o, parts)
    shrink_other = other_core(shrink_rows, parts)

    line = jnp.arange(total, dtype=jnp.int32)
    side, number = line // (total // 2), line // own_rows % chips
    position = ((number + chip) % chips * 2 + (side ^ core)) * own_rows + line % own_rows
    length_row, group_row, adapter_row = lengths[0], groups[0], adapter_of_request[0]
    ends = jnp.cumsum(length_row)
    starts = ends - length_row
    request = jnp.sum((ends[None, :] <= position[:, None]).astype(jnp.int32), axis=1)
    same = group_row[:, None] == group_row[None, :]
    group_first = jnp.min(jnp.where(same, starts[None, :], total), axis=1)
    slot_of_request = lookup(adapter_row, adapter_slot)
    group = lookup(request, group_row)
    rope_pos = position - lookup(request, group_first)
    slot = lookup(request, slot_of_request)
    meta_col = jnp.stack([slot, group, position], axis=1)
    meta_row = jnp.stack([group, position], axis=0)
    freq = jnp.exp(
        -jnp.arange(head_length // 2, dtype=F32) * (2.0 * math.log(ROPE_BASE) / head_length)
    )
    angle = rope_pos.astype(F32)[:, None] * freq[None, :]
    cosine, sine = jnp.cos(angle), jnp.sin(angle)
    cosine = jnp.concatenate([cosine, cosine], axis=1)
    sine = jnp.concatenate([-sine, sine], axis=1)
    colslot = (jnp.arange(adapters * ranks, dtype=jnp.int32) // ranks)[None, :]
    oslot = (jnp.arange(adapters * rank, dtype=jnp.int32) // rank)[None, :]

    up_kv = lax.dynamic_index_in_dim(
        key_value_up_factors.reshape(adapters, rank, kv_heads, 2, head_length), head, 2, keepdims=False
    )
    up = jnp.concatenate(
        [
            jnp.pad(query_up_factors, ((0, 0), (0, 2 * rank), (0, 0))),
            jnp.pad(up_kv[:, :, 0], ((0, 0), (rank, rank), (0, 0))),
            jnp.pad(up_kv[:, :, 1], ((0, 0), (2 * rank, 0), (0, 0))),
        ],
        axis=2,
    ).reshape(adapters * ranks, query_cols + 2 * head_length)

    weights = (
        attn_gain.reshape(1, -1),
        query_weight,
        up,
        q_gain.reshape(1, -1),
        k_gain.reshape(1, -1),
    )
    meta = (meta_col, meta_row, colslot, cosine, sine)
    mixed, mixed_part, entries = attention(
        jnp.stack(spots).astype(jnp.int32),
        gathered,
        weights,
        meta,
        pieces,
        head_parts,
        adapters,
        holders,
    )

    out_weights = (
        w_o,
        w_o_other,
        shrink_rows,
        shrink_other,
        expand_o.reshape(adapters * rank, width),
    )
    sums = output_terms(
        mixed, other_core(mixed_part, parts), out_weights, slot[: total // 2, None], oslot, chips
    )
    arrived = [sums[0]] + [turn_chips(sums[r], parts, r) for r in range(1, chips)]
    attn_own, moe_own = residual_norm(tokens, moe_gain, arrived)

    local_cols = kv_width // parts
    kept = lax.dynamic_slice_in_dim(
        entries, place * local_cols - head * 2 * head_length, local_cols, 1
    )
    page_row = page_table[0]
    per_request = page_row.shape[0] // length_row.shape[0]
    offset = PAGE * jnp.arange(per_request, dtype=jnp.int32)[None, :]
    page_first = (starts[:, None] + offset).reshape(-1)
    page_length = jnp.clip(length_row[:, None] - offset, 0, PAGE).reshape(-1)
    kv_pages = fill_pages(page_first, page_length, page_row, to_group(kept, chip, core, chips))

    experts = w_gate.shape[0]
    capacity = CAP_DEV * parts
    ids = from_here(expert_ids, chip, core, chips)
    gates = from_here(expert_gates, chip, core, chips)
    share = gates / jnp.sum(gates, axis=1, keepdims=True)
    own_experts = place * experts + jnp.arange(experts, dtype=jnp.int32)
    chosen = ids[:, :, None] == own_experts[None, None, :]
    hit = jnp.any(chosen, axis=1)
    weight = jnp.sum(jnp.where(chosen, share[:, :, None], 0.0), axis=1)
    before = dot((line[:, None] > line[None, :]).astype(BF16), hit.astype(BF16)).astype(jnp.int32)
    slot_in = jnp.where(hit, before, -1)

    own_terms, part_terms = expert_layer(
        jnp.stack([chip, core]).astype(jnp.int32),
        slot_in,
        weight,
        lax.all_gather(moe_own, "tensor", axis=0, tiled=True),
        w_gate,
        w_up,
        w_down,
        capacity,
        parts,
    )
    sums = pair_sum(own_terms, other_core(part_terms, parts), chips)
    arrived = [sums[0]] + [turn_chips(sums[r], parts, r) for r in range(1, chips)]
    moe_total = sum(part.astype(F32) for part in arrived).astype(BF16)
    return (attn_own, moe_total, kv_pages)


def solution(mesh):
    placed = (
        P(("dp", "tensor"), None),
        P(),
        P(),
        P(),
        P(),
        P(None, "tensor"),
        P("tensor", None, None),
        P("tensor", None),
        P("tensor", None, None),
        P("tensor", None, None),
        P("tensor", None, None),
        P("dp", None, None),
        P(None, None, "tensor"),
        P(None, None, "tensor"),
        P(),
        P(),
        P("dp", None),
        P("dp", None),
        P("dp", None),
        P(),
        P("dp", None),
        P("dp", None),
        P("dp", None),
    )
    return jax.shard_map(
        local,
        mesh=mesh,
        in_specs=placed,
        out_specs=(P(("dp", "tensor"), None), P(("dp", "tensor"), None), P("dp", "tensor", None)),
        check_vma=False,
    )
```

```python
import functools
import math

import jax
import jax.numpy as jnp
from jax import lax
from jax.experimental import pallas as pl
from jax.experimental.pallas import tpu as pltpu
from jax.sharding import PartitionSpec as P

PAGE = 128
CAP_DEV = 16
NORM_EPS = 1e-06
ROPE_BASE = 1000000.0
ADAPTER_FACTOR = 0.5
MIB = 1 << 20
BF16 = jnp.bfloat16
F32 = jnp.float32
VMEM = pl.BlockSpec(memory_space=pltpu.VMEM)
SMEM = pl.BlockSpec(memory_space=pltpu.SMEM)
ANY = pl.BlockSpec(memory_space=pl.ANY)
HBM = pl.BlockSpec(memory_space=pltpu.HBM)


def dot(a, b):
    return jnp.dot(a, b, preferred_element_type=F32)


def dot_nt(a, b):
    return lax.dot_general(a, b, (((1,), (1,)), ((), ())), preferred_element_type=F32)


def lookup(index_value, table):
    match = index_value[:, None] == jnp.arange(table.shape[0], dtype=jnp.int32)[None, :]
    return jnp.sum(jnp.where(match, table[None, :], 0), axis=1)


def loop(count, body, carry):
    if count <= 2:
        for i in range(count):
            carry = body(i, carry)
        return carry
    return lax.fori_loop(0, count, body, carry)


def rms(v, gain):
    return v * lax.rsqrt(jnp.mean(v * v, axis=-1, keepdims=True) + NORM_EPS) * gain


def residual_kernel(x_ref, gain_ref, *refs):
    parts, (attn_ref, out_ref) = refs[:-2], refs[-2:]
    total = parts[0][...].astype(F32)
    for part in parts[1:]:
        total = total + part[...].astype(F32)
    attn_ref[...] = total.astype(BF16)
    out_ref[...] = rms(x_ref[...].astype(F32) + total, gain_ref[...].astype(F32)).astype(BF16)


def residual_norm(x, gain, parts):
    shape = jax.ShapeDtypeStruct(x.shape, BF16)
    return pl.pallas_call(
        residual_kernel,
        out_shape=(shape, shape),
        in_specs=[VMEM] * (2 + len(parts)),
        out_specs=(VMEM, VMEM),
        name="residual_norm",
    )(x, gain.reshape(1, -1), *parts)


def pair_kernel(a_ref, b_ref, *outs):
    rows = outs[0].shape[0]
    for i, out in enumerate(outs):
        here = slice(i * rows, (i + 1) * rows)
        out[...] = (a_ref[here, :].astype(F32) + b_ref[here, :].astype(F32)).astype(BF16)


def pair_sum(a, b, count):
    shape = jax.ShapeDtypeStruct((a.shape[0] // count, a.shape[1]), BF16)
    return pl.pallas_call(
        pair_kernel,
        out_shape=(shape,) * count,
        in_specs=[VMEM, VMEM],
        out_specs=(VMEM,) * count,
        compiler_params=pltpu.CompilerParams(vmem_limit_bytes=24 * MIB),
        name="pair_sum",
    )(a, b)


def attention_kernel(
    factor_blocks,
    head_blocks,
    spot_ref,
    gain_ref,
    wq_ref,
    up_ref,
    meta_ref,
    row_ref,
    colslot_ref,
    cos_ref,
    sin_ref,
    qg_ref,
    kg_ref,
    *refs,
):
    tokens_ref, refs = refs[0], refs[1:]
    pieces, refs = refs[:factor_blocks], refs[factor_blocks:]
    parts, refs = refs[:head_blocks], refs[head_blocks:]
    own_ref, part_ref, kv_ref = refs[:3]
    x_ref, s_ref, w_ref, qf_ref, kvf_ref, q_ref, x_sems, s_sems, w_sems = refs[3:]
    rows, width = x_ref.shape
    query_cols = wq_ref.shape[1]
    head = qg_ref.shape[1]
    heads = query_cols // head
    block = min(256, rows // 2)
    blocks = rows // block
    scale = head**-0.5
    devices, holders, cols, piece_width = w_ref.shape
    chips = devices // 2
    own_rows = rows // devices
    chip, core, holder = spot_ref[0], spot_ref[1], spot_ref[2]
    token_copies, factor_copies, head_copies = [], [], []
    for q in range(2):
        for j in range(chips):
            i = q * chips + j
            device = lax.rem(chip + j, chips) * 2 + (core ^ q)
            source = tokens_ref.at[pl.ds(pl.multiple_of(device * own_rows, own_rows), own_rows)]
            target = x_ref.at[pl.ds(i * own_rows, own_rows)]
            token_copies.append(pltpu.make_async_copy(source, target, x_sems.at[i]))
            token_copies[-1].start()
    for q in range(2):
        for r in range(holders):
            for j in range(chips):
                device = lax.rem(chip + j, chips) * 2 + (core ^ q)
                target = w_ref.at[device, holder ^ r]
                head_copies.append(
                    pltpu.make_async_copy(
                        parts[q * holders + r].at[j],
                        target,
                        w_sems.at[(q * holders + r) * chips + j],
                    )
                )
                head_copies[-1].start()
    for i, piece in enumerate(pieces):
        target = s_ref.at[pl.ds(spot_ref[3 + i], piece.shape[0])]
        factor_copies.append(pltpu.make_async_copy(piece, target, s_sems.at[i]))
        factor_copies[-1].start()
    factors = s_ref.shape[0] * s_ref.shape[1]
    gain = gain_ref[...].astype(F32)
    qg = qg_ref[...].astype(F32)
    kg = kg_ref[...].astype(F32)

    for copy in token_copies + head_copies:
        copy.wait()

    def project(i, carry):
        here = pl.ds(pl.multiple_of(i * block, block), block)
        x = rms(x_ref[here, :].astype(F32), gain).astype(BF16)
        x_ref[here, :] = x
        qf_ref[here, :] = dot(x, wq_ref[...])
        kv = 0.0
        for r in range(holders):
            w = w_ref[:, r].reshape(devices * cols, piece_width)
            kv = kv + dot_nt(x[:, r * piece_width : (r + 1) * piece_width], w)
        kvf_ref[here, :] = kv
        return carry

    loop(blocks, project, 0)

    for copy in factor_copies:
        copy.wait()

    def turned(v, gain, here):
        v = rms(v, gain)
        return v * cos_ref[here, :] + pltpu.roll(v, head // 2, 1) * sin_ref[here, :]

    def adapt(i, carry):
        here = pl.ds(pl.multiple_of(i * block, block), block)
        low = dot_nt(x_ref[here, :], s_ref[...].reshape(factors, width))
        low = jnp.where(meta_ref[here, 0:1] == colslot_ref[...], low, 0.0).astype(BF16)
        delta = ADAPTER_FACTOR * dot(low, up_ref[...])
        q = qf_ref[here, :] + delta[:, :query_cols]
        kv = (kvf_ref[here, :] + delta[:, query_cols:]).astype(BF16)
        for h in range(heads):
            cut = slice(h * head, (h + 1) * head)
            q_ref[here, cut] = turned(q[:, cut], qg, here).astype(BF16)
        kv_ref[here, :head] = turned(kv[:, :head].astype(F32), kg, here).astype(BF16)
        kv_ref[here, head:] = kv[:, head:]
        return carry

    loop(blocks, adapt, 0)

    def attend(target, offset):
        def one(i, carry):
            there = pl.ds(pl.multiple_of(i * block, block), block)
            here = pl.ds(pl.multiple_of(offset + i * block, block), block)
            allowed = (row_ref[1:2, :] <= meta_ref[here, 2:3]) & (
                row_ref[0:1, :] == meta_ref[here, 1:2]
            )
            for h in range(heads):
                cut = slice(h * head, (h + 1) * head)
                s = dot_nt(q_ref[here, cut], kv_ref[:, :head]) * scale
                raised = jnp.where(allowed, jnp.exp(s), 0.0)
                mixed = dot(raised.astype(BF16), kv_ref[:, head:])
                mixed = mixed / jnp.sum(raised, axis=1, keepdims=True)
                target[there, cut] = mixed.astype(BF16)
            return carry

        loop(blocks // 2, one, 0)

    attend(part_ref, rows // 2)
    attend(own_ref, 0)


def attention(spots, tokens, weights, meta, pieces, parts, adapters, holders):
    gain, wq, up, qg, kg = weights
    rows, width = tokens.shape
    chips, cols, piece_width = parts[0].shape
    query_cols = wq.shape[1]
    head = qg.shape[1]
    ranks = pieces[0].shape[1]
    half = jax.ShapeDtypeStruct((rows // 2, query_cols), BF16)
    flops = 2 * rows * (width * (adapters * ranks + query_cols + 2 * head) + rows * query_cols)
    return pl.pallas_call(
        functools.partial(attention_kernel, len(pieces), len(parts)),
        out_shape=(half, half, jax.ShapeDtypeStruct((rows, 2 * head), BF16)),
        in_specs=[SMEM] + [VMEM] * 10 + [ANY] * (1 + len(pieces) + len(parts)),
        out_specs=(VMEM, VMEM, VMEM),
        scratch_shapes=[
            pltpu.VMEM((rows, width), BF16),
            pltpu.VMEM((adapters, ranks, width), BF16),
            pltpu.VMEM((2 * chips, holders, cols, piece_width), BF16),
            pltpu.VMEM((rows, query_cols), F32),
            pltpu.VMEM((rows, 2 * head), F32),
            pltpu.VMEM((rows, query_cols), BF16),
            pltpu.SemaphoreType.DMA((2 * chips,)),
            pltpu.SemaphoreType.DMA((len(pieces),)),
            pltpu.SemaphoreType.DMA((2 * chips * holders,)),
        ],
        compiler_params=pltpu.CompilerParams(vmem_limit_bytes=60 * MIB),
        cost_estimate=pl.CostEstimate(
            flops=flops, bytes_accessed=14 * MIB, transcendentals=rows * rows
        ),
        name="attention",
    )(spots, gain, wq, up, *meta, qg, kg, tokens, *pieces, *parts)


def output_kernel(
    own_ref, got_ref, wo_ref, wo2_ref, sho_ref, sho2_ref, exo_ref, slot_ref, oslot_ref, *outs
):
    rows = own_ref.shape[0]
    own_rows, width = outs[0].shape
    block = min(256, rows)
    per = block // own_rows
    step = min(512, width)
    for i in range(rows // block):
        here = slice(i * block, (i + 1) * block)
        own, got = own_ref[here, :], got_ref[here, :]
        low = dot_nt(own, sho_ref[...]) + dot_nt(got, sho2_ref[...])
        low = jnp.where(slot_ref[here, :] == oslot_ref[...], low, 0.0)
        high = low.astype(BF16)
        rest = (low - high.astype(F32)).astype(BF16)
        for c in range(0, width, step):
            cut = slice(c, c + step)
            expand = exo_ref[:, cut]
            term = dot(own, wo_ref[:, cut]) + dot(got, wo2_ref[:, cut])
            term = term + ADAPTER_FACTOR * (dot(high, expand) + dot(rest, expand))
            term = term.astype(BF16)
            for b in range(per):
                outs[i * per + b][:, cut] = term[b * own_rows : (b + 1) * own_rows, :]


def output_terms(own, got, weights, slot, oslot, chips):
    rows, query_cols = own.shape
    width = weights[0].shape[1]
    shape = jax.ShapeDtypeStruct((rows // chips, width), BF16)
    return pl.pallas_call(
        output_kernel,
        out_shape=(shape,) * chips,
        in_specs=[VMEM] * 9,
        out_specs=(VMEM,) * chips,
        compiler_params=pltpu.CompilerParams(vmem_limit_bytes=60 * MIB),
        cost_estimate=pl.CostEstimate(
            flops=4 * rows * query_cols * width, bytes_accessed=8 * MIB, transcendentals=0
        ),
        name="output_terms",
    )(own, got, *weights, slot, oslot)


def pages_kernel(first_ref, length_ref, page_ref, entries_ref, out_ref):
    columns, extent = entries_ref.shape
    rows = extent - PAGE
    window = 2 * PAGE
    gap = lax.broadcasted_iota(jnp.int32, (window, PAGE), 0) - lax.broadcasted_iota(
        jnp.int32, (window, PAGE), 1
    )
    lane = lax.broadcasted_iota(jnp.int32, (columns, PAGE), 1)

    def one(n, carry):
        length = length_ref[n]
        page = page_ref[n]

        @pl.when(length > 0)
        def _():
            first = jnp.minimum(first_ref[n], rows - 1)
            base = pl.multiple_of(first // PAGE * PAGE, PAGE)
            pick = (gap == first - base).astype(F32).astype(BF16)
            moved = dot(entries_ref[:, pl.ds(base, window)], pick)
            out_ref[page] = jnp.where(lane < length, moved, 0.0).astype(BF16)

        @pl.when(length <= 0)
        def _():
            out_ref[page] = jnp.zeros((columns, PAGE), BF16)

        return carry

    lax.fori_loop(0, page_ref.shape[0], one, 0)


def fill_pages(first, length, page, entries):
    rows, columns = entries.shape
    count = page.shape[0]
    turned = jnp.pad(entries.T, ((0, 0), (0, PAGE)))
    return pl.pallas_call(
        pages_kernel,
        out_shape=jax.ShapeDtypeStruct((count, columns, PAGE), BF16),
        in_specs=[SMEM, SMEM, SMEM, VMEM],
        out_specs=VMEM,
        compiler_params=pltpu.CompilerParams(vmem_limit_bytes=32 * MIB),
        cost_estimate=pl.CostEstimate(
            flops=count * columns * PAGE * PAGE * 16, bytes_accessed=4 * MIB, transcendentals=0
        ),
        name="fill_pages",
    )(first, length, page, turned)


def experts_kernel(spot_ref, slot_ref, slot_t_ref, weight_ref, gate_ref, tokens_ref, *refs):
    (up_ref, down_ref, own_ref, part_ref) = refs[:4]
    (x_ref, rows_ref, y_ref, up_buf, down_buf, x_sems, w_sems) = refs[4:]
    total, width = x_ref.shape
    devices = x_sems.shape[0]
    chips = devices // 2
    own_rows = total // devices
    experts = slot_ref.shape[1]
    capacity = rows_ref.shape[0] // experts
    chip, core = spot_ref[0], spot_ref[1]
    slots = up_buf.shape[0]
    streams = ((up_ref, up_buf), (down_ref, down_buf))

    def copy(k, e, s):
        source, buffer = streams[k]
        return pltpu.make_async_copy(source.at[e], buffer.at[s], w_sems.at[k, s])

    copies = []
    for q in range(2):
        for j in range(chips):
            i = q * chips + j
            device = lax.rem(chip + j, chips) * 2 + (core ^ q)
            source = tokens_ref.at[pl.ds(pl.multiple_of(device * own_rows, own_rows), own_rows)]
            target = x_ref.at[pl.ds(i * own_rows, own_rows)]
            copies.append(pltpu.make_async_copy(source, target, x_sems.at[i]))
            copies[-1].start()
    for e in range(min(slots, experts)):
        for k in range(2):
            copy(k, e, e).start()
    for item in copies:
        item.wait()
    step = min(512, width)
    line = lax.broadcasted_iota(jnp.int32, (capacity, total), 0)
    pick = jnp.concatenate(
        [(slot_t_ref[n : n + 1, :] == line).astype(F32).astype(BF16) for n in range(experts)], axis=0
    )
    for c in range(0, width, step):
        rows_ref[:, c : c + step] = dot(pick, x_ref[:, c : c + step]).astype(BF16)

    def one(e, carry):
        s = lax.rem(e, slots)
        here = pl.ds(pl.multiple_of(e * capacity, capacity), capacity)
        x = rows_ref[here, :]
        gate = dot_nt(x, gate_ref[e])
        copy(0, e, s).wait()
        up = dot_nt(x, up_buf[s])
        hidden = (gate / (1.0 + jnp.exp(-gate)) * up).astype(BF16)

        @pl.when(e + slots < experts)
        def _():
            copy(0, e + slots, s).start()

        copy(1, e, s).wait()
        y_ref[here, :] = dot(hidden, down_buf[s]).astype(BF16)

        @pl.when(e + slots < experts)
        def _():
            copy(1, e + slots, s).start()

        return carry

    lax.fori_loop(0, experts, one, 0)

    tile = min(256, total // 2)
    line = lax.broadcasted_iota(jnp.int32, (tile, capacity), 1)

    def combine(target, offset):
        def mix(i, carry):
            there = pl.ds(pl.multiple_of(i * tile, tile), tile)
            here = pl.ds(pl.multiple_of(offset + i * tile, tile), tile)
            spread = jnp.concatenate(
                [
                    jnp.where(
                        slot_ref[here, n : n + 1] == line, weight_ref[here, n : n + 1], 0.0
                    ).astype(BF16)
                    for n in range(experts)
                ],
                axis=1,
            )
            for c in range(0, width, step):
                target[there, c : c + step] = dot(spread, y_ref[:, c : c + step]).astype(BF16)
            return carry

        loop(total // 2 // tile, mix, 0)

    combine(part_ref, total // 2)
    combine(own_ref, 0)


def hold_kernel(source_ref, out_ref, sems):
    copies = [
        pltpu.make_async_copy(source_ref.at[i], out_ref.at[i], sems.at[i])
        for i in range(source_ref.shape[0])
    ]
    for copy in copies:
        copy.start()
    for copy in copies:
        copy.wait()


def hold(weights):
    size = 2 * weights.size
    return pl.pallas_call(
        hold_kernel,
        out_shape=pltpu.VMEM(weights.shape, BF16),
        in_specs=[HBM],
        out_specs=VMEM,
        scratch_shapes=[pltpu.SemaphoreType.DMA((weights.shape[0],))],
        compiler_params=pltpu.CompilerParams(vmem_limit_bytes=4 * MIB),
        cost_estimate=pl.CostEstimate(flops=0, bytes_accessed=2 * size, transcendentals=0),
        name="hold",
    )(pltpu.with_memory_space_constraint(weights, pltpu.HBM))


def expert_layer(spots, slot, slot_t, weight, tokens, gate, up, down, capacity, devices):
    experts, hidden, width = gate.shape
    total = slot.shape[0]
    slots = min(3 if total <= 512 else 2, experts)
    half = jax.ShapeDtypeStruct((total // 2, width), BF16)
    return pl.pallas_call(
        experts_kernel,
        out_shape=(half, half),
        in_specs=[SMEM] + [VMEM] * 4 + [HBM] * 3,
        out_specs=(VMEM, VMEM),
        scratch_shapes=[
            pltpu.VMEM((total, width), BF16),
            pltpu.VMEM((experts * capacity, width), BF16),
            pltpu.VMEM((experts * capacity, width), BF16),
            pltpu.VMEM((slots, hidden, width), BF16),
            pltpu.VMEM((slots, hidden, width), BF16),
            pltpu.SemaphoreType.DMA((devices,)),
            pltpu.SemaphoreType.DMA((2, slots)),
        ],
        compiler_params=pltpu.CompilerParams(
            vmem_limit_bytes=(36 if total <= 512 else 54) * MIB
        ),
        cost_estimate=pl.CostEstimate(
            flops=6 * experts * capacity * hidden * width,
            bytes_accessed=6 * experts * hidden * width,
            transcendentals=experts * capacity * hidden,
        ),
        name="experts",
    )(
        spots,
        slot,
        slot_t,
        weight,
        pltpu.with_memory_space_constraint(gate, pltpu.VMEM),
        tokens,
        up,
        down,
    )


def other_core(value, parts):
    return lax.ppermute(value, "tensor", [(i, i ^ 1) for i in range(parts)])


def turn_chips(value, parts, by):
    return lax.ppermute(value, "tensor", [(i, (i + 2 * by) % parts) for i in range(parts)])


def swap_holder(value, holders, by):
    return lax.ppermute(value, "dp", [(i, i ^ by) for i in range(holders)])


def from_here(rows, chip, core, chips):
    split = rows.reshape((chips, 2, -1) + rows.shape[1:])
    split = jnp.where(core == 0, split, split[:, ::-1])
    split = lax.dynamic_slice_in_dim(jnp.concatenate([split, split]), chip, chips, 0)
    return jnp.swapaxes(split, 0, 1).reshape(rows.shape)


def to_group(rows, chip, core, chips):
    split = jnp.swapaxes(rows.reshape((2, chips, -1) + rows.shape[1:]), 0, 1)
    split = lax.dynamic_slice_in_dim(
        jnp.concatenate([split, split]), (chips - chip) % chips, chips, 0
    )
    return jnp.where(core == 0, split, split[:, ::-1]).reshape(rows.shape)


def head_weights(w_kv, head_of_chip, chip, holder, parts, holders):
    chips = parts // 2
    cols, _, width = w_kv.shape
    piece = width // holders

    def cut(turn):
        to = head_of_chip((chip + turn) % chips)
        return lax.dynamic_slice(w_kv, (0, to, holder * piece), (cols, 1, piece))[:, 0]

    mine = [cut(0)] + [turn_chips(cut(r), parts, r) for r in range(chips - 1, 0, -1)]
    mine = jnp.stack(mine)
    full = [mine] + [swap_holder(mine, holders, r) for r in range(1, holders)]
    return full + [other_core(piece, parts) for piece in full]


def local(
    tokens,
    attn_gain,
    moe_gain,
    q_gain,
    k_gain,
    query_weight,
    w_kv,
    w_o,
    w_gate,
    w_up,
    w_down,
    shrink_qkv,
    shrink_o,
    query_up_factors,
    key_value_up_factors,
    expand_o,
    lengths,
    groups,
    adapter_of_request,
    adapter_slot,
    page_table,
    expert_ids,
    expert_gates,
):
    parts = lax.axis_size("tensor")
    place = lax.axis_index("tensor")
    holders = lax.axis_size("dp")
    holder = lax.axis_index("dp")
    chips, chip, core = parts // 2, place // 2, place % 2
    own_rows, width = tokens.shape
    total = own_rows * parts
    head_length = q_gain.shape[0]
    adapters, rank, kv_width = key_value_up_factors.shape
    kv_heads = kv_width // (2 * head_length)
    held, ranks = shrink_qkv.shape[:2]
    head = place * kv_heads // parts
    query_cols = query_weight.shape[1]

    gathered = lax.all_gather(tokens, "tensor", axis=0, tiled=True)
    half = held // 2
    half_own = lax.dynamic_slice_in_dim(shrink_qkv, core * half, half, 0)
    halves = [swap_holder(half_own, holders, r) for r in range(1, holders)]
    w_kv, halves = lax.optimization_barrier((w_kv, halves))
    pieces, spots = [shrink_qkv], [chip, core, holder, holder * held]
    for r, got in enumerate(halves, 1):
        pieces += [got, other_core(got, parts)]
        begin = (holder ^ r) * held
        spots += [begin + core * half, begin + (1 - core) * half]
    head_parts = head_weights(
        w_kv, lambda c: 2 * c * kv_heads // parts, chip, holder, parts, holders
    )
    shrink_rows = shrink_o.reshape(adapters * rank, query_cols)
    gathered, w_o_late, shrink_late = lax.optimization_barrier((gathered, w_o, shrink_rows))
    w_o_other = other_core(w_o_late, parts)
    shrink_other = other_core(shrink_late, parts)

    line = jnp.arange(total, dtype=jnp.int32)
    side, number = line // (total // 2), line // own_rows % chips
    position = ((number + chip) % chips * 2 + (side ^ core)) * own_rows + line % own_rows
    length_row, group_row, adapter_row = lengths[0], groups[0], adapter_of_request[0]
    ends = jnp.cumsum(length_row)
    starts = ends - length_row
    request = jnp.sum((ends[None, :] <= position[:, None]).astype(jnp.int32), axis=1)
    same = group_row[:, None] == group_row[None, :]
    group_first = jnp.min(jnp.where(same, starts[None, :], total), axis=1)
    slot_of_request = lookup(adapter_row, adapter_slot)
    group = lookup(request, group_row)
    rope_pos = position - lookup(request, group_first)
    slot = lookup(request, slot_of_request)
    meta_col = jnp.stack([slot, group, position], axis=1)
    meta_row = jnp.stack([group, position], axis=0)
    freq = jnp.exp(
        -jnp.arange(head_length // 2, dtype=F32) * (2.0 * math.log(ROPE_BASE) / head_length)
    )
    angle = rope_pos.astype(F32)[:, None] * freq[None, :]
    cosine, sine = jnp.cos(angle), jnp.sin(angle)
    cosine = jnp.concatenate([cosine, cosine], axis=1)
    sine = jnp.concatenate([-sine, sine], axis=1)
    colslot = (jnp.arange(adapters * ranks, dtype=jnp.int32) // ranks)[None, :]
    oslot = (jnp.arange(adapters * rank, dtype=jnp.int32) // rank)[None, :]

    up_kv = lax.dynamic_index_in_dim(
        key_value_up_factors.reshape(adapters, rank, kv_heads, 2, head_length), head, 2, keepdims=False
    )
    up = jnp.concatenate(
        [
            jnp.pad(query_up_factors, ((0, 0), (0, 2 * rank), (0, 0))),
            jnp.pad(up_kv[:, :, 0], ((0, 0), (rank, rank), (0, 0))),
            jnp.pad(up_kv[:, :, 1], ((0, 0), (2 * rank, 0), (0, 0))),
        ],
        axis=2,
    ).reshape(adapters * ranks, query_cols + 2 * head_length)

    weights = (
        attn_gain.reshape(1, -1),
        query_weight,
        up,
        q_gain.reshape(1, -1),
        k_gain.reshape(1, -1),
    )
    meta = (meta_col, meta_row, colslot, cosine, sine)
    mixed, mixed_part, entries = attention(
        jnp.stack(spots).astype(jnp.int32),
        gathered,
        weights,
        meta,
        pieces,
        head_parts,
        adapters,
        holders,
    )

    out_weights = (
        w_o,
        w_o_other,
        shrink_rows,
        shrink_other,
        expand_o.reshape(adapters * rank, width),
    )
    sums = output_terms(
        mixed, other_core(mixed_part, parts), out_weights, slot[: total // 2, None], oslot, chips
    )
    arrived = [sums[0]] + [turn_chips(sums[r], parts, r) for r in range(1, chips)]
    attn_own, moe_own = residual_norm(tokens, moe_gain, arrived)

    local_cols = kv_width // parts
    kept = lax.dynamic_slice_in_dim(
        entries, place * local_cols - head * 2 * head_length, local_cols, 1
    )
    page_row = page_table[0]
    per_request = page_row.shape[0] // length_row.shape[0]
    offset = PAGE * jnp.arange(per_request, dtype=jnp.int32)[None, :]
    page_first = (starts[:, None] + offset).reshape(-1)
    page_length = jnp.clip(length_row[:, None] - offset, 0, PAGE).reshape(-1)
    kv_pages = fill_pages(page_first, page_length, page_row, to_group(kept, chip, core, chips))

    experts = w_gate.shape[0]
    capacity = CAP_DEV * parts
    ids = from_here(expert_ids, chip, core, chips)
    gates = from_here(expert_gates, chip, core, chips)
    share = gates / jnp.sum(gates, axis=1, keepdims=True)
    own_experts = place * experts + jnp.arange(experts, dtype=jnp.int32)
    chosen = ids[:, :, None] == own_experts[None, None, :]
    hit = jnp.any(chosen, axis=1)
    weight = jnp.sum(jnp.where(chosen, share[:, :, None], 0.0), axis=1)
    before = dot((line[:, None] > line[None, :]).astype(BF16), hit.astype(BF16)).astype(jnp.int32)
    slot_in = jnp.where(hit, before, -1)

    moe_own, gate_late = lax.optimization_barrier((moe_own, w_gate))
    moe_in = lax.all_gather(moe_own, "tensor", axis=0, tiled=True)
    own_terms, part_terms = expert_layer(
        jnp.stack([chip, core]).astype(jnp.int32),
        slot_in,
        slot_in.T,
        weight,
        moe_in,
        hold(gate_late),
        w_up,
        w_down,
        capacity,
        parts,
    )
    sums = pair_sum(own_terms, other_core(part_terms, parts), chips)
    arrived = [sums[0]] + [turn_chips(sums[r], parts, r) for r in range(1, chips)]
    moe_total = sum(part.astype(F32) for part in arrived).astype(BF16)
    return (attn_own, moe_total, kv_pages)


def solution(mesh):
    placed = (
        P(("dp", "tensor"), None),
        P(),
        P(),
        P(),
        P(),
        P(None, "tensor"),
        P("tensor", None, None),
        P("tensor", None),
        P("tensor", None, None),
        P("tensor", None, None),
        P("tensor", None, None),
        P("dp", None, None),
        P(None, None, "tensor"),
        P(None, None, "tensor"),
        P(),
        P(),
        P("dp", None),
        P("dp", None),
        P("dp", None),
        P(),
        P("dp", None),
        P("dp", None),
        P("dp", None),
    )
    return jax.shard_map(
        local,
        mesh=mesh,
        in_specs=placed,
        out_specs=(P(("dp", "tensor"), None), P(("dp", "tensor"), None), P("dp", "tensor", None)),
        check_vma=False,
    )
```

```python
import functools
import math

import jax
import jax.numpy as jnp
from jax import lax
from jax.experimental import pallas as pl
from jax.experimental.pallas import tpu as pltpu
from jax.sharding import PartitionSpec as P

PAGE = 128
CAP_DEV = 16
NORM_EPS = 1e-06
ROPE_BASE = 1000000.0
ADAPTER_FACTOR = 0.5
MIB = 1 << 20
BF16 = jnp.bfloat16
F32 = jnp.float32
VMEM = pl.BlockSpec(memory_space=pltpu.VMEM)
SMEM = pl.BlockSpec(memory_space=pltpu.SMEM)
ANY = pl.BlockSpec(memory_space=pl.ANY)
HBM = pl.BlockSpec(memory_space=pltpu.HBM)


def dot(a, b):
    return jnp.dot(a, b, preferred_element_type=F32)


def dot_nt(a, b):
    return lax.dot_general(a, b, (((1,), (1,)), ((), ())), preferred_element_type=F32)


def lookup(index_value, table):
    match = index_value[:, None] == jnp.arange(table.shape[0], dtype=jnp.int32)[None, :]
    return jnp.sum(jnp.where(match, table[None, :], 0), axis=1)


def loop(count, body, carry):
    if count <= 2:
        for i in range(count):
            carry = body(i, carry)
        return carry
    return lax.fori_loop(0, count, body, carry)


def rms(v, gain):
    return v * lax.rsqrt(jnp.mean(v * v, axis=-1, keepdims=True) + NORM_EPS) * gain


def residual_kernel(x_ref, gain_ref, *refs):
    parts, (attn_ref, left_ref, right_ref) = refs[:-3], refs[-3:]
    total = parts[0][...].astype(F32)
    for part in parts[1:]:
        total = total + part[...].astype(F32)
    attn_ref[...] = total.astype(BF16)
    out = rms(x_ref[...].astype(F32) + total, gain_ref[...].astype(F32)).astype(BF16)
    left_ref[...] = out[:, : left_ref.shape[1]]
    right_ref[...] = out[:, left_ref.shape[1] :]


def residual_norm(x, gain, parts):
    rows, width = x.shape
    half = jax.ShapeDtypeStruct((rows, width // 2), BF16)
    return pl.pallas_call(
        residual_kernel,
        out_shape=(jax.ShapeDtypeStruct(x.shape, BF16), half, half),
        in_specs=[VMEM] * (2 + len(parts)),
        out_specs=(VMEM, VMEM, VMEM),
        name="residual_norm",
    )(x, gain.reshape(1, -1), *parts)


def pair_kernel(a_ref, b_ref, *outs):
    rows = outs[0].shape[0]
    for i, out in enumerate(outs):
        here = slice(i * rows, (i + 1) * rows)
        out[...] = (a_ref[here, :].astype(F32) + b_ref[here, :].astype(F32)).astype(BF16)


def pair_sum(a, b, count):
    shape = jax.ShapeDtypeStruct((a.shape[0] // count, a.shape[1]), BF16)
    return pl.pallas_call(
        pair_kernel,
        out_shape=(shape,) * count,
        in_specs=[VMEM, VMEM],
        out_specs=(VMEM,) * count,
        compiler_params=pltpu.CompilerParams(vmem_limit_bytes=24 * MIB),
        name="pair_sum",
    )(a, b)


def attention_kernel(
    factor_blocks,
    head_blocks,
    spot_ref,
    gain_ref,
    meta_ref,
    row_ref,
    colslot_ref,
    cos_ref,
    sin_ref,
    qg_ref,
    kg_ref,
    *refs,
):
    (wq_source, up_source, tokens_ref), refs = refs[:3], refs[3:]
    pieces, refs = refs[:factor_blocks], refs[factor_blocks:]
    parts, refs = refs[:head_blocks], refs[head_blocks:]
    own_ref, part_ref, kv_ref = refs[:3]
    wq_ref, up_ref, x_ref, s_ref, w_ref, qf_ref, kvf_ref, q_ref = refs[3:11]
    x_sems, s_sems, w_sems = refs[11:]
    rows, width = x_ref.shape
    query_cols = wq_ref.shape[1]
    head = qg_ref.shape[1]
    heads = query_cols // head
    block = min(256, rows // 2)
    blocks = rows // block
    scale = head**-0.5
    devices, holders, cols, piece_width = w_ref.shape
    chips = devices // 2
    own_rows = rows // devices
    chip, core, holder = spot_ref[0], spot_ref[1], spot_ref[2]
    token_copies, factor_copies, head_copies = [], [], []
    for q in range(2):
        for j in range(chips):
            i = q * chips + j
            device = lax.rem(chip + j, chips) * 2 + (core ^ q)
            source = tokens_ref.at[pl.ds(pl.multiple_of(device * own_rows, own_rows), own_rows)]
            target = x_ref.at[pl.ds(i * own_rows, own_rows)]
            token_copies.append(pltpu.make_async_copy(source, target, x_sems.at[i]))
            token_copies[-1].start()
    for q in range(2):
        for r in range(holders):
            for j in range(chips):
                device = lax.rem(chip + j, chips) * 2 + (core ^ q)
                target = w_ref.at[device, holder ^ r]
                head_copies.append(
                    pltpu.make_async_copy(
                        parts[q * holders + r].at[j],
                        target,
                        w_sems.at[(q * holders + r) * chips + j],
                    )
                )
                head_copies[-1].start()
    token_copies.append(pltpu.make_async_copy(wq_source, wq_ref, x_sems.at[devices]))
    token_copies[-1].start()
    factor_copies.append(pltpu.make_async_copy(up_source, up_ref, x_sems.at[devices + 1]))
    factor_copies[-1].start()
    for i, piece in enumerate(pieces):
        target = s_ref.at[pl.ds(spot_ref[3 + i], piece.shape[0])]
        factor_copies.append(pltpu.make_async_copy(piece, target, s_sems.at[i]))
        factor_copies[-1].start()
    factors = s_ref.shape[0] * s_ref.shape[1]
    gain = gain_ref[...].astype(F32)
    qg = qg_ref[...].astype(F32)
    kg = kg_ref[...].astype(F32)

    for copy in token_copies + head_copies:
        copy.wait()

    def project(i, carry):
        here = pl.ds(pl.multiple_of(i * block, block), block)
        x = rms(x_ref[here, :].astype(F32), gain).astype(BF16)
        x_ref[here, :] = x
        qf_ref[here, :] = dot(x, wq_ref[...])
        kv = 0.0
        for r in range(holders):
            w = w_ref[:, r].reshape(devices * cols, piece_width)
            kv = kv + dot_nt(x[:, r * piece_width : (r + 1) * piece_width], w)
        kvf_ref[here, :] = kv
        return carry

    loop(blocks, project, 0)

    for copy in factor_copies:
        copy.wait()

    def turned(v, gain, here):
        v = rms(v, gain)
        return v * cos_ref[here, :] + pltpu.roll(v, head // 2, 1) * sin_ref[here, :]

    def adapt(i, carry):
        here = pl.ds(pl.multiple_of(i * block, block), block)
        low = dot_nt(x_ref[here, :], s_ref[...].reshape(factors, width))
        low = jnp.where(meta_ref[here, 0:1] == colslot_ref[...], low, 0.0).astype(BF16)
        delta = ADAPTER_FACTOR * dot(low, up_ref[...])
        q = qf_ref[here, :] + delta[:, :query_cols]
        kv = (kvf_ref[here, :] + delta[:, query_cols:]).astype(BF16)
        for h in range(heads):
            cut = slice(h * head, (h + 1) * head)
            q_ref[here, cut] = turned(q[:, cut], qg, here).astype(BF16)
        kv_ref[here, :head] = turned(kv[:, :head].astype(F32), kg, here).astype(BF16)
        kv_ref[here, head:] = kv[:, head:]
        return carry

    loop(blocks, adapt, 0)

    def attend(target, offset):
        def one(i, carry):
            there = pl.ds(pl.multiple_of(i * block, block), block)
            here = pl.ds(pl.multiple_of(offset + i * block, block), block)
            allowed = (row_ref[1:2, :] <= meta_ref[here, 2:3]) & (
                row_ref[0:1, :] == meta_ref[here, 1:2]
            )
            for h in range(heads):
                cut = slice(h * head, (h + 1) * head)
                s = dot_nt(q_ref[here, cut], kv_ref[:, :head]) * scale
                raised = jnp.where(allowed, jnp.exp(s), 0.0)
                mixed = dot(raised.astype(BF16), kv_ref[:, head:])
                mixed = mixed / jnp.sum(raised, axis=1, keepdims=True)
                target[there, cut] = mixed.astype(BF16)
            return carry

        loop(blocks // 2, one, 0)

    attend(part_ref, rows // 2)
    attend(own_ref, 0)


def attention(spots, tokens, weights, meta, pieces, parts, adapters, holders):
    gain, wq, up, qg, kg = weights
    rows, width = tokens.shape
    chips, cols, piece_width = parts[0].shape
    query_cols = wq.shape[1]
    head = qg.shape[1]
    ranks = pieces[0].shape[1]
    half = jax.ShapeDtypeStruct((rows // 2, query_cols), BF16)
    flops = 2 * rows * (width * (adapters * ranks + query_cols + 2 * head) + rows * query_cols)
    return pl.pallas_call(
        functools.partial(attention_kernel, len(pieces), len(parts)),
        out_shape=(half, half, jax.ShapeDtypeStruct((rows, 2 * head), BF16)),
        in_specs=[SMEM] + [VMEM] * 8 + [ANY] * (3 + len(pieces) + len(parts)),
        out_specs=(VMEM, VMEM, VMEM),
        scratch_shapes=[
            pltpu.VMEM(wq.shape, BF16),
            pltpu.VMEM(up.shape, BF16),
            pltpu.VMEM((rows, width), BF16),
            pltpu.VMEM((adapters, ranks, width), BF16),
            pltpu.VMEM((2 * chips, holders, cols, piece_width), BF16),
            pltpu.VMEM((rows, query_cols), F32),
            pltpu.VMEM((rows, 2 * head), F32),
            pltpu.VMEM((rows, query_cols), BF16),
            pltpu.SemaphoreType.DMA((2 * chips + 2,)),
            pltpu.SemaphoreType.DMA((len(pieces),)),
            pltpu.SemaphoreType.DMA((2 * chips * holders,)),
        ],
        compiler_params=pltpu.CompilerParams(vmem_limit_bytes=60 * MIB),
        cost_estimate=pl.CostEstimate(
            flops=flops, bytes_accessed=14 * MIB, transcendentals=rows * rows
        ),
        name="attention",
    )(spots, gain, *meta, qg, kg, wq, up, tokens, *pieces, *parts)


def output_kernel(
    own_ref, got_ref, sho_ref, sho2_ref, slot_ref, oslot_ref, wo_in, wo2_in, exo_in, *refs
):
    outs, (wo_ref, wo2_ref, exo_ref, low_ref, sems) = refs[:-5], refs[-5:]
    rows = own_ref.shape[0]
    own_rows, width = outs[0].shape
    block = min(256, rows)
    per = block // own_rows
    step = width // sems.shape[1]
    rank_rows = low_ref.shape[1] // 2
    copies = []
    for n in range(sems.shape[1]):
        cut = pl.ds(n * step, step)
        pairs = ((wo_in, wo_ref), (wo2_in, wo2_ref), (exo_in, exo_ref))
        copies.append(
            [
                pltpu.make_async_copy(source.at[:, cut], target.at[:, cut], sems.at[k, n])
                for k, (source, target) in enumerate(pairs)
            ]
        )
        for copy in copies[-1]:
            copy.start()
    for i in range(rows // block):
        here = slice(i * block, (i + 1) * block)
        low = dot_nt(own_ref[here, :], sho_ref[...]) + dot_nt(got_ref[here, :], sho2_ref[...])
        low = jnp.where(slot_ref[here, :] == oslot_ref[...], low, 0.0)
        high = low.astype(BF16)
        low_ref[here, :rank_rows] = high
        low_ref[here, rank_rows:] = (low - high.astype(F32)).astype(BF16)
    for n in range(sems.shape[1]):
        for copy in copies[n]:
            copy.wait()
        cut = slice(n * step, (n + 1) * step)
        for i in range(rows // block):
            here = slice(i * block, (i + 1) * block)
            expand = exo_ref[:, cut]
            term = dot(own_ref[here, :], wo_ref[:, cut]) + dot(got_ref[here, :], wo2_ref[:, cut])
            term = term + ADAPTER_FACTOR * (
                dot(low_ref[here, :rank_rows], expand) + dot(low_ref[here, rank_rows:], expand)
            )
            term = term.astype(BF16)
            for b in range(per):
                outs[i * per + b][:, cut] = term[b * own_rows : (b + 1) * own_rows, :]


def output_terms(own, got, weights, slot, oslot, chips):
    wo, wo2, sho, sho2, exo = weights
    rows, query_cols = own.shape
    width = wo.shape[1]
    shape = jax.ShapeDtypeStruct((rows // chips, width), BF16)
    return pl.pallas_call(
        output_kernel,
        out_shape=(shape,) * chips,
        in_specs=[VMEM] * 6 + [ANY] * 3,
        out_specs=(VMEM,) * chips,
        scratch_shapes=[
            pltpu.VMEM(wo.shape, BF16),
            pltpu.VMEM(wo2.shape, BF16),
            pltpu.VMEM(exo.shape, BF16),
            pltpu.VMEM((rows, 2 * exo.shape[0]), BF16),
            pltpu.SemaphoreType.DMA((3, 4)),
        ],
        compiler_params=pltpu.CompilerParams(vmem_limit_bytes=60 * MIB),
        cost_estimate=pl.CostEstimate(
            flops=4 * rows * query_cols * width, bytes_accessed=8 * MIB, transcendentals=0
        ),
        name="output_terms",
    )(own, got, sho, sho2, slot, oslot, wo, wo2, exo)


def pages_kernel(first_ref, length_ref, page_ref, entries_ref, out_ref):
    columns, extent = entries_ref.shape
    rows = extent - PAGE
    window = 2 * PAGE
    gap = lax.broadcasted_iota(jnp.int32, (window, PAGE), 0) - lax.broadcasted_iota(
        jnp.int32, (window, PAGE), 1
    )
    lane = lax.broadcasted_iota(jnp.int32, (columns, PAGE), 1)

    def one(n, carry):
        length = length_ref[n]
        page = page_ref[n]

        @pl.when(length > 0)
        def _():
            first = jnp.minimum(first_ref[n], rows - 1)
            base = pl.multiple_of(first // PAGE * PAGE, PAGE)
            pick = (gap == first - base).astype(F32).astype(BF16)
            moved = dot(entries_ref[:, pl.ds(base, window)], pick)
            out_ref[page] = jnp.where(lane < length, moved, 0.0).astype(BF16)

        @pl.when(length <= 0)
        def _():
            out_ref[page] = jnp.zeros((columns, PAGE), BF16)

        return carry

    lax.fori_loop(0, page_ref.shape[0], one, 0)


def fill_pages(first, length, page, entries):
    rows, columns = entries.shape
    count = page.shape[0]
    turned = jnp.pad(entries.T, ((0, 0), (0, PAGE)))
    return pl.pallas_call(
        pages_kernel,
        out_shape=jax.ShapeDtypeStruct((count, columns, PAGE), BF16),
        in_specs=[SMEM, SMEM, SMEM, VMEM],
        out_specs=VMEM,
        compiler_params=pltpu.CompilerParams(vmem_limit_bytes=32 * MIB),
        cost_estimate=pl.CostEstimate(
            flops=count * columns * PAGE * PAGE * 16, bytes_accessed=4 * MIB, transcendentals=0
        ),
        name="fill_pages",
    )(first, length, page, turned)


def experts_kernel(blocks, spot_ref, slot_ref, slot_t_ref, weight_ref, left_ref, *refs):
    pieces, refs = refs[:blocks], refs[blocks:]
    (gate_ref, up_ref, up2_ref, down_ref, own_ref, part_ref) = refs[:6]
    (x_ref, rows_ref, y_ref, gate_buf, up_buf, down_buf, x_sems, w_sems) = refs[6:]
    total, width = x_ref.shape
    chips = blocks // 2
    own_rows = total // blocks
    experts = slot_ref.shape[1]
    capacity = rows_ref.shape[0] // experts
    chip, core = spot_ref[0], spot_ref[1]
    slots = gate_buf.shape[0]
    half = left_ref.shape[1]
    first = up_ref.shape[0]

    def fetch(k, e, s):
        if k == 0:
            pltpu.make_async_copy(gate_ref.at[e], gate_buf.at[s], w_sems.at[0, s]).start()
        elif k == 2:
            pltpu.make_async_copy(down_ref.at[e], down_buf.at[s], w_sems.at[2, s]).start()
        elif isinstance(e, int):
            source = up_ref.at[e] if e < first else up2_ref.at[e - first]
            pltpu.make_async_copy(source, up_buf.at[s], w_sems.at[1, s]).start()
        else:

            @pl.when(e < first)
            def _():
                pltpu.make_async_copy(
                    up_ref.at[jnp.minimum(e, first - 1)], up_buf.at[s], w_sems.at[1, s]
                ).start()

            @pl.when(e >= first)
            def _():
                pltpu.make_async_copy(
                    up2_ref.at[jnp.maximum(e - first, 0)], up_buf.at[s], w_sems.at[1, s]
                ).start()

    def arrive(k, s):
        buffer, source = ((gate_buf, gate_ref), (up_buf, up_ref), (down_buf, down_ref))[k]
        pltpu.make_async_copy(source.at[0], buffer.at[s], w_sems.at[k, s]).wait()

    copies = []
    for q in range(2):
        for j in range(chips):
            i = q * chips + j
            rows = pl.ds(i * own_rows, own_rows)
            device = lax.rem(chip + j, chips) * 2 + (core ^ q)
            source = left_ref.at[pl.ds(pl.multiple_of(device * own_rows, own_rows), own_rows)]
            copies.append(
                pltpu.make_async_copy(source, x_ref.at[rows, pl.ds(0, half)], x_sems.at[0, i])
            )
            copies.append(
                pltpu.make_async_copy(
                    pieces[i], x_ref.at[rows, pl.ds(half, width - half)], x_sems.at[1, i]
                )
            )
    for item in copies:
        item.start()
    for e in range(min(slots, experts)):
        for k in range(3):
            fetch(k, e, e)
    for item in copies:
        item.wait()
    step = min(512, width)
    line = lax.broadcasted_iota(jnp.int32, (capacity, total), 0)
    pick = jnp.concatenate(
        [(slot_t_ref[n : n + 1, :] == line).astype(F32).astype(BF16) for n in range(experts)], axis=0
    )
    for c in range(0, width, step):
        rows_ref[:, c : c + step] = dot(pick, x_ref[:, c : c + step]).astype(BF16)

    def one(e, carry):
        s = lax.rem(e, slots)
        here = pl.ds(pl.multiple_of(e * capacity, capacity), capacity)
        x = rows_ref[here, :]
        arrive(0, s)
        gate = dot_nt(x, gate_buf[s])
        arrive(1, s)
        up = dot(x, up_buf[s])
        hidden = (gate / (1.0 + jnp.exp(-gate)) * up).astype(BF16)
        arrive(2, s)
        y_ref[here, :] = dot(hidden, down_buf[s]).astype(BF16)

        @pl.when(e + slots < experts)
        def _():
            for k in range(3):
                fetch(k, e + slots, s)

        return carry

    lax.fori_loop(0, experts, one, 0)

    tile = min(256, total // 2)
    line = lax.broadcasted_iota(jnp.int32, (tile, capacity), 1)

    def combine(target, offset):
        def mix(i, carry):
            there = pl.ds(pl.multiple_of(i * tile, tile), tile)
            here = pl.ds(pl.multiple_of(offset + i * tile, tile), tile)
            spread = jnp.concatenate(
                [
                    jnp.where(
                        slot_ref[here, n : n + 1] == line, weight_ref[here, n : n + 1], 0.0
                    ).astype(BF16)
                    for n in range(experts)
                ],
                axis=1,
            )
            for c in range(0, width, step):
                target[there, c : c + step] = dot(spread, y_ref[:, c : c + step]).astype(BF16)
            return carry

        loop(total // 2 // tile, mix, 0)

    combine(part_ref, total // 2)
    combine(own_ref, 0)


def turn_kernel(in_ref, out_ref):
    out_ref[0] = in_ref[0].T


def turned_weights(weights, begin, end):
    _, hidden, width = weights.shape
    step = min(1024, width)
    return pl.pallas_call(
        turn_kernel,
        grid=(end - begin, width // step),
        out_shape=pltpu.HBM((end - begin, width, hidden), BF16),
        in_specs=[pl.BlockSpec((1, hidden, step), lambda e, c: (begin + e, 0, c))],
        out_specs=pl.BlockSpec((1, step, hidden), lambda e, c: (e, c, 0)),
        compiler_params=pltpu.CompilerParams(vmem_limit_bytes=24 * MIB),
        cost_estimate=pl.CostEstimate(
            flops=0, bytes_accessed=4 * (end - begin) * hidden * width, transcendentals=0
        ),
        name="turned_weights",
    )(pltpu.with_memory_space_constraint(weights, pltpu.HBM))


def expert_layer(spots, slot, weight, left, pieces, gate, up, up2, down, capacity):
    experts, hidden, width = gate.shape
    total = slot.shape[0]
    slots = min(3 if total <= 512 else 2, experts)
    half = jax.ShapeDtypeStruct((total // 2, width), BF16)
    return pl.pallas_call(
        functools.partial(experts_kernel, len(pieces)),
        out_shape=(half, half),
        in_specs=[SMEM] + [VMEM] * 3 + [ANY] * (5 + len(pieces)),
        out_specs=(VMEM, VMEM),
        scratch_shapes=[
            pltpu.VMEM((total, width), BF16),
            pltpu.VMEM((experts * capacity, width), BF16),
            pltpu.VMEM((experts * capacity, width), BF16),
            pltpu.VMEM((slots, hidden, width), BF16),
            pltpu.VMEM((slots, width, hidden), BF16),
            pltpu.VMEM((slots, hidden, width), BF16),
            pltpu.SemaphoreType.DMA((2, len(pieces))),
            pltpu.SemaphoreType.DMA((3, slots)),
        ],
        compiler_params=pltpu.CompilerParams(vmem_limit_bytes=60 * MIB),
        cost_estimate=pl.CostEstimate(
            flops=6 * experts * capacity * hidden * width,
            bytes_accessed=6 * experts * hidden * width,
            transcendentals=experts * capacity * hidden,
        ),
        name="experts",
    )(spots, slot, slot.T, weight, left, *pieces, gate, up, up2, down)


def other_core(value, parts):
    return lax.ppermute(value, "tensor", [(i, i ^ 1) for i in range(parts)])


def turn_chips(value, parts, by):
    return lax.ppermute(value, "tensor", [(i, (i + 2 * by) % parts) for i in range(parts)])


def swap_holder(value, holders, by):
    return lax.ppermute(value, "dp", [(i, i ^ by) for i in range(holders)])


def gather_blocks(own, parts):
    chips = parts // 2
    mine = [own] + [turn_chips(own, parts, r) for r in range(chips - 1, 0, -1)]
    return mine + [other_core(block, parts) for block in mine]


def from_here(rows, chip, core, chips):
    split = rows.reshape((chips, 2, -1) + rows.shape[1:])
    split = jnp.where(core == 0, split, split[:, ::-1])
    split = lax.dynamic_slice_in_dim(jnp.concatenate([split, split]), chip, chips, 0)
    return jnp.swapaxes(split, 0, 1).reshape(rows.shape)


def to_group(rows, chip, core, chips):
    split = jnp.swapaxes(rows.reshape((2, chips, -1) + rows.shape[1:]), 0, 1)
    split = lax.dynamic_slice_in_dim(
        jnp.concatenate([split, split]), (chips - chip) % chips, chips, 0
    )
    return jnp.where(core == 0, split, split[:, ::-1]).reshape(rows.shape)


def head_weights(w_kv, head_of_chip, chip, holder, parts, holders):
    chips = parts // 2
    cols, _, width = w_kv.shape
    piece = width // holders

    def cut(turn):
        to = head_of_chip((chip + turn) % chips)
        return lax.dynamic_slice(w_kv, (0, to, holder * piece), (cols, 1, piece))[:, 0]

    mine = [cut(0)] + [turn_chips(cut(r), parts, r) for r in range(chips - 1, 0, -1)]
    mine = jnp.stack(mine)
    full = [mine] + [swap_holder(mine, holders, r) for r in range(1, holders)]
    return full + [other_core(piece, parts) for piece in full]


def local(
    tokens,
    attn_gain,
    moe_gain,
    q_gain,
    k_gain,
    query_weight,
    w_kv,
    w_o,
    w_gate,
    w_up,
    w_down,
    shrink_qkv,
    shrink_o,
    query_up_factors,
    key_value_up_factors,
    expand_o,
    lengths,
    groups,
    adapter_of_request,
    adapter_slot,
    page_table,
    expert_ids,
    expert_gates,
):
    parts = lax.axis_size("tensor")
    place = lax.axis_index("tensor")
    holders = lax.axis_size("dp")
    holder = lax.axis_index("dp")
    chips, chip, core = parts // 2, place // 2, place % 2
    own_rows, width = tokens.shape
    total = own_rows * parts
    head_length = q_gain.shape[0]
    adapters, rank, kv_width = key_value_up_factors.shape
    kv_heads = kv_width // (2 * head_length)
    held, ranks = shrink_qkv.shape[:2]
    head = place * kv_heads // parts
    query_cols = query_weight.shape[1]
    experts = w_gate.shape[0]

    gathered = lax.all_gather(tokens, "tensor", axis=0, tiled=True)
    half = held // 2
    half_own = lax.dynamic_slice_in_dim(shrink_qkv, core * half, half, 0)
    halves = [swap_holder(half_own, holders, r) for r in range(1, holders)]
    w_kv, halves = lax.optimization_barrier((w_kv, halves))
    pieces, spots = [shrink_qkv], [chip, core, holder, holder * held]
    for r, got in enumerate(halves, 1):
        pieces += [got, other_core(got, parts)]
        begin = (holder ^ r) * held
        spots += [begin + core * half, begin + (1 - core) * half]
    head_parts = head_weights(
        w_kv, lambda c: 2 * c * kv_heads // parts, chip, holder, parts, holders
    )
    shrink_rows = shrink_o.reshape(adapters * rank, query_cols)

    line = jnp.arange(total, dtype=jnp.int32)
    side, number = line // (total // 2), line // own_rows % chips
    position = ((number + chip) % chips * 2 + (side ^ core)) * own_rows + line % own_rows
    length_row, group_row, adapter_row = lengths[0], groups[0], adapter_of_request[0]
    ends = jnp.cumsum(length_row)
    starts = ends - length_row
    request = jnp.sum((ends[None, :] <= position[:, None]).astype(jnp.int32), axis=1)
    same = group_row[:, None] == group_row[None, :]
    group_first = jnp.min(jnp.where(same, starts[None, :], total), axis=1)
    slot_of_request = lookup(adapter_row, adapter_slot)
    group = lookup(request, group_row)
    rope_pos = position - lookup(request, group_first)
    slot = lookup(request, slot_of_request)
    w_o_late, shrink_late, slot = lax.optimization_barrier((w_o, shrink_rows, slot))
    w_o_other = other_core(w_o_late, parts)
    shrink_other = other_core(shrink_late, parts)
    meta_col = jnp.stack([slot, group, position], axis=1)
    meta_row = jnp.stack([group, position], axis=0)
    freq = jnp.exp(
        -jnp.arange(head_length // 2, dtype=F32) * (2.0 * math.log(ROPE_BASE) / head_length)
    )
    angle = rope_pos.astype(F32)[:, None] * freq[None, :]
    cosine, sine = jnp.cos(angle), jnp.sin(angle)
    cosine = jnp.concatenate([cosine, cosine], axis=1)
    sine = jnp.concatenate([-sine, sine], axis=1)
    colslot = (jnp.arange(adapters * ranks, dtype=jnp.int32) // ranks)[None, :]
    oslot = (jnp.arange(adapters * rank, dtype=jnp.int32) // rank)[None, :]

    up_kv = lax.dynamic_index_in_dim(
        key_value_up_factors.reshape(adapters, rank, kv_heads, 2, head_length), head, 2, keepdims=False
    )
    up = jnp.concatenate(
        [
            jnp.pad(query_up_factors, ((0, 0), (0, 2 * rank), (0, 0))),
            jnp.pad(up_kv[:, :, 0], ((0, 0), (rank, rank), (0, 0))),
            jnp.pad(up_kv[:, :, 1], ((0, 0), (2 * rank, 0), (0, 0))),
        ],
        axis=2,
    ).reshape(adapters * ranks, query_cols + 2 * head_length)

    weights = (
        attn_gain.reshape(1, -1),
        query_weight,
        up,
        q_gain.reshape(1, -1),
        k_gain.reshape(1, -1),
    )
    meta = (meta_col, meta_row, colslot, cosine, sine)
    mixed, mixed_part, entries = attention(
        jnp.stack(spots).astype(jnp.int32),
        gathered,
        weights,
        meta,
        pieces,
        head_parts,
        adapters,
        holders,
    )

    out_weights = (
        w_o,
        w_o_other,
        shrink_rows,
        shrink_other,
        expand_o.reshape(adapters * rank, width),
    )
    sums = output_terms(
        mixed, other_core(mixed_part, parts), out_weights, slot[: total // 2, None], oslot, chips
    )
    arrived = [sums[0]] + [turn_chips(sums[r], parts, r) for r in range(1, chips)]
    w_up, sums = lax.optimization_barrier((w_up, sums))
    up_first = turned_weights(w_up, 0, experts // 2)
    arrived[0], up_first = lax.optimization_barrier((arrived[0], up_first))
    attn_own, moe_left, moe_right = residual_norm(tokens, moe_gain, arrived)

    local_cols = kv_width // parts
    kept = lax.dynamic_slice_in_dim(
        entries, place * local_cols - head * 2 * head_length, local_cols, 1
    )
    page_row = page_table[0]
    per_request = page_row.shape[0] // length_row.shape[0]
    offset = PAGE * jnp.arange(per_request, dtype=jnp.int32)[None, :]
    page_first = (starts[:, None] + offset).reshape(-1)
    page_length = jnp.clip(length_row[:, None] - offset, 0, PAGE).reshape(-1)
    kv_pages = fill_pages(page_first, page_length, page_row, to_group(kept, chip, core, chips))

    capacity = CAP_DEV * parts
    ids = from_here(expert_ids, chip, core, chips)
    gates = from_here(expert_gates, chip, core, chips)
    share = gates / jnp.sum(gates, axis=1, keepdims=True)
    own_experts = place * experts + jnp.arange(experts, dtype=jnp.int32)
    chosen = ids[:, :, None] == own_experts[None, None, :]
    hit = jnp.any(chosen, axis=1)
    weight = jnp.sum(jnp.where(chosen, share[:, :, None], 0.0), axis=1)
    before = dot((line[:, None] > line[None, :]).astype(BF16), hit.astype(BF16)).astype(jnp.int32)
    slot_in = jnp.where(hit, before, -1)

    w_up, moe_right = lax.optimization_barrier((w_up, moe_right))
    own_terms, part_terms = expert_layer(
        jnp.stack([chip, core]).astype(jnp.int32),
        slot_in,
        weight,
        lax.all_gather(moe_left, "tensor", axis=0, tiled=True),
        gather_blocks(moe_right, parts),
        w_gate,
        up_first,
        turned_weights(w_up, experts // 2, experts),
        w_down,
        capacity,
    )
    sums = pair_sum(own_terms, other_core(part_terms, parts), chips)
    arrived = [sums[0]] + [turn_chips(sums[r], parts, r) for r in range(1, chips)]
    moe_total = sum(part.astype(F32) for part in arrived).astype(BF16)
    return (attn_own, moe_total, kv_pages)


def solution(mesh):
    placed = (
        P(("dp", "tensor"), None),
        P(),
        P(),
        P(),
        P(),
        P(None, "tensor"),
        P("tensor", None, None),
        P("tensor", None),
        P("tensor", None, None),
        P("tensor", None, None),
        P("tensor", None, None),
        P("dp", None, None),
        P(None, None, "tensor"),
        P(None, None, "tensor"),
        P(),
        P(),
        P("dp", None),
        P("dp", None),
        P("dp", None),
        P(),
        P("dp", None),
        P("dp", None),
        P("dp", None),
    )
    return jax.shard_map(
        local,
        mesh=mesh,
        in_specs=placed,
        out_specs=(P(("dp", "tensor"), None), P(("dp", "tensor"), None), P("dp", "tensor", None)),
        check_vma=False,
    )
```

```python
import functools
import math

import jax
import jax.numpy as jnp
from jax import lax
from jax.experimental import pallas as pl
from jax.experimental.pallas import tpu as pltpu
from jax.sharding import PartitionSpec as P

PAGE = 128
CAP_DEV = 16
NORM_EPS = 1e-06
ROPE_BASE = 1000000.0
ADAPTER_FACTOR = 0.5
MIB = 1 << 20
BF16 = jnp.bfloat16
F32 = jnp.float32
VMEM = pl.BlockSpec(memory_space=pltpu.VMEM)
SMEM = pl.BlockSpec(memory_space=pltpu.SMEM)
ANY = pl.BlockSpec(memory_space=pl.ANY)
HBM = pl.BlockSpec(memory_space=pltpu.HBM)


def dot(a, b):
    return jnp.dot(a, b, preferred_element_type=F32)


def dot_nt(a, b):
    return lax.dot_general(a, b, (((1,), (1,)), ((), ())), preferred_element_type=F32)


def lookup(index_value, table):
    match = index_value[:, None] == jnp.arange(table.shape[0], dtype=jnp.int32)[None, :]
    return jnp.sum(jnp.where(match, table[None, :], 0), axis=1)


def loop(count, body, carry):
    if count <= 2:
        for i in range(count):
            carry = body(i, carry)
        return carry
    return lax.fori_loop(0, count, body, carry)


def rms(v, gain):
    return v * lax.rsqrt(jnp.mean(v * v, axis=-1, keepdims=True) + NORM_EPS) * gain


def residual_kernel(x_ref, gain_ref, *refs):
    parts, (attn_ref, left_ref, right_ref) = refs[:-3], refs[-3:]
    total = parts[0][...].astype(F32)
    for part in parts[1:]:
        total = total + part[...].astype(F32)
    attn_ref[...] = total.astype(BF16)
    out = rms(x_ref[...].astype(F32) + total, gain_ref[...].astype(F32)).astype(BF16)
    left_ref[...] = out[:, : left_ref.shape[1]]
    right_ref[...] = out[:, left_ref.shape[1] :]


def residual_norm(x, gain, parts):
    rows, width = x.shape
    half = jax.ShapeDtypeStruct((rows, width // 2), BF16)
    return pl.pallas_call(
        residual_kernel,
        out_shape=(jax.ShapeDtypeStruct(x.shape, BF16), half, half),
        in_specs=[VMEM] * (2 + len(parts)),
        out_specs=(VMEM, VMEM, VMEM),
        name="residual_norm",
    )(x, gain.reshape(1, -1), *parts)


def pair_kernel(a_ref, b_ref, *outs):
    rows = outs[0].shape[0]
    for i, out in enumerate(outs):
        here = slice(i * rows, (i + 1) * rows)
        out[...] = (a_ref[here, :].astype(F32) + b_ref[here, :].astype(F32)).astype(BF16)


def pair_sum(a, b, count):
    shape = jax.ShapeDtypeStruct((a.shape[0] // count, a.shape[1]), BF16)
    return pl.pallas_call(
        pair_kernel,
        out_shape=(shape,) * count,
        in_specs=[VMEM, VMEM],
        out_specs=(VMEM,) * count,
        compiler_params=pltpu.CompilerParams(vmem_limit_bytes=24 * MIB),
        name="pair_sum",
    )(a, b)


def attention_kernel(
    factor_blocks,
    head_blocks,
    spot_ref,
    gain_ref,
    meta_ref,
    row_ref,
    colslot_ref,
    cos_ref,
    sin_ref,
    qg_ref,
    kg_ref,
    *refs,
):
    (wq_source, up_source, tokens_ref), refs = refs[:3], refs[3:]
    pieces, refs = refs[:factor_blocks], refs[factor_blocks:]
    parts, refs = refs[:head_blocks], refs[head_blocks:]
    own_ref, part_ref, kv_ref = refs[:3]
    wq_ref, up_ref, x_ref, s_ref, w_ref, qf_ref, kvf_ref, q_ref = refs[3:11]
    x_sems, s_sems, w_sems = refs[11:]
    rows, width = x_ref.shape
    query_cols = wq_ref.shape[1]
    head = qg_ref.shape[1]
    heads = query_cols // head
    block = min(256, rows // 2)
    blocks = rows // block
    scale = head**-0.5
    devices, holders, cols, piece_width = w_ref.shape
    chips = devices // 2
    own_rows = rows // devices
    chip, core = spot_ref[0], spot_ref[1]
    token_copies, factor_copies, head_copies = [], [], []
    for q in range(2):
        for j in range(chips):
            i = q * chips + j
            device = lax.rem(chip + j, chips) * 2 + (core ^ q)
            source = tokens_ref.at[pl.ds(pl.multiple_of(device * own_rows, own_rows), own_rows)]
            target = x_ref.at[pl.ds(i * own_rows, own_rows)]
            token_copies.append(pltpu.make_async_copy(source, target, x_sems.at[i]))
            token_copies[-1].start()
    for q in range(2):
        for r in range(holders):
            for j in range(chips):
                device = lax.rem(chip + j, chips) * 2 + (core ^ q)
                target = w_ref.at[device, r]
                head_copies.append(
                    pltpu.make_async_copy(
                        parts[q * holders + r].at[j],
                        target,
                        w_sems.at[(q * holders + r) * chips + j],
                    )
                )
                head_copies[-1].start()
    token_copies.append(pltpu.make_async_copy(wq_source, wq_ref, x_sems.at[devices]))
    token_copies[-1].start()
    factor_copies.append(pltpu.make_async_copy(up_source, up_ref, x_sems.at[devices + 1]))
    factor_copies[-1].start()
    for i, piece in enumerate(pieces):
        target = s_ref.at[pl.ds(spot_ref[2 + i], piece.shape[0])]
        factor_copies.append(pltpu.make_async_copy(piece, target, s_sems.at[i]))
        factor_copies[-1].start()
    factors = s_ref.shape[0] * s_ref.shape[1]
    gain = gain_ref[...].astype(F32)
    qg = qg_ref[...].astype(F32)
    kg = kg_ref[...].astype(F32)

    for copy in token_copies + head_copies:
        copy.wait()

    def project(i, carry):
        here = pl.ds(pl.multiple_of(i * block, block), block)
        x = rms(x_ref[here, :].astype(F32), gain).astype(BF16)
        x_ref[here, :] = x
        qf_ref[here, :] = dot(x, wq_ref[...])
        kv = 0.0
        for r in range(holders):
            w = w_ref[:, r].reshape(devices * cols, piece_width)
            kv = kv + dot_nt(x[:, r * piece_width : (r + 1) * piece_width], w)
        kvf_ref[here, :] = kv
        return carry

    loop(blocks, project, 0)

    for copy in factor_copies:
        copy.wait()

    def turned(v, gain, here):
        v = rms(v, gain)
        return v * cos_ref[here, :] + pltpu.roll(v, head // 2, 1) * sin_ref[here, :]

    def adapt(i, carry):
        here = pl.ds(pl.multiple_of(i * block, block), block)
        low = dot_nt(x_ref[here, :], s_ref[...].reshape(factors, width))
        low = jnp.where(meta_ref[here, 0:1] == colslot_ref[...], low, 0.0).astype(BF16)
        delta = ADAPTER_FACTOR * dot(low, up_ref[...])
        q = qf_ref[here, :] + delta[:, :query_cols]
        kv = (kvf_ref[here, :] + delta[:, query_cols:]).astype(BF16)
        for h in range(heads):
            cut = slice(h * head, (h + 1) * head)
            q_ref[here, cut] = turned(q[:, cut], qg, here).astype(BF16)
        kv_ref[here, :head] = turned(kv[:, :head].astype(F32), kg, here).astype(BF16)
        kv_ref[here, head:] = kv[:, head:]
        return carry

    loop(blocks, adapt, 0)

    def attend(target, offset):
        def one(i, carry):
            there = pl.ds(pl.multiple_of(i * block, block), block)
            here = pl.ds(pl.multiple_of(offset + i * block, block), block)
            allowed = (row_ref[1:2, :] <= meta_ref[here, 2:3]) & (
                row_ref[0:1, :] == meta_ref[here, 1:2]
            )
            for h in range(heads):
                cut = slice(h * head, (h + 1) * head)
                s = dot_nt(q_ref[here, cut], kv_ref[:, :head]) * scale
                raised = jnp.where(allowed, jnp.exp(s), 0.0)
                mixed = dot(raised.astype(BF16), kv_ref[:, head:])
                mixed = mixed / jnp.sum(raised, axis=1, keepdims=True)
                target[there, cut] = mixed.astype(BF16)
            return carry

        loop(blocks // 2, one, 0)

    attend(part_ref, rows // 2)
    attend(own_ref, 0)


def attention(spots, tokens, weights, meta, pieces, parts, adapters, holders):
    gain, wq, up, qg, kg = weights
    rows, width = tokens.shape
    chips, cols, piece_width = parts[0].shape
    query_cols = wq.shape[1]
    head = qg.shape[1]
    ranks = pieces[0].shape[1]
    half = jax.ShapeDtypeStruct((rows // 2, query_cols), BF16)
    flops = 2 * rows * (width * (adapters * ranks + query_cols + 2 * head) + rows * query_cols)
    return pl.pallas_call(
        functools.partial(attention_kernel, len(pieces), len(parts)),
        out_shape=(half, half, jax.ShapeDtypeStruct((rows, 2 * head), BF16)),
        in_specs=[SMEM] + [VMEM] * 8 + [ANY] * (3 + len(pieces) + len(parts)),
        out_specs=(VMEM, VMEM, VMEM),
        scratch_shapes=[
            pltpu.VMEM(wq.shape, BF16),
            pltpu.VMEM(up.shape, BF16),
            pltpu.VMEM((rows, width), BF16),
            pltpu.VMEM((adapters, ranks, width), BF16),
            pltpu.VMEM((2 * chips, holders, cols, piece_width), BF16),
            pltpu.VMEM((rows, query_cols), F32),
            pltpu.VMEM((rows, 2 * head), F32),
            pltpu.VMEM((rows, query_cols), BF16),
            pltpu.SemaphoreType.DMA((2 * chips + 2,)),
            pltpu.SemaphoreType.DMA((len(pieces),)),
            pltpu.SemaphoreType.DMA((2 * chips * holders,)),
        ],
        compiler_params=pltpu.CompilerParams(vmem_limit_bytes=60 * MIB),
        cost_estimate=pl.CostEstimate(
            flops=flops, bytes_accessed=14 * MIB, transcendentals=rows * rows
        ),
        name="attention",
    )(spots, gain, *meta, qg, kg, wq, up, tokens, *pieces, *parts)


def output_kernel(
    own_ref, got_ref, sho_ref, sho2_ref, slot_ref, oslot_ref, wo_in, wo2_in, exo_in, *refs
):
    outs, (wo_ref, wo2_ref, exo_ref, low_ref, sems) = refs[:-5], refs[-5:]
    rows = own_ref.shape[0]
    own_rows, width = outs[0].shape
    block = min(256, rows)
    per = block // own_rows
    step = width // sems.shape[1]
    rank_rows = low_ref.shape[1] // 2
    copies = []
    for n in range(sems.shape[1]):
        cut = pl.ds(n * step, step)
        pairs = ((wo_in, wo_ref), (wo2_in, wo2_ref), (exo_in, exo_ref))
        copies.append(
            [
                pltpu.make_async_copy(source.at[:, cut], target.at[:, cut], sems.at[k, n])
                for k, (source, target) in enumerate(pairs)
            ]
        )
        for copy in copies[-1]:
            copy.start()
    for i in range(rows // block):
        here = slice(i * block, (i + 1) * block)
        low = dot_nt(own_ref[here, :], sho_ref[...]) + dot_nt(got_ref[here, :], sho2_ref[...])
        low = jnp.where(slot_ref[here, :] == oslot_ref[...], low, 0.0)
        high = low.astype(BF16)
        low_ref[here, :rank_rows] = high
        low_ref[here, rank_rows:] = (low - high.astype(F32)).astype(BF16)
    for n in range(sems.shape[1]):
        for copy in copies[n]:
            copy.wait()
        cut = slice(n * step, (n + 1) * step)
        for i in range(rows // block):
            here = slice(i * block, (i + 1) * block)
            expand = exo_ref[:, cut]
            term = dot(own_ref[here, :], wo_ref[:, cut]) + dot(got_ref[here, :], wo2_ref[:, cut])
            term = term + ADAPTER_FACTOR * (
                dot(low_ref[here, :rank_rows], expand) + dot(low_ref[here, rank_rows:], expand)
            )
            term = term.astype(BF16)
            for b in range(per):
                outs[i * per + b][:, cut] = term[b * own_rows : (b + 1) * own_rows, :]


def output_terms(own, got, weights, slot, oslot, chips):
    wo, wo2, sho, sho2, exo = weights
    rows, query_cols = own.shape
    width = wo.shape[1]
    shape = jax.ShapeDtypeStruct((rows // chips, width), BF16)
    return pl.pallas_call(
        output_kernel,
        out_shape=(shape,) * chips,
        in_specs=[VMEM] * 6 + [ANY] * 3,
        out_specs=(VMEM,) * chips,
        scratch_shapes=[
            pltpu.VMEM(wo.shape, BF16),
            pltpu.VMEM(wo2.shape, BF16),
            pltpu.VMEM(exo.shape, BF16),
            pltpu.VMEM((rows, 2 * exo.shape[0]), BF16),
            pltpu.SemaphoreType.DMA((3, 4)),
        ],
        compiler_params=pltpu.CompilerParams(vmem_limit_bytes=60 * MIB),
        cost_estimate=pl.CostEstimate(
            flops=4 * rows * query_cols * width, bytes_accessed=8 * MIB, transcendentals=0
        ),
        name="output_terms",
    )(own, got, sho, sho2, slot, oslot, wo, wo2, exo)


def pages_kernel(first_ref, length_ref, page_ref, entries_ref, out_ref):
    columns, extent = entries_ref.shape
    rows = extent - PAGE
    window = 2 * PAGE
    gap = lax.broadcasted_iota(jnp.int32, (window, PAGE), 0) - lax.broadcasted_iota(
        jnp.int32, (window, PAGE), 1
    )
    lane = lax.broadcasted_iota(jnp.int32, (columns, PAGE), 1)

    def one(n, carry):
        length = length_ref[n]
        page = page_ref[n]

        @pl.when(length > 0)
        def _():
            first = jnp.minimum(first_ref[n], rows - 1)
            base = pl.multiple_of(first // PAGE * PAGE, PAGE)
            pick = (gap == first - base).astype(F32).astype(BF16)
            moved = dot(entries_ref[:, pl.ds(base, window)], pick)
            out_ref[page] = jnp.where(lane < length, moved, 0.0).astype(BF16)

        @pl.when(length <= 0)
        def _():
            out_ref[page] = jnp.zeros((columns, PAGE), BF16)

        return carry

    lax.fori_loop(0, page_ref.shape[0], one, 0)


def fill_pages(first, length, page, entries):
    rows, columns = entries.shape
    count = page.shape[0]
    turned = jnp.pad(entries.T, ((0, 0), (0, PAGE)))
    return pl.pallas_call(
        pages_kernel,
        out_shape=jax.ShapeDtypeStruct((count, columns, PAGE), BF16),
        in_specs=[SMEM, SMEM, SMEM, VMEM],
        out_specs=VMEM,
        compiler_params=pltpu.CompilerParams(vmem_limit_bytes=32 * MIB),
        cost_estimate=pl.CostEstimate(
            flops=count * columns * PAGE * PAGE * 16, bytes_accessed=4 * MIB, transcendentals=0
        ),
        name="fill_pages",
    )(first, length, page, turned)


def start_all(copies):
    for copy in copies:
        copy.start()
    return copies


def wait_all(copies):
    for copy in copies:
        copy.wait()


def token_copies(pieces, x_ref, sems):
    rows = pieces[0].shape[0]
    return [
        pltpu.make_async_copy(piece, x_ref.at[pl.ds(i * rows, rows)], sems.at[i])
        for i, piece in enumerate(pieces)
    ]


def pick_rows(slot_t_ref, x_ref, rows_ref, begin, end, capacity):
    line = lax.broadcasted_iota(jnp.int32, (capacity, x_ref.shape[0]), 0)
    pick = jnp.concatenate(
        [
            (slot_t_ref[n : n + 1, :] == line).astype(F32).astype(BF16)
            for n in range(begin, end)
        ],
        axis=0,
    )
    width = x_ref.shape[1]
    step = min(512, width)
    for c in range(0, width, step):
        rows_ref[:, c : c + step] = dot(pick, x_ref[:, c : c + step]).astype(BF16)


def combine(slot_ref, weight_ref, y_ref, target, offset, capacity):
    rows, width = target.shape
    experts = slot_ref.shape[1]
    tile = min(256, rows)
    step = min(512, width)
    line = lax.broadcasted_iota(jnp.int32, (tile, capacity), 1)

    def mix(i, carry):
        there = pl.ds(pl.multiple_of(i * tile, tile), tile)
        here = pl.ds(pl.multiple_of(offset + i * tile, tile), tile)
        spread = jnp.concatenate(
            [
                jnp.where(
                    slot_ref[here, n : n + 1] == line, weight_ref[here, n : n + 1], 0.0
                ).astype(BF16)
                for n in range(experts)
            ],
            axis=1,
        )
        for c in range(0, width, step):
            target[there, c : c + step] = dot(spread, y_ref[:, c : c + step]).astype(BF16)
        return carry

    loop(rows // tile, mix, 0)


def first_kernel(blocks, begin, end, capacity, slot_t_ref, *refs):
    pieces, refs = refs[:blocks], refs[blocks:]
    gate_ref, up_ref, out_ref, x_ref, rows_ref, gate_buf, up_buf, x_sems, w_sems = refs
    half, hidden = x_ref.shape[1], gate_buf.shape[1]
    tokens = start_all(token_copies(pieces, x_ref, x_sems))
    copies = []
    for n in range(end - begin):
        source = (gate_ref.at[begin + n, :, pl.ds(0, half)], up_ref.at[begin + n, :, pl.ds(0, half)])
        copies.append(
            start_all(
                [
                    pltpu.make_async_copy(source[0], gate_buf.at[n], w_sems.at[0, n]),
                    pltpu.make_async_copy(source[1], up_buf.at[n], w_sems.at[1, n]),
                ]
            )
        )
    wait_all(tokens)
    pick_rows(slot_t_ref, x_ref, rows_ref, begin, end, capacity)
    for n in range(end - begin):
        x = rows_ref[n * capacity : (n + 1) * capacity, :]
        copies[n][0].wait()
        out_ref[n, :, :hidden] = dot_nt(x, gate_buf[n])
        copies[n][1].wait()
        out_ref[n, :, hidden:] = dot_nt(x, up_buf[n])


def first_half(slot_t, pieces, gate, up, begin, end, capacity):
    _, hidden, width = gate.shape
    own_rows, half = pieces[0].shape
    count = end - begin
    return pl.pallas_call(
        functools.partial(first_kernel, len(pieces), begin, end, capacity),
        out_shape=jax.ShapeDtypeStruct((count, capacity, 2 * hidden), F32),
        in_specs=[VMEM] + [ANY] * (2 + len(pieces)),
        out_specs=VMEM,
        scratch_shapes=[
            pltpu.VMEM((own_rows * len(pieces), half), BF16),
            pltpu.VMEM((count * capacity, half), BF16),
            pltpu.VMEM((count, hidden, half), BF16),
            pltpu.VMEM((count, hidden, half), BF16),
            pltpu.SemaphoreType.DMA((len(pieces),)),
            pltpu.SemaphoreType.DMA((2, count)),
        ],
        compiler_params=pltpu.CompilerParams(vmem_limit_bytes=56 * MIB),
        cost_estimate=pl.CostEstimate(
            flops=4 * count * capacity * hidden * half * 2,
            bytes_accessed=4 * count * hidden * half * 2,
            transcendentals=0,
        ),
        name="first_half",
    )(slot_t, *pieces, gate, up)


def second_kernel(
    blocks, sums, capacity, slot_ref, slot_t_ref, weight_ref, *refs
):
    pieces, refs = refs[:blocks], refs[blocks:]
    partial_refs, refs = refs[:sums], refs[sums:]
    gate_ref, up_ref, down_ref, own_ref, part_ref, hidden_ref = refs[:6]
    x_ref, rows_ref, y_ref, sum_ref, gate_buf, up_buf, down_buf = refs[6:13]
    x_sems, s_sems, w_sems = refs[13:]
    experts = slot_ref.shape[1]
    hidden, half = gate_buf.shape[1:]
    slots = gate_buf.shape[0]
    tokens = start_all(token_copies(pieces, x_ref, x_sems))

    def copy(k, e, s):
        source, buffer, begin = (
            (gate_ref, gate_buf, half),
            (up_ref, up_buf, half),
            (down_ref, down_buf, 0),
        )[k]
        source = source.at[e, :, pl.ds(begin, half)]
        return pltpu.make_async_copy(source, buffer.at[s], w_sems.at[k, s])

    for k in range(2):
        copy(k, 0, 0).start()
    totals, begin = [], 0
    for i, ref in enumerate(partial_refs):
        target = sum_ref.at[pl.ds(begin, ref.shape[0])]
        totals.append(pltpu.make_async_copy(ref, target, s_sems.at[i]))
        begin += ref.shape[0]
    start_all(totals)
    copy(2, 0, 0).start()
    for e in range(1, min(slots, experts)):
        for k in range(3):
            copy(k, e, e).start()
    wait_all(tokens)
    pick_rows(slot_t_ref, x_ref, rows_ref, 0, experts, capacity)
    wait_all(totals)

    def one(e, carry):
        s = lax.rem(e, slots)
        here = pl.ds(pl.multiple_of(e * capacity, capacity), capacity)
        x = rows_ref[here, :]
        copy(0, e, s).wait()
        gate = sum_ref[e, :, :hidden] + dot_nt(x, gate_buf[s])
        copy(1, e, s).wait()
        up = sum_ref[e, :, hidden:] + dot_nt(x, up_buf[s])
        inner = (gate / (1.0 + jnp.exp(-gate)) * up).astype(BF16)
        hidden_ref[here, :] = inner
        copy(2, e, s).wait()
        y_ref[here, :] = dot(inner, down_buf[s]).astype(BF16)

        @pl.when(e + slots < experts)
        def _():
            for k in range(3):
                copy(k, e + slots, s).start()

        return carry

    lax.fori_loop(0, experts, one, 0)
    combine(slot_ref, weight_ref, y_ref, part_ref, own_ref.shape[0], capacity)
    combine(slot_ref, weight_ref, y_ref, own_ref, 0, capacity)


def second_half(slot, slot_t, weight, pieces, partial_sums, gate, up, down, capacity):
    experts, hidden, width = gate.shape
    own_rows, half = pieces[0].shape
    total = own_rows * len(pieces)
    slots = min(4, experts)
    out = jax.ShapeDtypeStruct((total // 2, half), BF16)
    return pl.pallas_call(
        functools.partial(second_kernel, len(pieces), len(partial_sums), capacity),
        out_shape=(out, out, jax.ShapeDtypeStruct((experts * capacity, hidden), BF16)),
        in_specs=[VMEM] * 3 + [ANY] * (3 + len(pieces) + len(partial_sums)),
        out_specs=(VMEM, VMEM, VMEM),
        scratch_shapes=[
            pltpu.VMEM((total, half), BF16),
            pltpu.VMEM((experts * capacity, half), BF16),
            pltpu.VMEM((experts * capacity, half), BF16),
            pltpu.VMEM((experts, capacity, 2 * hidden), F32),
            pltpu.VMEM((slots, hidden, half), BF16),
            pltpu.VMEM((slots, hidden, half), BF16),
            pltpu.VMEM((slots, hidden, half), BF16),
            pltpu.SemaphoreType.DMA((len(pieces),)),
            pltpu.SemaphoreType.DMA((len(partial_sums),)),
            pltpu.SemaphoreType.DMA((3, slots)),
        ],
        compiler_params=pltpu.CompilerParams(vmem_limit_bytes=60 * MIB),
        cost_estimate=pl.CostEstimate(
            flops=6 * experts * capacity * hidden * half * 2,
            bytes_accessed=6 * experts * hidden * half * 2,
            transcendentals=experts * capacity * hidden,
        ),
        name="second_half",
    )(slot, slot_t, weight, *pieces, *partial_sums, gate, up, down)


def last_kernel(capacity, slot_ref, weight_ref, hidden_ref, down_ref, own_ref, part_ref, y_ref, buf, sems):
    experts = slot_ref.shape[1]
    half = y_ref.shape[1]
    copies = start_all(
        [
            pltpu.make_async_copy(
                down_ref.at[e, :, pl.ds(down_ref.shape[2] - half, half)], buf.at[e], sems.at[e]
            )
            for e in range(experts)
        ]
    )
    for e in range(experts):
        here = slice(e * capacity, (e + 1) * capacity)
        copies[e].wait()
        y_ref[here, :] = dot(hidden_ref[here, :], buf[e]).astype(BF16)
    combine(slot_ref, weight_ref, y_ref, part_ref, own_ref.shape[0], capacity)
    combine(slot_ref, weight_ref, y_ref, own_ref, 0, capacity)


def last_half(slot, weight, hidden_rows, down, capacity):
    experts, hidden, width = down.shape
    half = width // 2
    out = jax.ShapeDtypeStruct((slot.shape[0] // 2, half), BF16)
    return pl.pallas_call(
        functools.partial(last_kernel, capacity),
        out_shape=(out, out),
        in_specs=[VMEM] * 3 + [ANY],
        out_specs=(VMEM, VMEM),
        scratch_shapes=[
            pltpu.VMEM((experts * capacity, half), BF16),
            pltpu.VMEM((experts, hidden, half), BF16),
            pltpu.SemaphoreType.DMA((experts,)),
        ],
        compiler_params=pltpu.CompilerParams(vmem_limit_bytes=56 * MIB),
        cost_estimate=pl.CostEstimate(
            flops=2 * experts * capacity * hidden * half * 2,
            bytes_accessed=2 * experts * hidden * half * 2,
            transcendentals=0,
        ),
        name="last_half",
    )(slot, weight, hidden_rows, down)


def other_core(value, parts):
    return lax.ppermute(value, "tensor", [(i, i ^ 1) for i in range(parts)])


def turn_chips(value, parts, by):
    return lax.ppermute(value, "tensor", [(i, (i + 2 * by) % parts) for i in range(parts)])


def swap_holder(value, holders, by):
    return lax.ppermute(value, "dp", [(i, i ^ by) for i in range(holders)])


def gather_chips(own, parts):
    return [own] + [turn_chips(own, parts, r) for r in range(parts // 2 - 1, 0, -1)]


def gather_cores(mine, parts):
    return mine + [other_core(block, parts) for block in mine]


def scatter_sum(own, part, parts):
    chips = parts // 2
    sums = pair_sum(own, other_core(part, parts), chips)
    return sums, lambda sums: [sums[0]] + [turn_chips(sums[r], parts, r) for r in range(1, chips)]


def from_here(rows, chip, core, chips):
    split = rows.reshape((chips, 2, -1) + rows.shape[1:])
    split = jnp.where(core == 0, split, split[:, ::-1])
    split = lax.dynamic_slice_in_dim(jnp.concatenate([split, split]), chip, chips, 0)
    return jnp.swapaxes(split, 0, 1).reshape(rows.shape)


def to_group(rows, chip, core, chips):
    split = jnp.swapaxes(rows.reshape((2, chips, -1) + rows.shape[1:]), 0, 1)
    split = lax.dynamic_slice_in_dim(
        jnp.concatenate([split, split]), (chips - chip) % chips, chips, 0
    )
    return jnp.where(core == 0, split, split[:, ::-1]).reshape(rows.shape)


def head_weights(w_kv, head_of_chip, chip, parts):
    chips = parts // 2

    def cut(turn):
        to = head_of_chip((chip + turn) % chips)
        return lax.dynamic_index_in_dim(w_kv, to, 1, keepdims=False)

    mine = [cut(0)] + [turn_chips(cut(r), parts, r) for r in range(chips - 1, 0, -1)]
    mine = jnp.stack(mine)
    return [mine, other_core(mine, parts)]


def local(
    tokens,
    attn_gain,
    moe_gain,
    q_gain,
    k_gain,
    query_weight,
    w_kv,
    w_o,
    w_gate,
    w_up,
    w_down,
    shrink_qkv,
    shrink_o,
    query_up_factors,
    key_value_up_factors,
    expand_o,
    lengths,
    groups,
    adapter_of_request,
    adapter_slot,
    page_table,
    expert_ids,
    expert_gates,
):
    parts = lax.axis_size("tensor")
    place = lax.axis_index("tensor")
    holders = lax.axis_size("dp")
    holder = lax.axis_index("dp")
    chips, chip, core = parts // 2, place // 2, place % 2
    own_rows, width = tokens.shape
    total = own_rows * parts
    head_length = q_gain.shape[0]
    adapters, rank, kv_width = key_value_up_factors.shape
    kv_heads = kv_width // (2 * head_length)
    held, ranks = shrink_qkv.shape[:2]
    head = place * kv_heads // parts
    query_cols = query_weight.shape[1]
    experts = w_gate.shape[0]

    gathered = lax.all_gather(tokens, "tensor", axis=0, tiled=True)
    half = held // 2
    half_own = lax.dynamic_slice_in_dim(shrink_qkv, core * half, half, 0)
    halves = [swap_holder(half_own, holders, r) for r in range(1, holders)]
    pieces, spots = [shrink_qkv], [chip, core, holder * held]
    for r, got in enumerate(halves, 1):
        pieces += [got, other_core(got, parts)]
        begin = (holder ^ r) * held
        spots += [begin + core * half, begin + (1 - core) * half]
    head_parts = head_weights(w_kv, lambda c: 2 * c * kv_heads // parts, chip, parts)
    shrink_rows = shrink_o.reshape(adapters * rank, query_cols)

    line = jnp.arange(total, dtype=jnp.int32)
    side, number = line // (total // 2), line // own_rows % chips
    position = ((number + chip) % chips * 2 + (side ^ core)) * own_rows + line % own_rows
    length_row, group_row, adapter_row = lengths[0], groups[0], adapter_of_request[0]
    ends = jnp.cumsum(length_row)
    starts = ends - length_row
    request = jnp.sum((ends[None, :] <= position[:, None]).astype(jnp.int32), axis=1)
    same = group_row[:, None] == group_row[None, :]
    group_first = jnp.min(jnp.where(same, starts[None, :], total), axis=1)
    slot_of_request = lookup(adapter_row, adapter_slot)
    group = lookup(request, group_row)
    rope_pos = position - lookup(request, group_first)
    slot = lookup(request, slot_of_request)
    w_o_late, shrink_late, slot = lax.optimization_barrier((w_o, shrink_rows, slot))
    w_o_other = other_core(w_o_late, parts)
    shrink_other = other_core(shrink_late, parts)
    meta_col = jnp.stack([slot, group, position], axis=1)
    meta_row = jnp.stack([group, position], axis=0)
    freq = jnp.exp(
        -jnp.arange(head_length // 2, dtype=F32) * (2.0 * math.log(ROPE_BASE) / head_length)
    )
    angle = rope_pos.astype(F32)[:, None] * freq[None, :]
    cosine, sine = jnp.cos(angle), jnp.sin(angle)
    cosine = jnp.concatenate([cosine, cosine], axis=1)
    sine = jnp.concatenate([-sine, sine], axis=1)
    colslot = (jnp.arange(adapters * ranks, dtype=jnp.int32) // ranks)[None, :]
    oslot = (jnp.arange(adapters * rank, dtype=jnp.int32) // rank)[None, :]

    up_kv = lax.dynamic_index_in_dim(
        key_value_up_factors.reshape(adapters, rank, kv_heads, 2, head_length), head, 2, keepdims=False
    )
    up = jnp.concatenate(
        [
            jnp.pad(query_up_factors, ((0, 0), (0, 2 * rank), (0, 0))),
            jnp.pad(up_kv[:, :, 0], ((0, 0), (rank, rank), (0, 0))),
            jnp.pad(up_kv[:, :, 1], ((0, 0), (2 * rank, 0), (0, 0))),
        ],
        axis=2,
    ).reshape(adapters * ranks, query_cols + 2 * head_length)

    weights = (
        attn_gain.reshape(1, -1),
        query_weight,
        up,
        q_gain.reshape(1, -1),
        k_gain.reshape(1, -1),
    )
    meta = (meta_col, meta_row, colslot, cosine, sine)
    mixed, mixed_part, entries = attention(
        jnp.stack(spots).astype(jnp.int32),
        gathered,
        weights,
        meta,
        pieces,
        head_parts,
        adapters,
        1,
    )

    out_weights = (
        w_o,
        w_o_other,
        shrink_rows,
        shrink_other,
        expand_o.reshape(adapters * rank, width),
    )
    sums = output_terms(
        mixed, other_core(mixed_part, parts), out_weights, slot[: total // 2, None], oslot, chips
    )
    arrived = [sums[0]] + [turn_chips(sums[r], parts, r) for r in range(1, chips)]
    local_cols = kv_width // parts
    kept = lax.dynamic_slice_in_dim(
        entries, place * local_cols - head * 2 * head_length, local_cols, 1
    )
    page_row = page_table[0]
    per_request = page_row.shape[0] // length_row.shape[0]
    offset = PAGE * jnp.arange(per_request, dtype=jnp.int32)[None, :]
    page_first = (starts[:, None] + offset).reshape(-1)
    page_length = jnp.clip(length_row[:, None] - offset, 0, PAGE).reshape(-1)
    kv_pages = fill_pages(page_first, page_length, page_row, to_group(kept, chip, core, chips))

    arrived[0], kv_pages = lax.optimization_barrier((arrived[0], kv_pages))
    attn_own, moe_left, moe_right = residual_norm(tokens, moe_gain, arrived)

    capacity = CAP_DEV * parts
    ids = from_here(expert_ids, chip, core, chips)
    gates = from_here(expert_gates, chip, core, chips)
    share = gates / jnp.sum(gates, axis=1, keepdims=True)
    own_experts = place * experts + jnp.arange(experts, dtype=jnp.int32)
    chosen = ids[:, :, None] == own_experts[None, None, :]
    hit = jnp.any(chosen, axis=1)
    weight = jnp.sum(jnp.where(chosen, share[:, :, None], 0.0), axis=1)
    before = dot((line[:, None] > line[None, :]).astype(BF16), hit.astype(BF16)).astype(jnp.int32)
    slot_in = jnp.where(hit, before, -1)

    slot_t = slot_in.T
    left_chips = gather_chips(moe_left, parts)
    right_chips = gather_chips(moe_right, parts)
    left = gather_cores(left_chips, parts)
    middle = max(1, experts // 2)
    left, right_chips[1] = lax.optimization_barrier((left, right_chips[1]))
    partial_sums = [first_half(slot_t, left, w_gate, w_up, 0, middle, capacity)]
    if middle < experts:
        left, right_chips, partial_sums[0] = lax.optimization_barrier(
            (left, right_chips, partial_sums[0])
        )
        partial_sums.append(first_half(slot_t, left, w_gate, w_up, middle, experts, capacity))
    right = gather_cores(right_chips, parts)
    own, part, hidden_rows = second_half(
        slot_in, slot_t, weight, right, partial_sums, w_gate, w_up, w_down, capacity
    )
    sums, turn_left = scatter_sum(own, part, parts)
    hidden_rows, sums = lax.optimization_barrier((hidden_rows, sums))
    arrived_left = turn_left(sums)
    own, part = last_half(slot_in, weight, hidden_rows, w_down, capacity)
    part, arrived_left[1:3] = lax.optimization_barrier((part, arrived_left[1:3]))
    sums, turn_right = scatter_sum(own, part, parts)
    arrived_right = turn_right(sums)
    moe_total = jnp.concatenate(
        [sum(p.astype(F32) for p in arrived).astype(BF16) for arrived in (arrived_left, arrived_right)],
        axis=1,
    )
    return (attn_own, moe_total, kv_pages)


def solution(mesh):
    placed = (
        P(("dp", "tensor"), None),
        P(),
        P(),
        P(),
        P(),
        P(None, "tensor"),
        P("tensor", None, None),
        P("tensor", None),
        P("tensor", None, None),
        P("tensor", None, None),
        P("tensor", None, None),
        P("dp", None, None),
        P(None, None, "tensor"),
        P(None, None, "tensor"),
        P(),
        P(),
        P("dp", None),
        P("dp", None),
        P("dp", None),
        P(),
        P("dp", None),
        P("dp", None),
        P("dp", None),
    )
    return jax.shard_map(
        local,
        mesh=mesh,
        in_specs=placed,
        out_specs=(P(("dp", "tensor"), None), P(("dp", "tensor"), None), P("dp", "tensor", None)),
        check_vma=False,
    )
```

```python
import functools
import math

import jax
import jax.numpy as jnp
from jax import lax
from jax.experimental import pallas as pl
from jax.experimental.pallas import tpu as pltpu
from jax.sharding import PartitionSpec as P

PAGE = 128
CAP_DEV = 16
NORM_EPS = 1e-06
ROPE_BASE = 1000000.0
ADAPTER_FACTOR = 0.5
MIB = 1 << 20
BF16 = jnp.bfloat16
F32 = jnp.float32
VMEM = pl.BlockSpec(memory_space=pltpu.VMEM)
SMEM = pl.BlockSpec(memory_space=pltpu.SMEM)
ANY = pl.BlockSpec(memory_space=pl.ANY)
HBM = pl.BlockSpec(memory_space=pltpu.HBM)


def dot(a, b):
    return jnp.dot(a, b, preferred_element_type=F32)


def dot_nt(a, b):
    return lax.dot_general(a, b, (((1,), (1,)), ((), ())), preferred_element_type=F32)


def lookup(index_value, table):
    match = index_value[:, None] == jnp.arange(table.shape[0], dtype=jnp.int32)[None, :]
    return jnp.sum(jnp.where(match, table[None, :], 0), axis=1)


def loop(count, body, carry):
    if count <= 2:
        for i in range(count):
            carry = body(i, carry)
        return carry
    return lax.fori_loop(0, count, body, carry)


def rms(v, gain):
    return v * lax.rsqrt(jnp.mean(v * v, axis=-1, keepdims=True) + NORM_EPS) * gain


def residual_kernel(x_ref, gain_ref, *refs):
    parts, (attn_ref, out_ref) = refs[:-2], refs[-2:]
    total = parts[0][...].astype(F32)
    for part in parts[1:]:
        total = total + part[...].astype(F32)
    attn_ref[...] = total.astype(BF16)
    out_ref[...] = rms(x_ref[...].astype(F32) + total, gain_ref[...].astype(F32)).astype(BF16)


def residual_norm(x, gain, parts):
    shape = jax.ShapeDtypeStruct(x.shape, BF16)
    return pl.pallas_call(
        residual_kernel,
        out_shape=(shape, shape),
        in_specs=[VMEM] * (2 + len(parts)),
        out_specs=(VMEM, VMEM),
        name="residual_norm",
    )(x, gain.reshape(1, -1), *parts)


def pair_kernel(a_ref, b_ref, *outs):
    rows = outs[0].shape[0]
    for i, out in enumerate(outs):
        here = slice(i * rows, (i + 1) * rows)
        out[...] = (a_ref[here, :].astype(F32) + b_ref[here, :].astype(F32)).astype(BF16)


def hold_kernel(source_ref, out_ref, sem):
    copy = pltpu.make_async_copy(source_ref, out_ref, sem)
    copy.start()
    copy.wait()


def hold(rows):
    return pl.pallas_call(
        hold_kernel,
        out_shape=pltpu.VMEM(rows.shape, BF16),
        in_specs=[HBM],
        out_specs=VMEM,
        scratch_shapes=[pltpu.SemaphoreType.DMA],
        compiler_params=pltpu.CompilerParams(vmem_limit_bytes=4 * MIB),
        name="hold",
    )(pltpu.with_memory_space_constraint(rows, pltpu.HBM))


def pair_sum(a, b, count):
    shape = jax.ShapeDtypeStruct((a.shape[0] // count, a.shape[1]), BF16)
    return pl.pallas_call(
        pair_kernel,
        out_shape=(shape,) * count,
        in_specs=[VMEM, VMEM],
        out_specs=(VMEM,) * count,
        compiler_params=pltpu.CompilerParams(vmem_limit_bytes=24 * MIB),
        name="pair_sum",
    )(a, b)


def attention_kernel(
    token_blocks,
    factor_blocks,
    head_blocks,
    spot_ref,
    gain_ref,
    meta_ref,
    row_ref,
    colslot_ref,
    oslot_ref,
    cos_ref,
    sin_ref,
    qg_ref,
    kg_ref,
    sho_ref,
    *refs,
):
    (wq_source, up_source, wo_source, exo_source), refs = refs[:4], refs[4:]
    tokens, refs = refs[:token_blocks], refs[token_blocks:]
    pieces, refs = refs[:factor_blocks], refs[factor_blocks:]
    parts, refs = refs[:head_blocks], refs[head_blocks:]
    own_ref, part_ref, kv_ref = refs[:3]
    wq_ref, up_ref, wo_ref, exo_ref, x_ref, s_ref, w_ref, qf_ref, kvf_ref, q_ref = refs[3:13]
    x_sems, s_sems, w_sems = refs[13:]
    rows, width = x_ref.shape
    query_cols = wq_ref.shape[1]
    head = qg_ref.shape[1]
    heads = query_cols // head
    block = min(256, rows // 2)
    blocks = rows // block
    scale = head**-0.5
    devices, cols, _ = w_ref.shape
    chips = devices // 2
    own_rows = rows // devices
    chip, core = spot_ref[0], spot_ref[1]
    token_copies, factor_copies, head_copies = [], [], []
    for i, piece in enumerate(tokens):
        target = x_ref.at[pl.ds(i * own_rows, own_rows)]
        token_copies.append(pltpu.make_async_copy(piece, target, x_sems.at[i]))
        token_copies[-1].start()
    for q in range(2):
        for j in range(chips):
            device = (chip ^ j) * 2 + (core ^ q)
            head_copies.append(
                pltpu.make_async_copy(
                    parts[q].at[j], w_ref.at[device], w_sems.at[q * chips + j]
                )
            )
            head_copies[-1].start()
    token_copies.append(pltpu.make_async_copy(wq_source, wq_ref, x_sems.at[devices]))
    token_copies[-1].start()
    factor_copies.append(pltpu.make_async_copy(up_source, up_ref, x_sems.at[devices + 1]))
    factor_copies[-1].start()
    for i, piece in enumerate(pieces):
        target = s_ref.at[pl.ds(spot_ref[2 + i], piece.shape[0])]
        factor_copies.append(pltpu.make_async_copy(piece, target, s_sems.at[i]))
        factor_copies[-1].start()
    last_copies = [
        pltpu.make_async_copy(wo_source, wo_ref, x_sems.at[devices + 2]),
        pltpu.make_async_copy(exo_source, exo_ref, x_sems.at[devices + 3]),
    ]
    for copy in last_copies:
        copy.start()
    factors = s_ref.shape[0] * s_ref.shape[1]
    gain = gain_ref[...].astype(F32)
    qg = qg_ref[...].astype(F32)
    kg = kg_ref[...].astype(F32)

    for copy in token_copies + head_copies:
        copy.wait()

    def project(i, carry):
        here = pl.ds(pl.multiple_of(i * block, block), block)
        x = rms(x_ref[here, :].astype(F32), gain).astype(BF16)
        x_ref[here, :] = x
        qf_ref[here, :] = dot(x, wq_ref[...])
        kvf_ref[here, :] = dot_nt(x, w_ref[...].reshape(devices * cols, width))
        return carry

    loop(blocks, project, 0)

    for copy in factor_copies:
        copy.wait()

    def turned(v, gain, here):
        v = rms(v, gain)
        return v * cos_ref[here, :] + pltpu.roll(v, head // 2, 1) * sin_ref[here, :]

    def adapt(i, carry):
        here = pl.ds(pl.multiple_of(i * block, block), block)
        low = dot_nt(x_ref[here, :], s_ref[...].reshape(factors, width))
        low = jnp.where(meta_ref[here, 0:1] == colslot_ref[...], low, 0.0).astype(BF16)
        delta = ADAPTER_FACTOR * dot(low, up_ref[...])
        q = qf_ref[here, :] + delta[:, :query_cols]
        kv = (kvf_ref[here, :] + delta[:, query_cols:]).astype(BF16)
        for h in range(heads):
            cut = slice(h * head, (h + 1) * head)
            q_ref[here, cut] = turned(q[:, cut], qg, here).astype(BF16)
        kv_ref[here, :head] = turned(kv[:, :head].astype(F32), kg, here).astype(BF16)
        kv_ref[here, head:] = kv[:, head:]
        return carry

    loop(blocks, adapt, 0)

    for copy in last_copies:
        copy.wait()

    def attend(target, offset):
        def one(i, carry):
            there = pl.ds(pl.multiple_of(i * block, block), block)
            here = pl.ds(pl.multiple_of(offset + i * block, block), block)
            allowed = (row_ref[1:2, :] <= meta_ref[here, 2:3]) & (
                row_ref[0:1, :] == meta_ref[here, 1:2]
            )
            heads_mixed = []
            for h in range(heads):
                cut = slice(h * head, (h + 1) * head)
                s = dot_nt(q_ref[here, cut], kv_ref[:, :head]) * scale
                raised = jnp.where(allowed, jnp.exp(s), 0.0)
                mixed = dot(raised.astype(BF16), kv_ref[:, head:])
                mixed = mixed / jnp.sum(raised, axis=1, keepdims=True)
                heads_mixed.append(mixed.astype(BF16))
            mixed = jnp.concatenate(heads_mixed, axis=1)
            low = dot_nt(mixed, sho_ref[...])
            low = jnp.where(meta_ref[here, 0:1] == oslot_ref[...], low, 0.0)
            high = low.astype(BF16)
            rest = (low - high.astype(F32)).astype(BF16)
            step = min(512, width)
            for c in range(0, width, step):
                cut = slice(c, c + step)
                expand = exo_ref[:, cut]
                term = dot(mixed, wo_ref[:, cut])
                term = term + ADAPTER_FACTOR * (dot(high, expand) + dot(rest, expand))
                target[there, cut] = term.astype(BF16)
            return carry

        loop(blocks // 2, one, 0)

    attend(part_ref, rows // 2)
    attend(own_ref, 0)


def attention(spots, tokens, weights, meta, pieces, parts, adapters):
    gain, wq, up, qg, kg, sho, wo, exo = weights
    own_rows, width = tokens[0].shape
    rows = own_rows * len(tokens)
    chips, cols, _ = parts[0].shape
    query_cols = wq.shape[1]
    head = qg.shape[1]
    ranks = pieces[0].shape[1]
    half = jax.ShapeDtypeStruct((rows // 2, width), BF16)
    flops = 2 * rows * (width * (adapters * ranks + 2 * query_cols + 2 * head) + rows * query_cols)
    return pl.pallas_call(
        functools.partial(attention_kernel, len(tokens), len(pieces), len(parts)),
        out_shape=(half, half, jax.ShapeDtypeStruct((rows, 2 * head), BF16)),
        in_specs=[SMEM] + [VMEM] * 10 + [ANY] * (4 + len(tokens) + len(pieces) + len(parts)),
        out_specs=(VMEM, VMEM, VMEM),
        scratch_shapes=[
            pltpu.VMEM(wq.shape, BF16),
            pltpu.VMEM(up.shape, BF16),
            pltpu.VMEM(wo.shape, BF16),
            pltpu.VMEM(exo.shape, BF16),
            pltpu.VMEM((rows, width), BF16),
            pltpu.VMEM((adapters, ranks, width), BF16),
            pltpu.VMEM((2 * chips, cols, width), BF16),
            pltpu.VMEM((rows, query_cols), F32),
            pltpu.VMEM((rows, 2 * head), F32),
            pltpu.VMEM((rows, query_cols), BF16),
            pltpu.SemaphoreType.DMA((2 * chips + 4,)),
            pltpu.SemaphoreType.DMA((len(pieces),)),
            pltpu.SemaphoreType.DMA((2 * chips,)),
        ],
        compiler_params=pltpu.CompilerParams(vmem_limit_bytes=60 * MIB),
        cost_estimate=pl.CostEstimate(
            flops=flops, bytes_accessed=16 * MIB, transcendentals=rows * rows
        ),
        name="attention",
    )(spots, gain, *meta, qg, kg, sho, wq, up, wo, exo, *tokens, *pieces, *parts)


def pages_kernel(first_ref, length_ref, page_ref, entries_ref, out_ref):
    columns, extent = entries_ref.shape
    rows = extent - PAGE
    window = 2 * PAGE
    gap = lax.broadcasted_iota(jnp.int32, (window, PAGE), 0) - lax.broadcasted_iota(
        jnp.int32, (window, PAGE), 1
    )
    lane = lax.broadcasted_iota(jnp.int32, (columns, PAGE), 1)

    def one(n, carry):
        length = length_ref[n]
        page = page_ref[n]

        @pl.when(length > 0)
        def _():
            first = jnp.minimum(first_ref[n], rows - 1)
            base = pl.multiple_of(first // PAGE * PAGE, PAGE)
            pick = (gap == first - base).astype(F32).astype(BF16)
            moved = dot(entries_ref[:, pl.ds(base, window)], pick)
            out_ref[page] = jnp.where(lane < length, moved, 0.0).astype(BF16)

        @pl.when(length <= 0)
        def _():
            out_ref[page] = jnp.zeros((columns, PAGE), BF16)

        return carry

    lax.fori_loop(0, page_ref.shape[0], one, 0)


def fill_pages(first, length, page, entries):
    rows, columns = entries.shape
    count = page.shape[0]
    turned = jnp.pad(entries.T, ((0, 0), (0, PAGE)))
    return pl.pallas_call(
        pages_kernel,
        out_shape=jax.ShapeDtypeStruct((count, columns, PAGE), BF16),
        in_specs=[SMEM, SMEM, SMEM, VMEM],
        out_specs=VMEM,
        compiler_params=pltpu.CompilerParams(vmem_limit_bytes=32 * MIB),
        cost_estimate=pl.CostEstimate(
            flops=count * columns * PAGE * PAGE * 16, bytes_accessed=4 * MIB, transcendentals=0
        ),
        name="fill_pages",
    )(first, length, page, turned)


def start_all(copies):
    for copy in copies:
        copy.start()
    return copies


def wait_all(copies):
    for copy in copies:
        copy.wait()


def token_copies(pieces, x_ref, sems):
    rows = pieces[0].shape[0]
    return [
        pltpu.make_async_copy(piece, x_ref.at[pl.ds(i * rows, rows)], sems.at[i])
        for i, piece in enumerate(pieces)
    ]


def pick_rows(slot_t_ref, x_ref, rows_ref, begin, end, capacity):
    line = lax.broadcasted_iota(jnp.int32, (capacity, x_ref.shape[0]), 0)
    pick = jnp.concatenate(
        [
            (slot_t_ref[n : n + 1, :] == line).astype(F32).astype(BF16)
            for n in range(begin, end)
        ],
        axis=0,
    )
    width = x_ref.shape[1]
    step = min(512, width)
    for c in range(0, width, step):
        rows_ref[:, c : c + step] = dot(pick, x_ref[:, c : c + step]).astype(BF16)


def combine(slot_ref, weight_ref, y_ref, target, offset, capacity):
    rows, width = target.shape
    experts = slot_ref.shape[1]
    tile = min(256, rows)
    step = min(512, width)
    line = lax.broadcasted_iota(jnp.int32, (tile, capacity), 1)

    def mix(i, carry):
        there = pl.ds(pl.multiple_of(i * tile, tile), tile)
        here = pl.ds(pl.multiple_of(offset + i * tile, tile), tile)
        spread = jnp.concatenate(
            [
                jnp.where(
                    slot_ref[here, n : n + 1] == line, weight_ref[here, n : n + 1], 0.0
                ).astype(BF16)
                for n in range(experts)
            ],
            axis=1,
        )
        for c in range(0, width, step):
            target[there, c : c + step] = dot(spread, y_ref[:, c : c + step]).astype(BF16)
        return carry

    loop(rows // tile, mix, 0)


def experts_kernel(blocks, capacity, slot_ref, slot_t_ref, weight_ref, *refs):
    pieces, refs = refs[:blocks], refs[blocks:]
    gate_ref, up_ref, down_ref, own_ref, part_ref = refs[:5]
    x_ref, rows_ref, y_ref, gate_buf, up_buf, down_buf, x_sems, w_sems = refs[5:]
    experts = slot_ref.shape[1]
    slots = gate_buf.shape[0]
    streams = ((gate_ref, gate_buf), (up_ref, up_buf), (down_ref, down_buf))

    def copy(k, e, s):
        source, buffer = streams[k]
        return pltpu.make_async_copy(source.at[e], buffer.at[s], w_sems.at[k, s])

    tokens = start_all(token_copies(pieces, x_ref, x_sems))
    for e in range(min(slots, experts)):
        for k in range(3):
            copy(k, e, e).start()
    wait_all(tokens)
    pick_rows(slot_t_ref, x_ref, rows_ref, 0, experts, capacity)

    def one(e, carry):
        s = lax.rem(e, slots)
        here = pl.ds(pl.multiple_of(e * capacity, capacity), capacity)
        x = rows_ref[here, :]
        copy(0, e, s).wait()
        gate = dot_nt(x, gate_buf[s])
        copy(1, e, s).wait()
        up = dot_nt(x, up_buf[s])
        hidden = (gate / (1.0 + jnp.exp(-gate)) * up).astype(BF16)
        copy(2, e, s).wait()
        y_ref[here, :] = dot(hidden, down_buf[s]).astype(BF16)

        @pl.when(e + slots < experts)
        def _():
            for k in range(3):
                copy(k, e + slots, s).start()

        return carry

    lax.fori_loop(0, experts, one, 0)
    combine(slot_ref, weight_ref, y_ref, part_ref, own_ref.shape[0], capacity)
    combine(slot_ref, weight_ref, y_ref, own_ref, 0, capacity)


def expert_layer(slot, weight, pieces, gate, up, down, capacity):
    experts, hidden, width = gate.shape
    own_rows = pieces[0].shape[0]
    total = own_rows * len(pieces)
    slots = min(3 if total <= 512 else 2, experts)
    half = jax.ShapeDtypeStruct((total // 2, width), BF16)
    return pl.pallas_call(
        functools.partial(experts_kernel, len(pieces), capacity),
        out_shape=(half, half),
        in_specs=[VMEM] * 3 + [ANY] * (3 + len(pieces)),
        out_specs=(VMEM, VMEM),
        scratch_shapes=[
            pltpu.VMEM((total, width), BF16),
            pltpu.VMEM((experts * capacity, width), BF16),
            pltpu.VMEM((experts * capacity, width), BF16),
            pltpu.VMEM((slots, hidden, width), BF16),
            pltpu.VMEM((slots, hidden, width), BF16),
            pltpu.VMEM((slots, hidden, width), BF16),
            pltpu.SemaphoreType.DMA((len(pieces),)),
            pltpu.SemaphoreType.DMA((3, slots)),
        ],
        compiler_params=pltpu.CompilerParams(vmem_limit_bytes=60 * MIB),
        cost_estimate=pl.CostEstimate(
            flops=6 * experts * capacity * hidden * width,
            bytes_accessed=6 * experts * hidden * width,
            transcendentals=experts * capacity * hidden,
        ),
        name="experts",
    )(slot, slot.T, weight, *pieces, gate, up, down)


def other_core(value, parts):
    return lax.ppermute(value, "tensor", [(i, i ^ 1) for i in range(parts)])


def swap_chips(value, parts, by):
    return lax.ppermute(value, "tensor", [(i, i ^ (2 * by)) for i in range(parts)])


def swap_holder(value, holders, by):
    return lax.ppermute(value, "dp", [(i, i ^ by) for i in range(holders)])


def gather_blocks(own, parts, between=lambda blocks: blocks):
    chips = parts // 2
    blocks = {0: own}
    bit = chips // 2
    while bit:
        blocks.update({i ^ bit: swap_chips(block, parts, bit) for i, block in blocks.items()})
        if bit == chips // 2:
            blocks = between(blocks)
        bit //= 2
    mine = [blocks[i] for i in range(chips)]
    return mine + [other_core(block, parts) for block in mine]


def scatter_terms(own, part, parts):
    chips = parts // 2
    sums = pair_sum(hold(own), other_core(part, parts), chips)
    return [sums[0]] + [swap_chips(sums[i], parts, i) for i in range(1, chips)]


def from_here(rows, chip, core, chips):
    split = rows.reshape((chips, 2, -1) + rows.shape[1:])
    split = jnp.where(core == 0, split, split[:, ::-1])
    bit = 1
    while bit < chips:
        pairs = split.reshape((chips // (2 * bit), 2, bit) + split.shape[1:])
        split = jnp.where((chip & bit) == 0, pairs, pairs[:, ::-1]).reshape(split.shape)
        bit *= 2
    return split


def to_device(rows, chip, core, chips):
    return jnp.swapaxes(from_here(rows, chip, core, chips), 0, 1).reshape(rows.shape)


def to_group(rows, chip, core, chips):
    split = jnp.swapaxes(rows.reshape((2, chips, -1) + rows.shape[1:]), 0, 1)
    return from_here(split.reshape(rows.shape), chip, core, chips).reshape(rows.shape)


def local(
    tokens,
    attn_gain,
    moe_gain,
    q_gain,
    k_gain,
    query_weight,
    w_kv,
    w_o,
    w_gate,
    w_up,
    w_down,
    shrink_qkv,
    shrink_o,
    query_up_factors,
    key_value_up_factors,
    expand_o,
    lengths,
    groups,
    adapter_of_request,
    adapter_slot,
    page_table,
    expert_ids,
    expert_gates,
):
    parts = lax.axis_size("tensor")
    place = lax.axis_index("tensor")
    holders = lax.axis_size("dp")
    holder = lax.axis_index("dp")
    chips, chip, core = parts // 2, place // 2, place % 2
    own_rows, width = tokens.shape
    total = own_rows * parts
    head_length = q_gain.shape[0]
    adapters, rank, kv_width = key_value_up_factors.shape
    kv_heads = kv_width // (2 * head_length)
    held, ranks = shrink_qkv.shape[:2]
    head = place * kv_heads // parts
    query_cols = query_weight.shape[1]
    experts = w_gate.shape[0]

    half = held // 2
    half_own = lax.dynamic_slice_in_dim(shrink_qkv, core * half, half, 0)
    cuts = [
        lax.dynamic_index_in_dim(w_kv, 2 * (chip ^ j) * kv_heads // parts, 1, keepdims=False)
        for j in range(chips)
    ]
    tokens_late, half_own, cuts = lax.optimization_barrier((tokens, half_own, cuts))
    mine = [cuts[0]] + [swap_chips(cuts[j], parts, j) for j in range(1, chips)]
    mine = jnp.stack(mine)
    head_parts = [mine, other_core(mine, parts)]
    halves = [swap_holder(half_own, holders, r) for r in range(1, holders)]

    def between(blocks):
        blocks, halves[:] = lax.optimization_barrier((blocks, halves))
        return blocks

    gathered = gather_blocks(tokens_late, parts, between)
    pieces, spots = [shrink_qkv], [chip, core, holder * held]
    for r, got in enumerate(halves, 1):
        pieces += [got, other_core(got, parts)]
        begin = (holder ^ r) * held
        spots += [begin + core * half, begin + (1 - core) * half]
    shrink_rows = shrink_o.reshape(adapters * rank, query_cols)

    line = jnp.arange(total, dtype=jnp.int32)
    side, number = line // (total // 2), line // own_rows % chips
    position = ((number ^ chip) * 2 + (side ^ core)) * own_rows + line % own_rows
    length_row, group_row, adapter_row = lengths[0], groups[0], adapter_of_request[0]
    ends = jnp.cumsum(length_row)
    starts = ends - length_row
    request = jnp.sum((ends[None, :] <= position[:, None]).astype(jnp.int32), axis=1)
    same = group_row[:, None] == group_row[None, :]
    group_first = jnp.min(jnp.where(same, starts[None, :], total), axis=1)
    slot_of_request = lookup(adapter_row, adapter_slot)
    group = lookup(request, group_row)
    rope_pos = position - lookup(request, group_first)
    slot = lookup(request, slot_of_request)
    meta_col = jnp.stack([slot, group, position], axis=1)
    meta_row = jnp.stack([group, position], axis=0)
    freq = jnp.exp(
        -jnp.arange(head_length // 2, dtype=F32) * (2.0 * math.log(ROPE_BASE) / head_length)
    )
    angle = rope_pos.astype(F32)[:, None] * freq[None, :]
    cosine, sine = jnp.cos(angle), jnp.sin(angle)
    cosine = jnp.concatenate([cosine, cosine], axis=1)
    sine = jnp.concatenate([-sine, sine], axis=1)
    colslot = (jnp.arange(adapters * ranks, dtype=jnp.int32) // ranks)[None, :]
    oslot = (jnp.arange(adapters * rank, dtype=jnp.int32) // rank)[None, :]

    up_kv = lax.dynamic_index_in_dim(
        key_value_up_factors.reshape(adapters, rank, kv_heads, 2, head_length), head, 2, keepdims=False
    )
    up = jnp.concatenate(
        [
            jnp.pad(query_up_factors, ((0, 0), (0, 2 * rank), (0, 0))),
            jnp.pad(up_kv[:, :, 0], ((0, 0), (rank, rank), (0, 0))),
            jnp.pad(up_kv[:, :, 1], ((0, 0), (2 * rank, 0), (0, 0))),
        ],
        axis=2,
    ).reshape(adapters * ranks, query_cols + 2 * head_length)

    weights = (
        attn_gain.reshape(1, -1),
        query_weight,
        up,
        q_gain.reshape(1, -1),
        k_gain.reshape(1, -1),
        shrink_rows,
        w_o,
        expand_o.reshape(adapters * rank, width),
    )
    meta = (meta_col, meta_row, colslot, oslot, cosine, sine)
    own, part, entries = attention(
        jnp.stack(spots).astype(jnp.int32),
        gathered,
        weights,
        meta,
        pieces,
        head_parts,
        adapters,
    )
    arrived = scatter_terms(own, part, parts)

    (arrived[0], entries, starts, length_row, page_table, expert_ids, expert_gates, moe_gain) = (
        lax.optimization_barrier(
            (
                arrived[0],
                entries,
                starts,
                length_row,
                page_table,
                expert_ids,
                expert_gates,
                moe_gain,
            )
        )
    )

    local_cols = kv_width // parts
    kept = lax.dynamic_slice_in_dim(
        entries, place * local_cols - head * 2 * head_length, local_cols, 1
    )
    page_row = page_table[0]
    per_request = page_row.shape[0] // length_row.shape[0]
    offset = PAGE * jnp.arange(per_request, dtype=jnp.int32)[None, :]
    page_first = (starts[:, None] + offset).reshape(-1)
    page_length = jnp.clip(length_row[:, None] - offset, 0, PAGE).reshape(-1)
    kv_pages = fill_pages(page_first, page_length, page_row, to_group(kept, chip, core, chips))

    arrived[0], kv_pages = lax.optimization_barrier((arrived[0], kv_pages))
    attn_own, moe_own = residual_norm(tokens, moe_gain, arrived)

    capacity = CAP_DEV * parts
    ids = to_device(expert_ids, chip, core, chips)
    gates = to_device(expert_gates, chip, core, chips)
    share = gates / jnp.sum(gates, axis=1, keepdims=True)
    own_experts = place * experts + jnp.arange(experts, dtype=jnp.int32)
    chosen = ids[:, :, None] == own_experts[None, None, :]
    hit = jnp.any(chosen, axis=1)
    weight = jnp.sum(jnp.where(chosen, share[:, :, None], 0.0), axis=1)
    before = dot((line[:, None] > line[None, :]).astype(BF16), hit.astype(BF16)).astype(jnp.int32)
    slot_in = jnp.where(hit, before, -1)

    own, part = expert_layer(
        slot_in, weight, gather_blocks(moe_own, parts), w_gate, w_up, w_down, capacity
    )
    moe_total = sum(p.astype(F32) for p in scatter_terms(own, part, parts)).astype(BF16)
    return (attn_own, moe_total, kv_pages)


def solution(mesh):
    placed = (
        P(("dp", "tensor"), None),
        P(),
        P(),
        P(),
        P(),
        P(None, "tensor"),
        P("tensor", None, None),
        P("tensor", None),
        P("tensor", None, None),
        P("tensor", None, None),
        P("tensor", None, None),
        P("dp", None, None),
        P(None, None, "tensor"),
        P(None, None, "tensor"),
        P(),
        P(),
        P("dp", None),
        P("dp", None),
        P("dp", None),
        P(),
        P("dp", None),
        P("dp", None),
        P("dp", None),
    )
    return jax.shard_map(
        local,
        mesh=mesh,
        in_specs=placed,
        out_specs=(P(("dp", "tensor"), None), P(("dp", "tensor"), None), P("dp", "tensor", None)),
        check_vma=False,
    )
```

```python
import functools
import math

import jax
import jax.numpy as jnp
from jax import lax
from jax.experimental import pallas as pl
from jax.experimental.pallas import tpu as pltpu
from jax.sharding import PartitionSpec as P

PAGE = 128
CAP_DEV = 16
NORM_EPS = 1e-06
ROPE_BASE = 1000000.0
ADAPTER_FACTOR = 0.5
MIB = 1 << 20
BF16 = jnp.bfloat16
F32 = jnp.float32
VMEM = pl.BlockSpec(memory_space=pltpu.VMEM)
SMEM = pl.BlockSpec(memory_space=pltpu.SMEM)
ANY = pl.BlockSpec(memory_space=pl.ANY)
HBM = pl.BlockSpec(memory_space=pltpu.HBM)


def dot(a, b):
    return jnp.dot(a, b, preferred_element_type=F32)


def dot_nt(a, b):
    return lax.dot_general(a, b, (((1,), (1,)), ((), ())), preferred_element_type=F32)


def lookup(index_value, table):
    match = index_value[:, None] == jnp.arange(table.shape[0], dtype=jnp.int32)[None, :]
    return jnp.sum(jnp.where(match, table[None, :], 0), axis=1)


def loop(count, body, carry):
    if count <= 2:
        for i in range(count):
            carry = body(i, carry)
        return carry
    return lax.fori_loop(0, count, body, carry)


def store_rows(own_ref, part_ref, i, blocks, cut, term):
    block = term.shape[0]
    if blocks == 1:
        own_ref[:, cut] = term[: block // 2]
        part_ref[:, cut] = term[block // 2 :]
        return
    half = blocks // 2

    @pl.when(i < half)
    def _():
        own_ref[pl.ds(pl.multiple_of(jnp.minimum(i, half - 1) * block, block), block), cut] = term

    @pl.when(i >= half)
    def _():
        part_ref[pl.ds(pl.multiple_of(jnp.maximum(i - half, 0) * block, block), block), cut] = term


def rms(v, gain):
    return v * lax.rsqrt(jnp.mean(v * v, axis=-1, keepdims=True) + NORM_EPS) * gain


def residual_kernel(x_ref, gain_ref, *refs):
    parts, (attn_ref, out_ref) = refs[:-2], refs[-2:]
    total = parts[0][...].astype(F32)
    for part in parts[1:]:
        total = total + part[...].astype(F32)
    attn_ref[...] = total.astype(BF16)
    out_ref[...] = rms(x_ref[...].astype(F32) + total, gain_ref[...].astype(F32)).astype(BF16)


def residual_norm(x, gain, parts):
    shape = jax.ShapeDtypeStruct(x.shape, BF16)
    return pl.pallas_call(
        residual_kernel,
        out_shape=(shape, shape),
        in_specs=[VMEM] * (2 + len(parts)),
        out_specs=(VMEM, VMEM),
        name="residual_norm",
    )(x, gain.reshape(1, -1), *parts)


def pair_kernel(a_ref, b_ref, *outs):
    rows = outs[0].shape[0]
    for i, out in enumerate(outs):
        here = slice(i * rows, (i + 1) * rows)
        out[...] = (a_ref[here, :].astype(F32) + b_ref[here, :].astype(F32)).astype(BF16)


def hold_kernel(source_ref, out_ref, sem):
    copy = pltpu.make_async_copy(source_ref, out_ref, sem)
    copy.start()
    copy.wait()


def hold(rows):
    return pl.pallas_call(
        hold_kernel,
        out_shape=pltpu.VMEM(rows.shape, BF16),
        in_specs=[HBM],
        out_specs=VMEM,
        scratch_shapes=[pltpu.SemaphoreType.DMA],
        compiler_params=pltpu.CompilerParams(vmem_limit_bytes=4 * MIB),
        name="hold",
    )(pltpu.with_memory_space_constraint(rows, pltpu.HBM))


def pair_sum(a, b, count):
    shape = jax.ShapeDtypeStruct((a.shape[0] // count, a.shape[1]), BF16)
    return pl.pallas_call(
        pair_kernel,
        out_shape=(shape,) * count,
        in_specs=[VMEM, VMEM],
        out_specs=(VMEM,) * count,
        compiler_params=pltpu.CompilerParams(vmem_limit_bytes=24 * MIB),
        name="pair_sum",
    )(a, b)


def attention_kernel(
    token_blocks,
    factor_blocks,
    head_blocks,
    spot_ref,
    gain_ref,
    meta_ref,
    row_ref,
    colslot_ref,
    oslot_ref,
    cos_ref,
    sin_ref,
    qg_ref,
    kg_ref,
    sho_ref,
    *refs,
):
    (wq_source, up_source, wo_source, exo_source), refs = refs[:4], refs[4:]
    tokens, refs = refs[:token_blocks], refs[token_blocks:]
    pieces, refs = refs[:factor_blocks], refs[factor_blocks:]
    parts, refs = refs[:head_blocks], refs[head_blocks:]
    own_ref, part_ref, kv_ref = refs[:3]
    wq_ref, up_ref, wo_ref, exo_ref, x_ref, s_ref, w_ref, qf_ref, kvf_ref, q_ref = refs[3:13]
    x_sems, s_sems, w_sems = refs[13:]
    rows, width = x_ref.shape
    query_cols = wq_ref.shape[1]
    head = qg_ref.shape[1]
    heads = query_cols // head
    block = min(512, rows)
    blocks = rows // block
    scale = head**-0.5
    devices, cols, _ = w_ref.shape
    chips = devices // 2
    own_rows = rows // devices
    chip, core = spot_ref[0], spot_ref[1]
    token_copies, factor_copies, head_copies = [], [], []
    for i, piece in enumerate(tokens):
        target = x_ref.at[pl.ds(i * own_rows, own_rows)]
        token_copies.append(pltpu.make_async_copy(piece, target, x_sems.at[i]))
        token_copies[-1].start()
    for q in range(2):
        for j in range(chips):
            device = (chip ^ j) * 2 + (core ^ q)
            head_copies.append(
                pltpu.make_async_copy(
                    parts[q].at[j], w_ref.at[device], w_sems.at[q * chips + j]
                )
            )
            head_copies[-1].start()
    token_copies.append(pltpu.make_async_copy(wq_source, wq_ref, x_sems.at[devices]))
    token_copies[-1].start()
    factor_copies.append(pltpu.make_async_copy(up_source, up_ref, x_sems.at[devices + 1]))
    factor_copies[-1].start()
    for i, piece in enumerate(pieces):
        target = s_ref.at[pl.ds(spot_ref[2 + i], piece.shape[0])]
        factor_copies.append(pltpu.make_async_copy(piece, target, s_sems.at[i]))
        factor_copies[-1].start()
    last_copies = [
        pltpu.make_async_copy(wo_source, wo_ref, x_sems.at[devices + 2]),
        pltpu.make_async_copy(exo_source, exo_ref, x_sems.at[devices + 3]),
    ]
    for copy in last_copies:
        copy.start()
    factors = s_ref.shape[0] * s_ref.shape[1]
    gain = gain_ref[...].astype(F32)
    qg = qg_ref[...].astype(F32)
    kg = kg_ref[...].astype(F32)

    for copy in token_copies + head_copies:
        copy.wait()

    def project(i, carry):
        here = pl.ds(pl.multiple_of(i * block, block), block)
        x = rms(x_ref[here, :].astype(F32), gain).astype(BF16)
        x_ref[here, :] = x
        qf_ref[here, :] = dot(x, wq_ref[...])
        kvf_ref[here, :] = dot_nt(x, w_ref[...].reshape(devices * cols, width))
        return carry

    loop(blocks, project, 0)

    for copy in factor_copies:
        copy.wait()

    def turned(v, gain, here):
        v = rms(v, gain)
        return v * cos_ref[here, :] + pltpu.roll(v, head // 2, 1) * sin_ref[here, :]

    def adapt(i, carry):
        here = pl.ds(pl.multiple_of(i * block, block), block)
        low = dot_nt(x_ref[here, :], s_ref[...].reshape(factors, width))
        low = jnp.where(meta_ref[here, 0:1] == colslot_ref[...], low, 0.0).astype(BF16)
        delta = ADAPTER_FACTOR * dot(low, up_ref[...])
        q = qf_ref[here, :] + delta[:, :query_cols]
        kv = (kvf_ref[here, :] + delta[:, query_cols:]).astype(BF16)
        for h in range(heads):
            cut = slice(h * head, (h + 1) * head)
            q_ref[here, cut] = turned(q[:, cut], qg, here).astype(BF16)
        kv_ref[here, :head] = turned(kv[:, :head].astype(F32), kg, here).astype(BF16)
        kv_ref[here, head:] = kv[:, head:]
        return carry

    loop(blocks, adapt, 0)

    for copy in last_copies:
        copy.wait()

    def attend(i, carry):
        here = pl.ds(pl.multiple_of(i * block, block), block)
        allowed = (row_ref[1:2, :] <= meta_ref[here, 2:3]) & (
            row_ref[0:1, :] == meta_ref[here, 1:2]
        )
        heads_mixed = []
        for h in range(heads):
            cut = slice(h * head, (h + 1) * head)
            s = dot_nt(q_ref[here, cut], kv_ref[:, :head]) * scale
            raised = jnp.where(allowed, jnp.exp(s), 0.0)
            mixed = dot(raised.astype(BF16), kv_ref[:, head:])
            mixed = mixed / jnp.sum(raised, axis=1, keepdims=True)
            heads_mixed.append(mixed.astype(BF16))
        mixed = jnp.concatenate(heads_mixed, axis=1)
        low = dot_nt(mixed, sho_ref[...])
        low = jnp.where(meta_ref[here, 0:1] == oslot_ref[...], low, 0.0)
        high = low.astype(BF16)
        rest = (low - high.astype(F32)).astype(BF16)
        step = min(512, width)
        for c in range(0, width, step):
            cut = slice(c, c + step)
            expand = exo_ref[:, cut]
            term = dot(mixed, wo_ref[:, cut])
            term = term + ADAPTER_FACTOR * (dot(high, expand) + dot(rest, expand))
            store_rows(own_ref, part_ref, i, blocks, cut, term.astype(BF16))
        return carry

    loop(blocks, attend, 0)


def attention(spots, tokens, weights, meta, pieces, parts, adapters):
    gain, wq, up, qg, kg, sho, wo, exo = weights
    own_rows, width = tokens[0].shape
    rows = own_rows * len(tokens)
    chips, cols, _ = parts[0].shape
    query_cols = wq.shape[1]
    head = qg.shape[1]
    ranks = pieces[0].shape[1]
    half = jax.ShapeDtypeStruct((rows // 2, width), BF16)
    flops = 2 * rows * (width * (adapters * ranks + 2 * query_cols + 2 * head) + rows * query_cols)
    return pl.pallas_call(
        functools.partial(attention_kernel, len(tokens), len(pieces), len(parts)),
        out_shape=(half, half, jax.ShapeDtypeStruct((rows, 2 * head), BF16)),
        in_specs=[SMEM] + [VMEM] * 10 + [ANY] * (4 + len(tokens) + len(pieces) + len(parts)),
        out_specs=(VMEM, VMEM, VMEM),
        scratch_shapes=[
            pltpu.VMEM(wq.shape, BF16),
            pltpu.VMEM(up.shape, BF16),
            pltpu.VMEM(wo.shape, BF16),
            pltpu.VMEM(exo.shape, BF16),
            pltpu.VMEM((rows, width), BF16),
            pltpu.VMEM((adapters, ranks, width), BF16),
            pltpu.VMEM((2 * chips, cols, width), BF16),
            pltpu.VMEM((rows, query_cols), F32),
            pltpu.VMEM((rows, 2 * head), F32),
            pltpu.VMEM((rows, query_cols), BF16),
            pltpu.SemaphoreType.DMA((2 * chips + 4,)),
            pltpu.SemaphoreType.DMA((len(pieces),)),
            pltpu.SemaphoreType.DMA((2 * chips,)),
        ],
        compiler_params=pltpu.CompilerParams(vmem_limit_bytes=60 * MIB),
        cost_estimate=pl.CostEstimate(
            flops=flops, bytes_accessed=16 * MIB, transcendentals=rows * rows
        ),
        name="attention",
    )(spots, gain, *meta, qg, kg, sho, wq, up, wo, exo, *tokens, *pieces, *parts)


def pages_kernel(first_ref, length_ref, page_ref, entries_ref, out_ref):
    columns, extent = entries_ref.shape
    rows = extent - PAGE
    window = 2 * PAGE
    gap = lax.broadcasted_iota(jnp.int32, (window, PAGE), 0) - lax.broadcasted_iota(
        jnp.int32, (window, PAGE), 1
    )
    lane = lax.broadcasted_iota(jnp.int32, (columns, PAGE), 1)

    def one(n, carry):
        length = length_ref[n]
        page = page_ref[n]

        @pl.when(length > 0)
        def _():
            first = jnp.minimum(first_ref[n], rows - 1)
            base = pl.multiple_of(first // PAGE * PAGE, PAGE)
            pick = (gap == first - base).astype(F32).astype(BF16)
            moved = dot(entries_ref[:, pl.ds(base, window)], pick)
            out_ref[page] = jnp.where(lane < length, moved, 0.0).astype(BF16)

        @pl.when(length <= 0)
        def _():
            out_ref[page] = jnp.zeros((columns, PAGE), BF16)

        return carry

    lax.fori_loop(0, page_ref.shape[0], one, 0)


def fill_pages(first, length, page, entries):
    rows, columns = entries.shape
    count = page.shape[0]
    turned = jnp.pad(entries.T, ((0, 0), (0, PAGE)))
    return pl.pallas_call(
        pages_kernel,
        out_shape=jax.ShapeDtypeStruct((count, columns, PAGE), BF16),
        in_specs=[SMEM, SMEM, SMEM, VMEM],
        out_specs=VMEM,
        compiler_params=pltpu.CompilerParams(vmem_limit_bytes=32 * MIB),
        cost_estimate=pl.CostEstimate(
            flops=count * columns * PAGE * PAGE * 16, bytes_accessed=4 * MIB, transcendentals=0
        ),
        name="fill_pages",
    )(first, length, page, turned)


def start_all(copies):
    for copy in copies:
        copy.start()
    return copies


def wait_all(copies):
    for copy in copies:
        copy.wait()


def token_copies(pieces, x_ref, sems):
    rows = pieces[0].shape[0]
    return [
        pltpu.make_async_copy(piece, x_ref.at[pl.ds(i * rows, rows)], sems.at[i])
        for i, piece in enumerate(pieces)
    ]


def pick_rows(slot_t_ref, x_ref, rows_ref, begin, end, capacity):
    line = lax.broadcasted_iota(jnp.int32, (capacity, x_ref.shape[0]), 0)
    pick = jnp.concatenate(
        [
            (slot_t_ref[n : n + 1, :] == line).astype(F32).astype(BF16)
            for n in range(begin, end)
        ],
        axis=0,
    )
    width = x_ref.shape[1]
    step = min(512, width)
    for c in range(0, width, step):
        rows_ref[:, c : c + step] = dot(pick, x_ref[:, c : c + step]).astype(BF16)


def combine(slot_ref, weight_ref, y_ref, own_ref, part_ref, capacity):
    rows, experts = slot_ref.shape
    width = y_ref.shape[1]
    tile = min(512, rows)
    step = min(512, width)
    line = lax.broadcasted_iota(jnp.int32, (tile, capacity), 1)

    def mix(i, carry):
        here = pl.ds(pl.multiple_of(i * tile, tile), tile)
        spread = jnp.concatenate(
            [
                jnp.where(
                    slot_ref[here, n : n + 1] == line, weight_ref[here, n : n + 1], 0.0
                ).astype(BF16)
                for n in range(experts)
            ],
            axis=1,
        )
        for c in range(0, width, step):
            cut = slice(c, c + step)
            term = dot(spread, y_ref[:, cut]).astype(BF16)
            store_rows(own_ref, part_ref, i, rows // tile, cut, term)
        return carry

    loop(rows // tile, mix, 0)


def experts_kernel(blocks, capacity, slot_ref, slot_t_ref, weight_ref, *refs):
    pieces, refs = refs[:blocks], refs[blocks:]
    gate_ref, up_ref, down_ref, own_ref, part_ref = refs[:5]
    x_ref, rows_ref, y_ref, gate_buf, up_buf, down_buf, x_sems, w_sems = refs[5:]
    experts = slot_ref.shape[1]
    slots = gate_buf.shape[0]
    streams = ((gate_ref, gate_buf), (up_ref, up_buf), (down_ref, down_buf))

    def copy(k, e, s):
        source, buffer = streams[k]
        return pltpu.make_async_copy(source.at[e], buffer.at[s], w_sems.at[k, s])

    tokens = start_all(token_copies(pieces, x_ref, x_sems))
    for e in range(min(slots, experts)):
        for k in range(3):
            copy(k, e, e).start()
    wait_all(tokens)
    pick_rows(slot_t_ref, x_ref, rows_ref, 0, experts, capacity)

    def one(e, carry):
        s = lax.rem(e, slots)
        here = pl.ds(pl.multiple_of(e * capacity, capacity), capacity)
        x = rows_ref[here, :]
        copy(0, e, s).wait()
        gate = dot_nt(x, gate_buf[s])
        copy(1, e, s).wait()
        up = dot_nt(x, up_buf[s])
        hidden = (gate / (1.0 + jnp.exp(-gate)) * up).astype(BF16)
        copy(2, e, s).wait()
        y_ref[here, :] = dot(hidden, down_buf[s]).astype(BF16)

        @pl.when(e + slots < experts)
        def _():
            for k in range(3):
                copy(k, e + slots, s).start()

        return carry

    lax.fori_loop(0, experts, one, 0)
    combine(slot_ref, weight_ref, y_ref, own_ref, part_ref, capacity)


def expert_layer(slot, slot_t, weight, pieces, gate, up, down, capacity):
    experts, hidden, width = gate.shape
    own_rows = pieces[0].shape[0]
    total = own_rows * len(pieces)
    slots = min(3 if total <= 512 else 2, experts)
    half = jax.ShapeDtypeStruct((total // 2, width), BF16)
    return pl.pallas_call(
        functools.partial(experts_kernel, len(pieces), capacity),
        out_shape=(half, half),
        in_specs=[VMEM] * 3 + [ANY] * (3 + len(pieces)),
        out_specs=(VMEM, VMEM),
        scratch_shapes=[
            pltpu.VMEM((total, width), BF16),
            pltpu.VMEM((experts * capacity, width), BF16),
            pltpu.VMEM((experts * capacity, width), BF16),
            pltpu.VMEM((slots, hidden, width), BF16),
            pltpu.VMEM((slots, hidden, width), BF16),
            pltpu.VMEM((slots, hidden, width), BF16),
            pltpu.SemaphoreType.DMA((len(pieces),)),
            pltpu.SemaphoreType.DMA((3, slots)),
        ],
        compiler_params=pltpu.CompilerParams(vmem_limit_bytes=60 * MIB),
        cost_estimate=pl.CostEstimate(
            flops=6 * experts * capacity * hidden * width,
            bytes_accessed=6 * experts * hidden * width,
            transcendentals=experts * capacity * hidden,
        ),
        name="experts",
    )(slot, slot_t, weight, *pieces, gate, up, down)


def other_core(value, parts):
    return lax.ppermute(value, "tensor", [(i, i ^ 1) for i in range(parts)])


def swap_chips(value, parts, by):
    return lax.ppermute(value, "tensor", [(i, i ^ (2 * by)) for i in range(parts)])


def swap_holder(value, holders, by):
    return lax.ppermute(value, "dp", [(i, i ^ by) for i in range(holders)])


def gather_blocks(own, parts, between=lambda blocks: blocks):
    chips = parts // 2
    blocks = {0: own}
    bit = chips // 2
    while bit:
        for i, block in list(blocks.items()):
            if i ^ bit not in blocks:
                blocks[i ^ bit] = swap_chips(block, parts, bit)
        if bit == chips // 2:
            if 1 not in blocks:
                blocks[1] = swap_chips(own, parts, 1)
            blocks = between(blocks)
        bit //= 2
    mine = [blocks[i] for i in range(chips)]
    return mine + [other_core(block, parts) for block in mine]


def scatter_terms(own, part, parts):
    chips = parts // 2
    sums = pair_sum(hold(own), other_core(part, parts), chips)
    return [sums[0]] + [swap_chips(sums[i], parts, i) for i in range(1, chips)]


def from_here(rows, chip, core, chips):
    split = rows.reshape((chips, 2, -1) + rows.shape[1:])
    split = jnp.where(core == 0, split, split[:, ::-1])
    bit = 1
    while bit < chips:
        pairs = split.reshape((chips // (2 * bit), 2, bit) + split.shape[1:])
        split = jnp.where((chip & bit) == 0, pairs, pairs[:, ::-1]).reshape(split.shape)
        bit *= 2
    return split


def to_device(rows, chip, core, chips):
    return jnp.swapaxes(from_here(rows, chip, core, chips), 0, 1).reshape(rows.shape)


def to_group(rows, chip, core, chips):
    split = jnp.swapaxes(rows.reshape((2, chips, -1) + rows.shape[1:]), 0, 1)
    return from_here(split.reshape(rows.shape), chip, core, chips).reshape(rows.shape)


def local(
    tokens,
    attn_gain,
    moe_gain,
    q_gain,
    k_gain,
    query_weight,
    w_kv,
    w_o,
    w_gate,
    w_up,
    w_down,
    shrink_qkv,
    shrink_o,
    query_up_factors,
    key_value_up_factors,
    expand_o,
    lengths,
    groups,
    adapter_of_request,
    adapter_slot,
    page_table,
    expert_ids,
    expert_gates,
):
    parts = lax.axis_size("tensor")
    place = lax.axis_index("tensor")
    holders = lax.axis_size("dp")
    holder = lax.axis_index("dp")
    chips, chip, core = parts // 2, place // 2, place % 2
    own_rows, width = tokens.shape
    total = own_rows * parts
    head_length = q_gain.shape[0]
    adapters, rank, kv_width = key_value_up_factors.shape
    kv_heads = kv_width // (2 * head_length)
    held, ranks = shrink_qkv.shape[:2]
    head = place * kv_heads // parts
    query_cols = query_weight.shape[1]
    experts = w_gate.shape[0]

    line = jnp.arange(total, dtype=jnp.int32)
    side, number = line // (total // 2), line // own_rows % chips
    position = ((number ^ chip) * 2 + (side ^ core)) * own_rows + line % own_rows
    length_row, group_row, adapter_row = lengths[0], groups[0], adapter_of_request[0]
    ends = jnp.cumsum(length_row)
    starts = ends - length_row
    request = jnp.sum((ends[None, :] <= position[:, None]).astype(jnp.int32), axis=1)
    same = group_row[:, None] == group_row[None, :]
    group_first = jnp.min(jnp.where(same, starts[None, :], total), axis=1)
    slot_of_request = lookup(adapter_row, adapter_slot)
    group = lookup(request, group_row)
    rope_pos = position - lookup(request, group_first)
    slot = lookup(request, slot_of_request)
    meta_col = jnp.stack([slot, group, position], axis=1)
    meta_row = jnp.stack([group, position], axis=0)
    freq = jnp.exp(
        -jnp.arange(head_length // 2, dtype=F32) * (2.0 * math.log(ROPE_BASE) / head_length)
    )
    angle = rope_pos.astype(F32)[:, None] * freq[None, :]
    cosine, sine = jnp.cos(angle), jnp.sin(angle)
    cosine = jnp.concatenate([cosine, cosine], axis=1)
    sine = jnp.concatenate([-sine, sine], axis=1)
    colslot = (jnp.arange(adapters * ranks, dtype=jnp.int32) // ranks)[None, :]
    oslot = (jnp.arange(adapters * rank, dtype=jnp.int32) // rank)[None, :]

    up_kv = lax.dynamic_index_in_dim(
        key_value_up_factors.reshape(adapters, rank, kv_heads, 2, head_length), head, 2, keepdims=False
    )
    up = jnp.concatenate(
        [
            jnp.pad(query_up_factors, ((0, 0), (0, 2 * rank), (0, 0))),
            jnp.pad(up_kv[:, :, 0], ((0, 0), (rank, rank), (0, 0))),
            jnp.pad(up_kv[:, :, 1], ((0, 0), (2 * rank, 0), (0, 0))),
        ],
        axis=2,
    ).reshape(adapters * ranks, query_cols + 2 * head_length)

    weights = (
        attn_gain.reshape(1, -1),
        query_weight,
        up,
        q_gain.reshape(1, -1),
        k_gain.reshape(1, -1),
        shrink_o.reshape(adapters * rank, query_cols),
        w_o,
        expand_o.reshape(adapters * rank, width),
    )
    meta = (meta_col, meta_row, colslot, oslot, cosine, sine)
    half = held // 2
    half_own = lax.dynamic_slice_in_dim(shrink_qkv, core * half, half, 0)
    halves = [swap_holder(half_own, holders, r) for r in range(1, holders)]
    spots = [chip, core, holder * held]
    for r in range(1, holders):
        begin = (holder ^ r) * held
        spots += [begin + core * half, begin + (1 - core) * half]
    spots = jnp.stack(spots).astype(jnp.int32)
    cuts = [
        lax.dynamic_index_in_dim(w_kv, 2 * (chip ^ j) * kv_heads // parts, 1, keepdims=False)
        for j in range(chips)
    ]

    def between(blocks):
        nonlocal cuts, weights, meta, spots
        blocks, halves[:2], cuts, weights, meta, spots = lax.optimization_barrier(
            (blocks, halves[:2], cuts, weights, meta, spots)
        )
        return blocks

    gathered = gather_blocks(tokens, parts, between)
    mine = [cuts[0]] + [swap_chips(cuts[j], parts, j) for j in range(1, chips)]
    mine = jnp.stack(mine)
    head_parts = [mine, other_core(mine, parts)]
    pieces = [shrink_qkv]
    for got in halves:
        pieces += [got, other_core(got, parts)]
    own, part, entries = attention(
        spots,
        gathered,
        weights,
        meta,
        pieces,
        head_parts,
        adapters,
    )
    arrived = scatter_terms(own, part, parts)

    (arrived[0], entries, starts, length_row, page_table, expert_ids, expert_gates, moe_gain) = (
        lax.optimization_barrier(
            (
                arrived[0],
                entries,
                starts,
                length_row,
                page_table,
                expert_ids,
                expert_gates,
                moe_gain,
            )
        )
    )

    local_cols = kv_width // parts
    kept = lax.dynamic_slice_in_dim(
        entries, place * local_cols - head * 2 * head_length, local_cols, 1
    )
    page_row = page_table[0]
    per_request = page_row.shape[0] // length_row.shape[0]
    offset = PAGE * jnp.arange(per_request, dtype=jnp.int32)[None, :]
    page_first = (starts[:, None] + offset).reshape(-1)
    page_length = jnp.clip(length_row[:, None] - offset, 0, PAGE).reshape(-1)
    kv_pages = fill_pages(page_first, page_length, page_row, to_group(kept, chip, core, chips))

    arrived[0], kv_pages = lax.optimization_barrier((arrived[0], kv_pages))
    attn_own, moe_own = residual_norm(tokens, moe_gain, arrived)

    capacity = CAP_DEV * parts
    ids = to_device(expert_ids, chip, core, chips)
    gates = to_device(expert_gates, chip, core, chips)
    share = gates / jnp.sum(gates, axis=1, keepdims=True)
    own_experts = place * experts + jnp.arange(experts, dtype=jnp.int32)
    chosen = ids[:, :, None] == own_experts[None, None, :]
    hit = jnp.any(chosen, axis=1)
    weight = jnp.sum(jnp.where(chosen, share[:, :, None], 0.0), axis=1)
    before = dot((line[:, None] > line[None, :]).astype(BF16), hit.astype(BF16)).astype(jnp.int32)
    slot_in = jnp.where(hit, before, -1)

    slot_t = slot_in.T

    def tables_first(blocks):
        nonlocal slot_in, slot_t, weight
        blocks, slot_in, slot_t, weight = lax.optimization_barrier(
            (blocks, slot_in, slot_t, weight)
        )
        return blocks

    gathered = gather_blocks(moe_own, parts, tables_first)
    own, part = expert_layer(slot_in, slot_t, weight, gathered, w_gate, w_up, w_down, capacity)
    moe_total = sum(p.astype(F32) for p in scatter_terms(own, part, parts)).astype(BF16)
    return (attn_own, moe_total, kv_pages)


def solution(mesh):
    placed = (
        P(("dp", "tensor"), None),
        P(),
        P(),
        P(),
        P(),
        P(None, "tensor"),
        P("tensor", None, None),
        P("tensor", None),
        P("tensor", None, None),
        P("tensor", None, None),
        P("tensor", None, None),
        P("dp", None, None),
        P(None, None, "tensor"),
        P(None, None, "tensor"),
        P(),
        P(),
        P("dp", None),
        P("dp", None),
        P("dp", None),
        P(),
        P("dp", None),
        P("dp", None),
        P("dp", None),
    )
    return jax.shard_map(
        local,
        mesh=mesh,
        in_specs=placed,
        out_specs=(P(("dp", "tensor"), None), P(("dp", "tensor"), None), P("dp", "tensor", None)),
        check_vma=False,
    )
```

```python
import functools
import math

import jax
import jax.numpy as jnp
from jax import lax
from jax.experimental import pallas as pl
from jax.experimental.pallas import tpu as pltpu
from jax.sharding import PartitionSpec as P

PAGE = 128
CAP_DEV = 16
NORM_EPS = 1e-06
ROPE_BASE = 1000000.0
ADAPTER_FACTOR = 0.5
MIB = 1 << 20
BF16 = jnp.bfloat16
F32 = jnp.float32
VMEM = pl.BlockSpec(memory_space=pltpu.VMEM)
SMEM = pl.BlockSpec(memory_space=pltpu.SMEM)
ANY = pl.BlockSpec(memory_space=pl.ANY)
HBM = pl.BlockSpec(memory_space=pltpu.HBM)


def dot(a, b):
    return jnp.dot(a, b, preferred_element_type=F32)


def dot_nt(a, b):
    return lax.dot_general(a, b, (((1,), (1,)), ((), ())), preferred_element_type=F32)


def lookup(index_value, table):
    match = index_value[:, None] == jnp.arange(table.shape[0], dtype=jnp.int32)[None, :]
    return jnp.sum(jnp.where(match, table[None, :], 0), axis=1)


def loop(count, body, carry):
    if count <= 2:
        for i in range(count):
            carry = body(i, carry)
        return carry
    return lax.fori_loop(0, count, body, carry)


def rms(v, gain):
    return v * lax.rsqrt(jnp.mean(v * v, axis=-1, keepdims=True) + NORM_EPS) * gain


def total_of(parts):
    total = parts[0][...].astype(F32)
    for part in parts[1:]:
        total = total + part[...].astype(F32)
    return total


def residual_kernel(count, x_ref, gain_ref, *refs):
    attn_ref, out_ref = refs[-2:]
    total = jnp.concatenate([total_of(refs[:count]), total_of(refs[count:-2])], axis=1)
    attn_ref[...] = total.astype(BF16)
    out_ref[...] = rms(x_ref[...].astype(F32) + total, gain_ref[...].astype(F32)).astype(BF16)


def residual_norm(x, gain, left, right):
    shape = jax.ShapeDtypeStruct(x.shape, BF16)
    return pl.pallas_call(
        functools.partial(residual_kernel, len(left)),
        out_shape=(shape, shape),
        in_specs=[VMEM] * (2 + len(left) + len(right)),
        out_specs=(VMEM, VMEM),
        name="residual_norm",
    )(x, gain.reshape(1, -1), *left, *right)


def total_kernel(count, *refs):
    out_ref = refs[-1]
    half = out_ref.shape[1] // 2
    out_ref[:, :half] = total_of(refs[:count]).astype(BF16)
    out_ref[:, half:] = total_of(refs[count:-1]).astype(BF16)


def total_rows(left, right):
    rows, half = left[0].shape
    return pl.pallas_call(
        functools.partial(total_kernel, len(left)),
        out_shape=jax.ShapeDtypeStruct((rows, 2 * half), BF16),
        in_specs=[VMEM] * (len(left) + len(right)),
        out_specs=VMEM,
        name="total_rows",
    )(*left, *right)


def hold_kernel(source_ref, out_ref, sem):
    copy = pltpu.make_async_copy(source_ref, out_ref, sem)
    copy.start()
    copy.wait()


def hold(rows):
    return pl.pallas_call(
        hold_kernel,
        out_shape=pltpu.VMEM(rows.shape, BF16),
        in_specs=[HBM],
        out_specs=VMEM,
        scratch_shapes=[pltpu.SemaphoreType.DMA],
        compiler_params=pltpu.CompilerParams(vmem_limit_bytes=4 * MIB),
        name="hold",
    )(pltpu.with_memory_space_constraint(rows, pltpu.HBM))


def pair_kernel(a_ref, b_ref, *outs):
    rows, half = outs[0].shape
    for i in range(len(outs) // 2):
        here = slice(i * rows, (i + 1) * rows)
        total = (a_ref[here, :].astype(F32) + b_ref[here, :].astype(F32)).astype(BF16)
        outs[2 * i][...] = total[:, :half]
        outs[2 * i + 1][...] = total[:, half:]


def pair_sum(a, b, count):
    shape = jax.ShapeDtypeStruct((a.shape[0] // count, a.shape[1] // 2), BF16)
    return pl.pallas_call(
        pair_kernel,
        out_shape=(shape,) * (2 * count),
        in_specs=[VMEM, VMEM],
        out_specs=(VMEM,) * (2 * count),
        compiler_params=pltpu.CompilerParams(vmem_limit_bytes=24 * MIB),
        name="pair_sum",
    )(a, b)


def attention_kernel(
    token_blocks,
    factor_blocks,
    head_blocks,
    spot_ref,
    gain_ref,
    meta_ref,
    row_ref,
    colslot_ref,
    oslot_ref,
    cos_ref,
    sin_ref,
    qg_ref,
    kg_ref,
    sho_ref,
    *refs,
):
    (wq_source, up_source, wo_source, exo_source), refs = refs[:4], refs[4:]
    tokens, refs = refs[:token_blocks], refs[token_blocks:]
    pieces, refs = refs[:factor_blocks], refs[factor_blocks:]
    parts, refs = refs[:head_blocks], refs[head_blocks:]
    own_ref, part_ref, kv_ref = refs[:3]
    wq_ref, up_ref, wo_ref, exo_ref, x_ref, s_ref, w_ref, qf_ref, kvf_ref, q_ref = refs[3:13]
    x_sems, s_sems, w_sems = refs[13:]
    rows, width = x_ref.shape
    query_cols = wq_ref.shape[1]
    head = qg_ref.shape[1]
    heads = query_cols // head
    block = min(256, rows // 2)
    blocks = rows // block
    scale = head**-0.5
    devices, cols, _ = w_ref.shape
    chips = devices // 2
    own_rows = rows // devices
    chip, core = spot_ref[0], spot_ref[1]
    token_copies, factor_copies, head_copies = [], [], []
    for i, piece in enumerate(tokens):
        target = x_ref.at[pl.ds(i * own_rows, own_rows)]
        token_copies.append(pltpu.make_async_copy(piece, target, x_sems.at[i]))
        token_copies[-1].start()
    for q in range(2):
        for j in range(chips):
            device = (chip ^ j) * 2 + (core ^ q)
            head_copies.append(
                pltpu.make_async_copy(
                    parts[q].at[j], w_ref.at[device], w_sems.at[q * chips + j]
                )
            )
            head_copies[-1].start()
    token_copies.append(pltpu.make_async_copy(wq_source, wq_ref, x_sems.at[devices]))
    token_copies[-1].start()
    factor_copies.append(pltpu.make_async_copy(up_source, up_ref, x_sems.at[devices + 1]))
    factor_copies[-1].start()
    for i, piece in enumerate(pieces):
        target = s_ref.at[pl.ds(spot_ref[2 + i], piece.shape[0])]
        factor_copies.append(pltpu.make_async_copy(piece, target, s_sems.at[i]))
        factor_copies[-1].start()
    last_copies = [
        pltpu.make_async_copy(wo_source, wo_ref, x_sems.at[devices + 2]),
        pltpu.make_async_copy(exo_source, exo_ref, x_sems.at[devices + 3]),
    ]
    for copy in last_copies:
        copy.start()
    factors = s_ref.shape[0] * s_ref.shape[1]
    gain = gain_ref[...].astype(F32)
    qg = qg_ref[...].astype(F32)
    kg = kg_ref[...].astype(F32)

    for copy in token_copies + head_copies:
        copy.wait()

    def project(i, carry):
        here = pl.ds(pl.multiple_of(i * block, block), block)
        x = rms(x_ref[here, :].astype(F32), gain).astype(BF16)
        x_ref[here, :] = x
        qf_ref[here, :] = dot(x, wq_ref[...])
        kvf_ref[here, :] = dot_nt(x, w_ref[...].reshape(devices * cols, width))
        return carry

    loop(blocks, project, 0)

    for copy in factor_copies:
        copy.wait()

    def turned(v, gain, here):
        v = rms(v, gain)
        return v * cos_ref[here, :] + pltpu.roll(v, head // 2, 1) * sin_ref[here, :]

    def adapt(i, carry):
        here = pl.ds(pl.multiple_of(i * block, block), block)
        low = dot_nt(x_ref[here, :], s_ref[...].reshape(factors, width))
        low = jnp.where(meta_ref[here, 0:1] == colslot_ref[...], low, 0.0).astype(BF16)
        delta = ADAPTER_FACTOR * dot(low, up_ref[...])
        q = qf_ref[here, :] + delta[:, :query_cols]
        kv = (kvf_ref[here, :] + delta[:, query_cols:]).astype(BF16)
        for h in range(heads):
            cut = slice(h * head, (h + 1) * head)
            q_ref[here, cut] = turned(q[:, cut], qg, here).astype(BF16)
        kv_ref[here, :head] = turned(kv[:, :head].astype(F32), kg, here).astype(BF16)
        kv_ref[here, head:] = kv[:, head:]
        return carry

    loop(blocks, adapt, 0)

    for copy in last_copies:
        copy.wait()

    def attend(target, offset):
        def one(i, carry):
            there = pl.ds(pl.multiple_of(i * block, block), block)
            here = pl.ds(pl.multiple_of(offset + i * block, block), block)
            allowed = (row_ref[1:2, :] <= meta_ref[here, 2:3]) & (
                row_ref[0:1, :] == meta_ref[here, 1:2]
            )
            heads_mixed = []
            for h in range(heads):
                cut = slice(h * head, (h + 1) * head)
                s = dot_nt(q_ref[here, cut], kv_ref[:, :head]) * scale
                raised = jnp.where(allowed, jnp.exp(s), 0.0)
                mixed = dot(raised.astype(BF16), kv_ref[:, head:])
                mixed = mixed / jnp.sum(raised, axis=1, keepdims=True)
                heads_mixed.append(mixed.astype(BF16))
            mixed = jnp.concatenate(heads_mixed, axis=1)
            low = dot_nt(mixed, sho_ref[...])
            low = jnp.where(meta_ref[here, 0:1] == oslot_ref[...], low, 0.0).astype(BF16)
            step = min(512, width)
            for c in range(0, width, step):
                cut = slice(c, c + step)
                term = dot(mixed, wo_ref[:, cut]) + ADAPTER_FACTOR * dot(low, exo_ref[:, cut])
                target[there, cut] = term.astype(BF16)
            return carry

        loop(blocks // 2, one, 0)

    attend(part_ref, rows // 2)
    attend(own_ref, 0)


def attention(spots, tokens, weights, meta, pieces, parts, adapters):
    gain, wq, up, qg, kg, sho, wo, exo = weights
    own_rows, width = tokens[0].shape
    rows = own_rows * len(tokens)
    chips, cols, _ = parts[0].shape
    query_cols = wq.shape[1]
    head = qg.shape[1]
    ranks = pieces[0].shape[1]
    half = jax.ShapeDtypeStruct((rows // 2, width), BF16)
    flops = 2 * rows * (width * (adapters * ranks + 2 * query_cols + 2 * head) + rows * query_cols)
    return pl.pallas_call(
        functools.partial(attention_kernel, len(tokens), len(pieces), len(parts)),
        out_shape=(half, half, jax.ShapeDtypeStruct((rows, 2 * head), BF16)),
        in_specs=[SMEM] + [VMEM] * 10 + [ANY] * (4 + len(tokens) + len(pieces) + len(parts)),
        out_specs=(VMEM, VMEM, VMEM),
        scratch_shapes=[
            pltpu.VMEM(wq.shape, BF16),
            pltpu.VMEM(up.shape, BF16),
            pltpu.VMEM(wo.shape, BF16),
            pltpu.VMEM(exo.shape, BF16),
            pltpu.VMEM((rows, width), BF16),
            pltpu.VMEM((adapters, ranks, width), BF16),
            pltpu.VMEM((2 * chips, cols, width), BF16),
            pltpu.VMEM((rows, query_cols), F32),
            pltpu.VMEM((rows, 2 * head), F32),
            pltpu.VMEM((rows, query_cols), BF16),
            pltpu.SemaphoreType.DMA((2 * chips + 4,)),
            pltpu.SemaphoreType.DMA((len(pieces),)),
            pltpu.SemaphoreType.DMA((2 * chips,)),
        ],
        compiler_params=pltpu.CompilerParams(vmem_limit_bytes=60 * MIB),
        cost_estimate=pl.CostEstimate(
            flops=flops, bytes_accessed=16 * MIB, transcendentals=rows * rows
        ),
        name="attention",
    )(spots, gain, *meta, qg, kg, sho, wq, up, wo, exo, *tokens, *pieces, *parts)


def pages_kernel(first_ref, length_ref, page_ref, entries_ref, out_ref):
    columns, extent = entries_ref.shape
    rows = extent - PAGE
    window = 2 * PAGE
    gap = lax.broadcasted_iota(jnp.int32, (window, PAGE), 0) - lax.broadcasted_iota(
        jnp.int32, (window, PAGE), 1
    )
    lane = lax.broadcasted_iota(jnp.int32, (columns, PAGE), 1)

    def one(n, carry):
        length = length_ref[n]
        page = page_ref[n]

        @pl.when(length > 0)
        def _():
            first = jnp.minimum(first_ref[n], rows - 1)
            base = pl.multiple_of(first // PAGE * PAGE, PAGE)
            pick = (gap == first - base).astype(F32).astype(BF16)
            moved = dot(entries_ref[:, pl.ds(base, window)], pick)
            out_ref[page] = jnp.where(lane < length, moved, 0.0).astype(BF16)

        @pl.when(length <= 0)
        def _():
            out_ref[page] = jnp.zeros((columns, PAGE), BF16)

        return carry

    lax.fori_loop(0, page_ref.shape[0], one, 0)


def fill_pages(first, length, page, entries):
    rows, columns = entries.shape
    count = page.shape[0]
    turned = jnp.pad(entries.T, ((0, 0), (0, PAGE)))
    return pl.pallas_call(
        pages_kernel,
        out_shape=jax.ShapeDtypeStruct((count, columns, PAGE), BF16),
        in_specs=[SMEM, SMEM, SMEM, VMEM],
        out_specs=VMEM,
        compiler_params=pltpu.CompilerParams(vmem_limit_bytes=32 * MIB),
        cost_estimate=pl.CostEstimate(
            flops=count * columns * PAGE * PAGE * 16, bytes_accessed=4 * MIB, transcendentals=0
        ),
        name="fill_pages",
    )(first, length, page, turned)


def start_all(copies):
    for copy in copies:
        copy.start()
    return copies


def wait_all(copies):
    for copy in copies:
        copy.wait()


def token_copies(pieces, x_ref, sems):
    rows = pieces[0].shape[0]
    return [
        pltpu.make_async_copy(piece, x_ref.at[pl.ds(i * rows, rows)], sems.at[i])
        for i, piece in enumerate(pieces)
    ]


def pick_rows(slot_t_ref, x_ref, rows_ref, pair, room, capacity):
    experts, total = slot_t_ref.shape
    width = x_ref.shape[1]
    step = min(512, width)
    line = lax.broadcasted_iota(jnp.int32, (room, pair), 0)
    for b in range(total // pair):
        there = slice(b * pair, (b + 1) * pair)
        pick = jnp.concatenate(
            [
                (slot_t_ref[n : n + 1, there] == line + b * room).astype(F32).astype(BF16)
                for n in range(experts)
            ],
            axis=0,
        )
        for c in range(0, width, step):
            cut = slice(c, c + step)
            got = dot(pick, x_ref[there, cut]).astype(BF16)
            for n in range(experts):
                begin = n * capacity + b * room
                rows_ref[begin : begin + room, cut] = got[n * room : (n + 1) * room]


def combine(slot_ref, weight_ref, y_ref, own_ref, part_ref, pair, room, capacity):
    total, experts = slot_ref.shape
    width = y_ref.shape[1]
    step = min(512, width)
    half = total // 2
    line = lax.broadcasted_iota(jnp.int32, (pair, experts * room), 1)
    for b in range(total // pair):
        here = slice(b * pair, (b + 1) * pair)
        spread = jnp.zeros((pair, experts * room), F32)
        for n in range(experts):
            place = slot_ref[here, n : n + 1] + (n - b) * room
            spread = jnp.where(place == line, weight_ref[here, n : n + 1], spread)
        spread = spread.astype(BF16)
        target, first = (own_ref, b * pair) if b * pair < half else (part_ref, b * pair - half)
        for c in range(0, width, step):
            cut = slice(c, c + step)
            begins = [n * capacity + b * room for n in range(experts)]
            y = jnp.concatenate([y_ref[begin : begin + room, cut] for begin in begins], axis=0)
            target[first : first + pair, cut] = dot(spread, y).astype(BF16)


def experts_kernel(blocks, capacity, slot_ref, slot_t_ref, weight_ref, *refs):
    pieces, refs = refs[:blocks], refs[blocks:]
    gate_ref, up_ref, down_ref, own_ref, part_ref = refs[:5]
    x_ref, rows_ref, y_ref, gate_buf, up_buf, down_buf, x_sems, w_sems = refs[5:]
    experts = slot_ref.shape[1]
    slots = gate_buf.shape[0]
    streams = ((gate_ref, gate_buf), (up_ref, up_buf), (down_ref, down_buf))

    def copy(k, e, s):
        source, buffer = streams[k]
        return pltpu.make_async_copy(source.at[e], buffer.at[s], w_sems.at[k, s])

    tokens = start_all(token_copies(pieces, x_ref, x_sems))
    for e in range(min(slots, experts)):
        for k in range(3):
            copy(k, e, e).start()
    wait_all(tokens)
    pair = 2 * x_ref.shape[0] // blocks
    pick_rows(slot_t_ref, x_ref, rows_ref, pair, 2 * CAP_DEV, capacity)

    def one(e, carry):
        s = lax.rem(e, slots)
        here = pl.ds(pl.multiple_of(e * capacity, capacity), capacity)
        x = rows_ref[here, :]
        copy(0, e, s).wait()
        gate = dot_nt(x, gate_buf[s])
        copy(1, e, s).wait()
        up = dot_nt(x, up_buf[s])
        hidden = (gate / (1.0 + jnp.exp(-gate)) * up).astype(BF16)
        copy(2, e, s).wait()
        y_ref[here, :] = dot(hidden, down_buf[s]).astype(BF16)

        @pl.when(e + slots < experts)
        def _():
            for k in range(3):
                copy(k, e + slots, s).start()

        return carry

    lax.fori_loop(0, experts, one, 0)
    combine(slot_ref, weight_ref, y_ref, own_ref, part_ref, pair, 2 * CAP_DEV, capacity)


def expert_layer(slot, slot_t, weight, pieces, gate, up, down, capacity):
    experts, hidden, width = gate.shape
    own_rows = pieces[0].shape[0]
    total = own_rows * len(pieces)
    slots = min(3 if total <= 512 else 2, experts)
    half = jax.ShapeDtypeStruct((total // 2, width), BF16)
    return pl.pallas_call(
        functools.partial(experts_kernel, len(pieces), capacity),
        out_shape=(half, half),
        in_specs=[VMEM] * 3 + [ANY] * (3 + len(pieces)),
        out_specs=(VMEM, VMEM),
        scratch_shapes=[
            pltpu.VMEM((total, width), BF16),
            pltpu.VMEM((experts * capacity, width), BF16),
            pltpu.VMEM((experts * capacity, width), BF16),
            pltpu.VMEM((slots, hidden, width), BF16),
            pltpu.VMEM((slots, hidden, width), BF16),
            pltpu.VMEM((slots, hidden, width), BF16),
            pltpu.SemaphoreType.DMA((len(pieces),)),
            pltpu.SemaphoreType.DMA((3, slots)),
        ],
        compiler_params=pltpu.CompilerParams(vmem_limit_bytes=60 * MIB),
        cost_estimate=pl.CostEstimate(
            flops=6 * experts * capacity * hidden * width,
            bytes_accessed=6 * experts * hidden * width,
            transcendentals=experts * capacity * hidden,
        ),
        name="experts",
    )(slot, slot_t, weight, *pieces, gate, up, down)


def other_core(value, parts):
    return lax.ppermute(value, "tensor", [(i, i ^ 1) for i in range(parts)])


def swap_chips(value, parts, by):
    return lax.ppermute(value, "tensor", [(i, i ^ (2 * by)) for i in range(parts)])


def swap_holder(value, holders, by):
    return lax.ppermute(value, "dp", [(i, i ^ by) for i in range(holders)])


def gather_blocks(own, parts, between=lambda blocks: blocks):
    chips = parts // 2
    blocks = {0: own}
    bit = chips // 2
    while bit:
        for i, block in list(blocks.items()):
            if i ^ bit not in blocks:
                blocks[i ^ bit] = swap_chips(block, parts, bit)
        if bit == chips // 2:
            if 1 not in blocks:
                blocks[1] = swap_chips(own, parts, 1)
            blocks = between(blocks)
        bit //= 2
    mine = [blocks[i] for i in range(chips)]
    return mine + [other_core(block, parts) for block in mine]


def scatter_terms(own, part, parts):
    chips = parts // 2
    sums = pair_sum(hold(own), other_core(part, parts), chips)
    halves = []
    for k in range(2):
        terms = {j: [sums[2 * j + k]] for j in range(chips)}
        bit = 1
        while bit < chips:
            for j in sorted((j for j in terms if j & bit), reverse=True):
                sent = terms.pop(j)
                if len(sent) > 1:
                    sent = [sum(term.astype(F32) for term in sent).astype(BF16)]
                terms[j ^ bit].append(swap_chips(sent[0], parts, bit))
            bit *= 2
        halves.append(terms[0])
    return halves


def from_here(rows, chip, core, chips):
    split = rows.reshape((chips, 2, -1) + rows.shape[1:])
    split = jnp.where(core == 0, split, split[:, ::-1])
    bit = 1
    while bit < chips:
        pairs = split.reshape((chips // (2 * bit), 2, bit) + split.shape[1:])
        split = jnp.where((chip & bit) == 0, pairs, pairs[:, ::-1]).reshape(split.shape)
        bit *= 2
    return split


def to_device(rows, chip, core, chips):
    return jnp.swapaxes(from_here(rows, chip, core, chips), 0, 1).reshape(rows.shape)


def to_group(rows, chip, core, chips):
    split = jnp.swapaxes(rows.reshape((2, chips, -1) + rows.shape[1:]), 0, 1)
    return from_here(split.reshape(rows.shape), chip, core, chips).reshape(rows.shape)


def local(
    tokens,
    attn_gain,
    moe_gain,
    q_gain,
    k_gain,
    query_weight,
    w_kv,
    w_o,
    w_gate,
    w_up,
    w_down,
    shrink_qkv,
    shrink_o,
    query_up_factors,
    key_value_up_factors,
    expand_o,
    lengths,
    groups,
    adapter_of_request,
    adapter_slot,
    page_table,
    expert_ids,
    expert_gates,
):
    parts = lax.axis_size("tensor")
    place = lax.axis_index("tensor")
    holders = lax.axis_size("dp")
    holder = lax.axis_index("dp")
    chips, chip, core = parts // 2, place // 2, place % 2
    own_rows, width = tokens.shape
    total = own_rows * parts
    head_length = q_gain.shape[0]
    adapters, rank, kv_width = key_value_up_factors.shape
    kv_heads = kv_width // (2 * head_length)
    held, ranks = shrink_qkv.shape[:2]
    head = place * kv_heads // parts
    query_cols = query_weight.shape[1]
    experts = w_gate.shape[0]

    line = jnp.arange(total, dtype=jnp.int32)
    side, number = line // (total // 2), line // own_rows % chips
    position = ((number ^ chip) * 2 + (side ^ core)) * own_rows + line % own_rows
    length_row, group_row, adapter_row = lengths[0], groups[0], adapter_of_request[0]
    ends = jnp.cumsum(length_row)
    starts = ends - length_row
    request = jnp.sum((ends[None, :] <= position[:, None]).astype(jnp.int32), axis=1)
    same = group_row[:, None] == group_row[None, :]
    group_first = jnp.min(jnp.where(same, starts[None, :], total), axis=1)
    slot_of_request = lookup(adapter_row, adapter_slot)
    group = lookup(request, group_row)
    rope_pos = position - lookup(request, group_first)
    slot = lookup(request, slot_of_request)
    meta_col = jnp.stack([slot, group, position], axis=1)
    meta_row = jnp.stack([group, position], axis=0)
    freq = jnp.exp(
        -jnp.arange(head_length // 2, dtype=F32) * (2.0 * math.log(ROPE_BASE) / head_length)
    )
    angle = rope_pos.astype(F32)[:, None] * freq[None, :]
    cosine, sine = jnp.cos(angle), jnp.sin(angle)
    cosine = jnp.concatenate([cosine, cosine], axis=1)
    sine = jnp.concatenate([-sine, sine], axis=1)
    colslot = (jnp.arange(adapters * ranks, dtype=jnp.int32) // ranks)[None, :]
    oslot = (jnp.arange(adapters * rank, dtype=jnp.int32) // rank)[None, :]

    up_kv = lax.dynamic_index_in_dim(
        key_value_up_factors.reshape(adapters, rank, kv_heads, 2, head_length), head, 2, keepdims=False
    )
    up = jnp.concatenate(
        [
            jnp.pad(query_up_factors, ((0, 0), (0, 2 * rank), (0, 0))),
            jnp.pad(up_kv[:, :, 0], ((0, 0), (rank, rank), (0, 0))),
            jnp.pad(up_kv[:, :, 1], ((0, 0), (2 * rank, 0), (0, 0))),
        ],
        axis=2,
    ).reshape(adapters * ranks, query_cols + 2 * head_length)

    weights = (
        attn_gain.reshape(1, -1),
        query_weight,
        up,
        q_gain.reshape(1, -1),
        k_gain.reshape(1, -1),
        shrink_o.reshape(adapters * rank, query_cols),
        w_o,
        expand_o.reshape(adapters * rank, width),
    )
    meta = (meta_col, meta_row, colslot, oslot, cosine, sine)
    half = held // 2
    half_own = lax.dynamic_slice_in_dim(shrink_qkv, core * half, half, 0)
    halves = [swap_holder(half_own, holders, r) for r in range(1, holders)]
    spots = [chip, core, holder * held]
    for r in range(1, holders):
        begin = (holder ^ r) * held
        spots += [begin + core * half, begin + (1 - core) * half]
    spots = jnp.stack(spots).astype(jnp.int32)
    cuts = [
        lax.dynamic_index_in_dim(w_kv, 2 * (chip ^ j) * kv_heads // parts, 1, keepdims=False)
        for j in range(chips)
    ]

    def between(blocks):
        nonlocal cuts, weights, meta, spots
        blocks, halves[:2], cuts, weights, meta, spots = lax.optimization_barrier(
            (blocks, halves[:2], cuts, weights, meta, spots)
        )
        return blocks

    gathered = gather_blocks(tokens, parts, between)
    mine = [cuts[0]] + [swap_chips(cuts[j], parts, j) for j in range(1, chips)]
    mine = jnp.stack(mine)
    head_parts = [mine, other_core(mine, parts)]
    pieces = [shrink_qkv]
    for got in halves:
        pieces += [got, other_core(got, parts)]
    own, part, entries = attention(
        spots,
        gathered,
        weights,
        meta,
        pieces,
        head_parts,
        adapters,
    )
    left, right = scatter_terms(own, part, parts)

    attn_own, moe_own = residual_norm(tokens, moe_gain, left, right)

    moe_own, entries, starts, length_row, page_table, expert_ids, expert_gates = (
        lax.optimization_barrier(
            (moe_own, entries, starts, length_row, page_table, expert_ids, expert_gates)
        )
    )

    capacity = CAP_DEV * parts
    ids = to_device(expert_ids, chip, core, chips)
    gates = to_device(expert_gates, chip, core, chips)
    share = gates / jnp.sum(gates, axis=1, keepdims=True)
    own_experts = place * experts + jnp.arange(experts, dtype=jnp.int32)
    chosen = ids[:, :, None] == own_experts[None, None, :]
    hit = jnp.any(chosen, axis=1)
    weight = jnp.sum(jnp.where(chosen, share[:, :, None], 0.0), axis=1)
    block = line // own_rows
    earlier = (line[:, None] > line[None, :]) & (block[:, None] == block[None, :])
    before = dot(earlier.astype(BF16), hit.astype(BF16)).astype(jnp.int32)
    slot_in = jnp.where(hit, block[:, None] * CAP_DEV + before, -(1 << 20))

    slot_t = slot_in.T

    def tables_first(blocks):
        nonlocal slot_in, slot_t, weight
        blocks, slot_in, slot_t, weight = lax.optimization_barrier(
            (blocks, slot_in, slot_t, weight)
        )
        return blocks

    gathered = gather_blocks(moe_own, parts, tables_first)
    own, part = expert_layer(slot_in, slot_t, weight, gathered, w_gate, w_up, w_down, capacity)
    left, right = scatter_terms(own, part, parts)

    local_cols = kv_width // parts
    kept = lax.dynamic_slice_in_dim(
        entries, place * local_cols - head * 2 * head_length, local_cols, 1
    )
    entries_in, left[1] = lax.optimization_barrier((kept, left[1]))
    page_row = page_table[0]
    per_request = page_row.shape[0] // length_row.shape[0]
    offset = PAGE * jnp.arange(per_request, dtype=jnp.int32)[None, :]
    page_first = (starts[:, None] + offset).reshape(-1)
    page_length = jnp.clip(length_row[:, None] - offset, 0, PAGE).reshape(-1)
    kv_pages = fill_pages(page_first, page_length, page_row, to_group(entries_in, chip, core, chips))
    left[0], kv_pages = lax.optimization_barrier((left[0], kv_pages))
    moe_total = total_rows(left, right)
    return (attn_own, moe_total, kv_pages)


def solution(mesh):
    placed = (
        P(("dp", "tensor"), None),
        P(),
        P(),
        P(),
        P(),
        P(None, "tensor"),
        P("tensor", None, None),
        P("tensor", None),
        P("tensor", None, None),
        P("tensor", None, None),
        P("tensor", None, None),
        P("dp", None, None),
        P(None, None, "tensor"),
        P(None, None, "tensor"),
        P(),
        P(),
        P("dp", None),
        P("dp", None),
        P("dp", None),
        P(),
        P("dp", None),
        P("dp", None),
        P("dp", None),
    )
    return jax.shard_map(
        local,
        mesh=mesh,
        in_specs=placed,
        out_specs=(P(("dp", "tensor"), None), P(("dp", "tensor"), None), P("dp", "tensor", None)),
        check_vma=False,
    )
```

```python
import functools
import math

import jax
import jax.numpy as jnp
from jax import lax
from jax.experimental import pallas as pl
from jax.experimental.pallas import tpu as pltpu
from jax.sharding import PartitionSpec as P

PAGE = 128
CAP_DEV = 16
NORM_EPS = 1e-06
ROPE_BASE = 1000000.0
ADAPTER_FACTOR = 0.5
MIB = 1 << 20
BF16 = jnp.bfloat16
F32 = jnp.float32
VMEM = pl.BlockSpec(memory_space=pltpu.VMEM)
SMEM = pl.BlockSpec(memory_space=pltpu.SMEM)
ANY = pl.BlockSpec(memory_space=pl.ANY)
HBM = pl.BlockSpec(memory_space=pltpu.HBM)


def dot(a, b):
    return jnp.dot(a, b, preferred_element_type=F32)


def dot_nt(a, b):
    return lax.dot_general(a, b, (((1,), (1,)), ((), ())), preferred_element_type=F32)


def lookup(index_value, table):
    match = index_value[:, None] == jnp.arange(table.shape[0], dtype=jnp.int32)[None, :]
    return jnp.sum(jnp.where(match, table[None, :], 0), axis=1)


def loop(count, body, carry):
    if count <= 2:
        for i in range(count):
            carry = body(i, carry)
        return carry
    return lax.fori_loop(0, count, body, carry)


def rms(v, gain):
    return v * lax.rsqrt(jnp.mean(v * v, axis=-1, keepdims=True) + NORM_EPS) * gain


def total_of(parts):
    total = parts[0][...].astype(F32)
    for part in parts[1:]:
        total = total + part[...].astype(F32)
    return total


def residual_kernel(count, x_ref, gain_ref, *refs):
    attn_ref, out_ref = refs[-2:]
    total = jnp.concatenate([total_of(refs[:count]), total_of(refs[count:-2])], axis=1)
    attn_ref[...] = total.astype(BF16)
    out_ref[...] = rms(x_ref[...].astype(F32) + total, gain_ref[...].astype(F32)).astype(BF16)


def residual_norm(x, gain, left, right):
    shape = jax.ShapeDtypeStruct(x.shape, BF16)
    return pl.pallas_call(
        functools.partial(residual_kernel, len(left)),
        out_shape=(shape, shape),
        in_specs=[VMEM] * (2 + len(left) + len(right)),
        out_specs=(VMEM, VMEM),
        name="residual_norm",
    )(x, gain.reshape(1, -1), *left, *right)


def total_kernel(count, *refs):
    out_ref = refs[-1]
    half = out_ref.shape[1] // 2
    out_ref[:, :half] = total_of(refs[:count]).astype(BF16)
    out_ref[:, half:] = total_of(refs[count:-1]).astype(BF16)


def total_rows(left, right):
    rows, half = left[0].shape
    return pl.pallas_call(
        functools.partial(total_kernel, len(left)),
        out_shape=jax.ShapeDtypeStruct((rows, 2 * half), BF16),
        in_specs=[VMEM] * (len(left) + len(right)),
        out_specs=VMEM,
        name="total_rows",
    )(*left, *right)


def hold_kernel(source_ref, out_ref, sem):
    copy = pltpu.make_async_copy(source_ref, out_ref, sem)
    copy.start()
    copy.wait()


def hold(rows):
    return pl.pallas_call(
        hold_kernel,
        out_shape=pltpu.VMEM(rows.shape, BF16),
        in_specs=[HBM],
        out_specs=VMEM,
        scratch_shapes=[pltpu.SemaphoreType.DMA],
        compiler_params=pltpu.CompilerParams(vmem_limit_bytes=4 * MIB),
        name="hold",
    )(pltpu.with_memory_space_constraint(rows, pltpu.HBM))


def pair_kernel(a_ref, b_ref, *outs):
    rows, half = outs[0].shape
    for i in range(len(outs) // 2):
        here = slice(i * rows, (i + 1) * rows)
        total = (a_ref[here, :].astype(F32) + b_ref[here, :].astype(F32)).astype(BF16)
        outs[2 * i][...] = total[:, :half]
        outs[2 * i + 1][...] = total[:, half:]


def pair_sum(a, b, count):
    shape = jax.ShapeDtypeStruct((a.shape[0] // count, a.shape[1] // 2), BF16)
    return pl.pallas_call(
        pair_kernel,
        out_shape=(shape,) * (2 * count),
        in_specs=[VMEM, VMEM],
        out_specs=(VMEM,) * (2 * count),
        compiler_params=pltpu.CompilerParams(vmem_limit_bytes=24 * MIB),
        name="pair_sum",
    )(a, b)


def attention_kernel(
    token_blocks,
    factor_blocks,
    head_blocks,
    spot_ref,
    gain_ref,
    row_ref,
    colslot_ref,
    oslot_ref,
    cos_ref,
    sin_ref,
    qg_ref,
    kg_ref,
    sho_ref,
    *refs,
):
    (wq_source, up_source, wo_source, exo_source), refs = refs[:4], refs[4:]
    tokens, refs = refs[:token_blocks], refs[token_blocks:]
    pieces, refs = refs[:factor_blocks], refs[factor_blocks:]
    parts, refs = refs[:head_blocks], refs[head_blocks:]
    own_ref, part_ref, kv_ref = refs[:3]
    wq_ref, up_ref, wo_ref, exo_ref, x_ref, s_ref, w_ref, qf_ref, kvf_ref, q_ref = refs[3:13]
    meta_ref, x_sems, s_sems, w_sems = refs[13:]
    meta_ref[...] = row_ref[...].T
    rows, width = x_ref.shape
    query_cols = wq_ref.shape[1]
    head = qg_ref.shape[1]
    heads = query_cols // head
    block = min(256, rows // 2)
    blocks = rows // block
    scale = head**-0.5
    devices, cols, _ = w_ref.shape
    chips = devices // 2
    own_rows = rows // devices
    chip, core = spot_ref[0], spot_ref[1]
    token_copies, factor_copies, head_copies = [], [], []
    for i, piece in enumerate(tokens):
        target = x_ref.at[pl.ds(i * own_rows, own_rows)]
        token_copies.append(pltpu.make_async_copy(piece, target, x_sems.at[i]))
        token_copies[-1].start()
    for q in range(2):
        for j in range(chips):
            device = (chip ^ j) * 2 + (core ^ q)
            head_copies.append(
                pltpu.make_async_copy(
                    parts[q].at[j], w_ref.at[device], w_sems.at[q * chips + j]
                )
            )
            head_copies[-1].start()
    token_copies.append(pltpu.make_async_copy(wq_source, wq_ref, x_sems.at[devices]))
    token_copies[-1].start()
    factor_copies.append(pltpu.make_async_copy(up_source, up_ref, x_sems.at[devices + 1]))
    factor_copies[-1].start()
    for i, piece in enumerate(pieces):
        target = s_ref.at[pl.ds(spot_ref[2 + i], piece.shape[0])]
        factor_copies.append(pltpu.make_async_copy(piece, target, s_sems.at[i]))
        factor_copies[-1].start()
    last_copies = [
        pltpu.make_async_copy(wo_source, wo_ref, x_sems.at[devices + 2]),
        pltpu.make_async_copy(exo_source, exo_ref, x_sems.at[devices + 3]),
    ]
    for copy in last_copies:
        copy.start()
    factors = s_ref.shape[0] * s_ref.shape[1]
    gain = gain_ref[...].astype(F32)
    qg = qg_ref[...].astype(F32)
    kg = kg_ref[...].astype(F32)

    for copy in token_copies + head_copies:
        copy.wait()

    def project(i, carry):
        here = pl.ds(pl.multiple_of(i * block, block), block)
        x = rms(x_ref[here, :].astype(F32), gain).astype(BF16)
        x_ref[here, :] = x
        qf_ref[here, :] = dot(x, wq_ref[...])
        kvf_ref[here, :] = dot_nt(x, w_ref[...].reshape(devices * cols, width))
        return carry

    loop(blocks, project, 0)

    for copy in factor_copies:
        copy.wait()

    def turned(v, gain, here):
        v = rms(v, gain)
        return v * cos_ref[here, :] + pltpu.roll(v, head // 2, 1) * sin_ref[here, :]

    def adapt(i, carry):
        here = pl.ds(pl.multiple_of(i * block, block), block)
        low = dot_nt(x_ref[here, :], s_ref[...].reshape(factors, width))
        low = jnp.where(meta_ref[here, 0:1] == colslot_ref[...], low, 0.0).astype(BF16)
        delta = ADAPTER_FACTOR * dot(low, up_ref[...])
        q = qf_ref[here, :] + delta[:, :query_cols]
        kv = (kvf_ref[here, :] + delta[:, query_cols:]).astype(BF16)
        for h in range(heads):
            cut = slice(h * head, (h + 1) * head)
            q_ref[here, cut] = turned(q[:, cut], qg, here).astype(BF16)
        kv_ref[here, :head] = turned(kv[:, :head].astype(F32), kg, here).astype(BF16)
        kv_ref[here, head:] = kv[:, head:]
        return carry

    loop(blocks, adapt, 0)

    for copy in last_copies:
        copy.wait()

    def attend(target, offset):
        def one(i, carry):
            there = pl.ds(pl.multiple_of(i * block, block), block)
            here = pl.ds(pl.multiple_of(offset + i * block, block), block)
            allowed = (row_ref[2:3, :] <= meta_ref[here, 2:3]) & (
                row_ref[1:2, :] == meta_ref[here, 1:2]
            )
            heads_mixed = []
            for h in range(heads):
                cut = slice(h * head, (h + 1) * head)
                s = dot_nt(q_ref[here, cut], kv_ref[:, :head]) * scale
                raised = jnp.where(allowed, jnp.exp(s), 0.0)
                mixed = dot(raised.astype(BF16), kv_ref[:, head:])
                mixed = mixed / jnp.sum(raised, axis=1, keepdims=True)
                heads_mixed.append(mixed.astype(BF16))
            mixed = jnp.concatenate(heads_mixed, axis=1)
            low = dot_nt(mixed, sho_ref[...])
            low = jnp.where(meta_ref[here, 0:1] == oslot_ref[...], low, 0.0).astype(BF16)
            step = min(512, width)
            for c in range(0, width, step):
                cut = slice(c, c + step)
                term = dot(mixed, wo_ref[:, cut]) + ADAPTER_FACTOR * dot(low, exo_ref[:, cut])
                target[there, cut] = term.astype(BF16)
            return carry

        loop(blocks // 2, one, 0)

    attend(part_ref, rows // 2)
    attend(own_ref, 0)


def attention(spots, tokens, weights, meta, pieces, parts, adapters):
    gain, wq, up, qg, kg, sho, wo, exo = weights
    own_rows, width = tokens[0].shape
    rows = own_rows * len(tokens)
    chips, cols, _ = parts[0].shape
    query_cols = wq.shape[1]
    head = qg.shape[1]
    ranks = pieces[0].shape[1]
    half = jax.ShapeDtypeStruct((rows // 2, width), BF16)
    flops = 2 * rows * (width * (adapters * ranks + 2 * query_cols + 2 * head) + rows * query_cols)
    return pl.pallas_call(
        functools.partial(attention_kernel, len(tokens), len(pieces), len(parts)),
        out_shape=(half, half, jax.ShapeDtypeStruct((rows, 2 * head), BF16)),
        in_specs=[SMEM] + [VMEM] * 9 + [ANY] * (4 + len(tokens) + len(pieces) + len(parts)),
        out_specs=(VMEM, VMEM, VMEM),
        scratch_shapes=[
            pltpu.VMEM(wq.shape, BF16),
            pltpu.VMEM(up.shape, BF16),
            pltpu.VMEM(wo.shape, BF16),
            pltpu.VMEM(exo.shape, BF16),
            pltpu.VMEM((rows, width), BF16),
            pltpu.VMEM((adapters, ranks, width), BF16),
            pltpu.VMEM((2 * chips, cols, width), BF16),
            pltpu.VMEM((rows, query_cols), F32),
            pltpu.VMEM((rows, 2 * head), F32),
            pltpu.VMEM((rows, query_cols), BF16),
            pltpu.VMEM((rows, meta[0].shape[0]), F32),
            pltpu.SemaphoreType.DMA((2 * chips + 4,)),
            pltpu.SemaphoreType.DMA((len(pieces),)),
            pltpu.SemaphoreType.DMA((2 * chips,)),
        ],
        compiler_params=pltpu.CompilerParams(vmem_limit_bytes=60 * MIB),
        cost_estimate=pl.CostEstimate(
            flops=flops, bytes_accessed=16 * MIB, transcendentals=rows * rows
        ),
        name="attention",
    )(spots, gain, *meta, qg, kg, sho, wq, up, wo, exo, *tokens, *pieces, *parts)


def pages_kernel(first_ref, length_ref, page_ref, entries_ref, out_ref):
    columns, extent = entries_ref.shape
    rows = extent - PAGE
    window = 2 * PAGE
    gap = lax.broadcasted_iota(jnp.int32, (window, PAGE), 0) - lax.broadcasted_iota(
        jnp.int32, (window, PAGE), 1
    )
    lane = lax.broadcasted_iota(jnp.int32, (columns, PAGE), 1)

    def one(n, carry):
        length = length_ref[n]
        page = page_ref[n]

        @pl.when(length > 0)
        def _():
            first = jnp.minimum(first_ref[n], rows - 1)
            base = pl.multiple_of(first // PAGE * PAGE, PAGE)
            pick = (gap == first - base).astype(F32).astype(BF16)
            moved = dot(entries_ref[:, pl.ds(base, window)], pick)
            out_ref[page] = jnp.where(lane < length, moved, 0.0).astype(BF16)

        @pl.when(length <= 0)
        def _():
            out_ref[page] = jnp.zeros((columns, PAGE), BF16)

        return carry

    lax.fori_loop(0, page_ref.shape[0], one, 0)


def fill_pages(first, length, page, entries):
    rows, columns = entries.shape
    count = page.shape[0]
    turned = jnp.pad(entries.T, ((0, 0), (0, PAGE)))
    return pl.pallas_call(
        pages_kernel,
        out_shape=jax.ShapeDtypeStruct((count, columns, PAGE), BF16),
        in_specs=[SMEM, SMEM, SMEM, VMEM],
        out_specs=VMEM,
        compiler_params=pltpu.CompilerParams(vmem_limit_bytes=32 * MIB),
        cost_estimate=pl.CostEstimate(
            flops=count * columns * PAGE * PAGE * 16, bytes_accessed=4 * MIB, transcendentals=0
        ),
        name="fill_pages",
    )(first, length, page, turned)


def start_all(copies):
    for copy in copies:
        copy.start()
    return copies


def wait_all(copies):
    for copy in copies:
        copy.wait()


def token_copies(pieces, x_ref, sems):
    rows = pieces[0].shape[0]
    return [
        pltpu.make_async_copy(piece, x_ref.at[pl.ds(i * rows, rows)], sems.at[i])
        for i, piece in enumerate(pieces)
    ]


def pick_rows(route_ref, x_ref, rows_ref, experts, pair, room, capacity):
    total, width = x_ref.shape
    step = min(512, width)
    line = lax.broadcasted_iota(jnp.int32, (room, pair), 0).astype(F32)
    for b in range(total // pair):
        there = slice(b * pair, (b + 1) * pair)
        pick = jnp.concatenate(
            [
                (route_ref[n : n + 1, there] == line + b * room).astype(F32).astype(BF16)
                for n in range(experts)
            ],
            axis=0,
        )
        for c in range(0, width, step):
            cut = slice(c, c + step)
            got = dot(pick, x_ref[there, cut]).astype(BF16)
            for n in range(experts):
                begin = n * capacity + b * room
                rows_ref[begin : begin + room, cut] = got[n * room : (n + 1) * room]


def combine(turned_ref, y_ref, own_ref, part_ref, experts, pair, room, capacity):
    total, width = turned_ref.shape[0], y_ref.shape[1]
    step = min(512, width)
    half = total // 2
    line = lax.broadcasted_iota(jnp.int32, (pair, experts * room), 1).astype(F32)
    for b in range(total // pair):
        here = slice(b * pair, (b + 1) * pair)
        spread = jnp.zeros((pair, experts * room), F32)
        for n in range(experts):
            place = turned_ref[here, n : n + 1] + (n - b) * room
            share = turned_ref[here, experts + n : experts + n + 1]
            spread = jnp.where(place == line, share, spread)
        spread = spread.astype(BF16)
        target, first = (own_ref, b * pair) if b * pair < half else (part_ref, b * pair - half)
        for c in range(0, width, step):
            cut = slice(c, c + step)
            begins = [n * capacity + b * room for n in range(experts)]
            y = jnp.concatenate([y_ref[begin : begin + room, cut] for begin in begins], axis=0)
            target[first : first + pair, cut] = dot(spread, y).astype(BF16)


def experts_kernel(blocks, capacity, route_ref, *refs):
    pieces, refs = refs[:blocks], refs[blocks:]
    gate_ref, up_ref, down_ref, own_ref, part_ref = refs[:5]
    x_ref, rows_ref, y_ref, turned_ref, gate_buf, up_buf, down_buf, x_sems, w_sems = refs[5:]
    experts = rows_ref.shape[0] // capacity
    slots = gate_buf.shape[0]
    streams = ((gate_ref, gate_buf), (up_ref, up_buf), (down_ref, down_buf))

    def copy(k, e, s):
        source, buffer = streams[k]
        return pltpu.make_async_copy(source.at[e], buffer.at[s], w_sems.at[k, s])

    tokens = start_all(token_copies(pieces, x_ref, x_sems))
    for e in range(min(slots, experts)):
        for k in range(3):
            copy(k, e, e).start()
    turned_ref[...] = route_ref[...].T
    wait_all(tokens)
    pair = 2 * x_ref.shape[0] // blocks
    pick_rows(route_ref, x_ref, rows_ref, experts, pair, 2 * CAP_DEV, capacity)

    def one(e, carry):
        s = lax.rem(e, slots)
        here = pl.ds(pl.multiple_of(e * capacity, capacity), capacity)
        x = rows_ref[here, :]
        copy(0, e, s).wait()
        gate = dot_nt(x, gate_buf[s])
        copy(1, e, s).wait()
        up = dot_nt(x, up_buf[s])
        hidden = (gate / (1.0 + jnp.exp(-gate)) * up).astype(BF16)
        copy(2, e, s).wait()
        y_ref[here, :] = dot(hidden, down_buf[s]).astype(BF16)

        @pl.when(e + slots < experts)
        def _():
            for k in range(3):
                copy(k, e + slots, s).start()

        return carry

    lax.fori_loop(0, experts, one, 0)
    combine(turned_ref, y_ref, own_ref, part_ref, experts, pair, 2 * CAP_DEV, capacity)


def expert_layer(routes, pieces, gate, up, down, capacity):
    experts, hidden, width = gate.shape
    own_rows = pieces[0].shape[0]
    total = own_rows * len(pieces)
    slots = min(3 if total <= 512 else 2, experts)
    half = jax.ShapeDtypeStruct((total // 2, width), BF16)
    return pl.pallas_call(
        functools.partial(experts_kernel, len(pieces), capacity),
        out_shape=(half, half),
        in_specs=[VMEM] + [ANY] * (3 + len(pieces)),
        out_specs=(VMEM, VMEM),
        scratch_shapes=[
            pltpu.VMEM((total, width), BF16),
            pltpu.VMEM((experts * capacity, width), BF16),
            pltpu.VMEM((experts * capacity, width), BF16),
            pltpu.VMEM(routes.shape[::-1], F32),
            pltpu.VMEM((slots, hidden, width), BF16),
            pltpu.VMEM((slots, hidden, width), BF16),
            pltpu.VMEM((slots, hidden, width), BF16),
            pltpu.SemaphoreType.DMA((len(pieces),)),
            pltpu.SemaphoreType.DMA((3, slots)),
        ],
        compiler_params=pltpu.CompilerParams(vmem_limit_bytes=60 * MIB),
        cost_estimate=pl.CostEstimate(
            flops=6 * experts * capacity * hidden * width,
            bytes_accessed=6 * experts * hidden * width,
            transcendentals=experts * capacity * hidden,
        ),
        name="experts",
    )(routes, *pieces, gate, up, down)


def other_core(value, parts):
    return lax.ppermute(value, "tensor", [(i, i ^ 1) for i in range(parts)])


def swap_chips(value, parts, by):
    return lax.ppermute(value, "tensor", [(i, i ^ (2 * by)) for i in range(parts)])


def swap_holder(value, holders, by):
    return lax.ppermute(value, "dp", [(i, i ^ by) for i in range(holders)])


def gather_blocks(own, parts, between=lambda blocks: blocks):
    chips = parts // 2
    blocks = {0: own}
    bit = chips // 2
    while bit:
        for i, block in list(blocks.items()):
            if i ^ bit not in blocks:
                blocks[i ^ bit] = swap_chips(block, parts, bit)
        if bit == chips // 2:
            if 1 not in blocks:
                blocks[1] = swap_chips(own, parts, 1)
            blocks = between(blocks)
        bit //= 2
    mine = [blocks[i] for i in range(chips)]
    return mine + [other_core(block, parts) for block in mine]


def scatter_terms(own, part, parts):
    chips = parts // 2
    sums = pair_sum(hold(own), other_core(part, parts), chips)
    halves = []
    for k in range(2):
        terms = {j: [sums[2 * j + k]] for j in range(chips)}
        late, last, bit = [], None, 1
        while bit < chips:
            for j in sorted((j for j in terms if j & bit), reverse=True):
                sent = terms.pop(j)
                if len(sent) > 1:
                    sent = [sum(term.astype(F32) for term in sent).astype(BF16)]
                if j == bit and 2 * bit < chips:
                    late.append((bit, sent[0]))
                    continue
                last = sent[0]
                terms[j ^ bit].append(swap_chips(last, parts, bit))
            bit *= 2
        for bit, sent in late:
            sent, last = lax.optimization_barrier((sent, last))
            terms[0].append(swap_chips(sent, parts, bit))
        halves.append(terms[0])
    return halves


def from_here(rows, chip, core, chips):
    split = rows.reshape((chips, 2, -1) + rows.shape[1:])
    split = jnp.where(core == 0, split, split[:, ::-1])
    bit = 1
    while bit < chips:
        pairs = split.reshape((chips // (2 * bit), 2, bit) + split.shape[1:])
        split = jnp.where((chip & bit) == 0, pairs, pairs[:, ::-1]).reshape(split.shape)
        bit *= 2
    return split


def to_device(rows, chip, core, chips):
    return jnp.swapaxes(from_here(rows, chip, core, chips), 0, 1).reshape(rows.shape)


def to_group(rows, chip, core, chips):
    split = jnp.swapaxes(rows.reshape((2, chips, -1) + rows.shape[1:]), 0, 1)
    return from_here(split.reshape(rows.shape), chip, core, chips).reshape(rows.shape)


def local(
    tokens,
    attn_gain,
    moe_gain,
    q_gain,
    k_gain,
    query_weight,
    w_kv,
    w_o,
    w_gate,
    w_up,
    w_down,
    shrink_qkv,
    shrink_o,
    query_up_factors,
    key_value_up_factors,
    expand_o,
    lengths,
    groups,
    adapter_of_request,
    adapter_slot,
    page_table,
    expert_ids,
    expert_gates,
):
    parts = lax.axis_size("tensor")
    place = lax.axis_index("tensor")
    holders = lax.axis_size("dp")
    holder = lax.axis_index("dp")
    chips, chip, core = parts // 2, place // 2, place % 2
    own_rows, width = tokens.shape
    total = own_rows * parts
    head_length = q_gain.shape[0]
    adapters, rank, kv_width = key_value_up_factors.shape
    kv_heads = kv_width // (2 * head_length)
    held, ranks = shrink_qkv.shape[:2]
    head = place * kv_heads // parts
    query_cols = query_weight.shape[1]
    experts = w_gate.shape[0]

    line = jnp.arange(total, dtype=jnp.int32)
    side, number = line // (total // 2), line // own_rows % chips
    position = ((number ^ chip) * 2 + (side ^ core)) * own_rows + line % own_rows
    length_row, group_row, adapter_row = lengths[0], groups[0], adapter_of_request[0]
    ends = jnp.cumsum(length_row)
    starts = ends - length_row
    request = jnp.sum((ends[None, :] <= position[:, None]).astype(jnp.int32), axis=1)
    same = group_row[:, None] == group_row[None, :]
    group_first = jnp.min(jnp.where(same, starts[None, :], total), axis=1)
    slot_of_request = lookup(adapter_row, adapter_slot)
    group = lookup(request, group_row)
    rope_pos = position - lookup(request, group_first)
    slot = lookup(request, slot_of_request)
    meta_row = jnp.stack([slot, group, position] + [position] * 5, axis=0).astype(F32)
    freq = jnp.exp(
        -jnp.arange(head_length // 2, dtype=F32) * (2.0 * math.log(ROPE_BASE) / head_length)
    )
    angle = rope_pos.astype(F32)[:, None] * freq[None, :]
    cosine, sine = jnp.cos(angle), jnp.sin(angle)
    cosine = jnp.concatenate([cosine, cosine], axis=1)
    sine = jnp.concatenate([-sine, sine], axis=1)
    colslot = (jnp.arange(adapters * ranks, dtype=jnp.int32) // ranks)[None, :].astype(F32)
    oslot = (jnp.arange(adapters * rank, dtype=jnp.int32) // rank)[None, :].astype(F32)

    up_kv = lax.dynamic_index_in_dim(
        key_value_up_factors.reshape(adapters, rank, kv_heads, 2, head_length), head, 2, keepdims=False
    )
    up = jnp.concatenate(
        [
            jnp.pad(query_up_factors, ((0, 0), (0, 2 * rank), (0, 0))),
            jnp.pad(up_kv[:, :, 0], ((0, 0), (rank, rank), (0, 0))),
            jnp.pad(up_kv[:, :, 1], ((0, 0), (2 * rank, 0), (0, 0))),
        ],
        axis=2,
    ).reshape(adapters * ranks, query_cols + 2 * head_length)

    weights = (
        attn_gain.reshape(1, -1),
        query_weight,
        up,
        q_gain.reshape(1, -1),
        k_gain.reshape(1, -1),
        shrink_o.reshape(adapters * rank, query_cols),
        w_o,
        expand_o.reshape(adapters * rank, width),
    )
    meta = (meta_row, colslot, oslot, cosine, sine)
    half = held // 2
    half_own = lax.dynamic_slice_in_dim(shrink_qkv, core * half, half, 0)
    halves = [swap_holder(half_own, holders, r) for r in range(1, holders)]
    spots = [chip, core, holder * held]
    for r in range(1, holders):
        begin = (holder ^ r) * held
        spots += [begin + core * half, begin + (1 - core) * half]
    spots = jnp.stack(spots).astype(jnp.int32)
    cuts = [
        lax.dynamic_index_in_dim(w_kv, 2 * (chip ^ j) * kv_heads // parts, 1, keepdims=False)
        for j in range(chips)
    ]

    def between(blocks):
        nonlocal cuts, meta
        blocks, halves[:2], cuts, meta = lax.optimization_barrier(
            (blocks, halves[:2], cuts, meta)
        )
        return blocks

    gathered = gather_blocks(tokens, parts, between)
    mine = [cuts[0]] + [swap_chips(cuts[j], parts, j) for j in range(1, chips)]
    mine = jnp.stack(mine)
    mine, weights, spots = lax.optimization_barrier((mine, weights, spots))
    head_parts = [mine, other_core(mine, parts)]
    pieces = [shrink_qkv]
    for got in halves:
        pieces += [got, other_core(got, parts)]
    own, part, entries = attention(
        spots,
        gathered,
        weights,
        meta,
        pieces,
        head_parts,
        adapters,
    )
    left, right = scatter_terms(own, part, parts)

    attn_own, moe_own = residual_norm(tokens, moe_gain, left, right)

    moe_own, entries, starts, length_row, page_table, expert_ids, expert_gates = (
        lax.optimization_barrier(
            (moe_own, entries, starts, length_row, page_table, expert_ids, expert_gates)
        )
    )

    local_cols = kv_width // parts
    kept = lax.dynamic_slice_in_dim(
        entries, place * local_cols - head * 2 * head_length, local_cols, 1
    )
    page_row = page_table[0]
    per_request = page_row.shape[0] // length_row.shape[0]
    offset = PAGE * jnp.arange(per_request, dtype=jnp.int32)[None, :]
    page_first = (starts[:, None] + offset).reshape(-1)
    page_length = jnp.clip(length_row[:, None] - offset, 0, PAGE).reshape(-1)
    kv_pages = fill_pages(page_first, page_length, page_row, to_group(kept, chip, core, chips))

    capacity = CAP_DEV * parts
    ids = to_device(expert_ids, chip, core, chips)
    gates = to_device(expert_gates, chip, core, chips)
    share = gates / jnp.sum(gates, axis=1, keepdims=True)
    own_experts = place * experts + jnp.arange(experts, dtype=jnp.int32)
    chosen = ids[:, :, None] == own_experts[None, None, :]
    hit = jnp.any(chosen, axis=1)
    weight = jnp.sum(jnp.where(chosen, share[:, :, None], 0.0), axis=1)
    block = line // own_rows
    earlier = (line[:, None] > line[None, :]) & (block[:, None] == block[None, :])
    before = dot(earlier.astype(BF16), hit.astype(BF16)).astype(jnp.int32)
    slot_in = jnp.where(hit, block[:, None] * CAP_DEV + before, -(1 << 20))

    routes = jnp.concatenate([slot_in.astype(F32).T, weight.T], axis=0)
    routes = jnp.pad(routes, ((0, -routes.shape[0] % 8), (0, 0)))

    def tables_first(blocks):
        nonlocal routes, kv_pages
        blocks, routes, kv_pages = lax.optimization_barrier((blocks, routes, kv_pages))
        return blocks

    gathered = gather_blocks(moe_own, parts, tables_first)
    own, part = expert_layer(routes, gathered, w_gate, w_up, w_down, capacity)
    left, right = scatter_terms(own, part, parts)

    moe_total = total_rows(left, right)
    return (attn_own, moe_total, kv_pages)


def solution(mesh):
    placed = (
        P(("dp", "tensor"), None),
        P(),
        P(),
        P(),
        P(),
        P(None, "tensor"),
        P("tensor", None, None),
        P("tensor", None),
        P("tensor", None, None),
        P("tensor", None, None),
        P("tensor", None, None),
        P("dp", None, None),
        P(None, None, "tensor"),
        P(None, None, "tensor"),
        P(),
        P(),
        P("dp", None),
        P("dp", None),
        P("dp", None),
        P(),
        P("dp", None),
        P("dp", None),
        P("dp", None),
    )
    return jax.shard_map(
        local,
        mesh=mesh,
        in_specs=placed,
        out_specs=(P(("dp", "tensor"), None), P(("dp", "tensor"), None), P("dp", "tensor", None)),
        check_vma=False,
    )
```

```python
import functools
import math

import jax
import jax.numpy as jnp
from jax import lax
from jax.experimental import pallas as pl
from jax.experimental.pallas import tpu as pltpu
from jax.sharding import PartitionSpec as P

PAGE = 128
CAP_DEV = 16
NORM_EPS = 1e-06
ROPE_BASE = 1000000.0
ADAPTER_FACTOR = 0.5
MIB = 1 << 20
BF16 = jnp.bfloat16
F32 = jnp.float32
VMEM = pl.BlockSpec(memory_space=pltpu.VMEM)
SMEM = pl.BlockSpec(memory_space=pltpu.SMEM)
ANY = pl.BlockSpec(memory_space=pl.ANY)
HBM = pl.BlockSpec(memory_space=pltpu.HBM)


def dot(a, b):
    return jnp.dot(a, b, preferred_element_type=F32)


def dot_nt(a, b):
    return lax.dot_general(a, b, (((1,), (1,)), ((), ())), preferred_element_type=F32)


def lookup(index_value, table):
    match = index_value[:, None] == jnp.arange(table.shape[0], dtype=jnp.int32)[None, :]
    return jnp.sum(jnp.where(match, table[None, :], 0), axis=1)


def loop(count, body, carry):
    if count <= 2:
        for i in range(count):
            carry = body(i, carry)
        return carry
    return lax.fori_loop(0, count, body, carry)


def rms(v, gain):
    return v * lax.rsqrt(jnp.mean(v * v, axis=-1, keepdims=True) + NORM_EPS) * gain


def total_of(parts):
    total = parts[0][...].astype(F32)
    for part in parts[1:]:
        total = total + part[...].astype(F32)
    return total


def residual_kernel(count, x_ref, gain_ref, *refs):
    attn_ref, out_ref = refs[-2:]
    total = jnp.concatenate([total_of(refs[:count]), total_of(refs[count:-2])], axis=1)
    attn_ref[...] = total.astype(BF16)
    out_ref[...] = rms(x_ref[...].astype(F32) + total, gain_ref[...].astype(F32)).astype(BF16)


def residual_norm(x, gain, left, right):
    shape = jax.ShapeDtypeStruct(x.shape, BF16)
    return pl.pallas_call(
        functools.partial(residual_kernel, len(left)),
        out_shape=(shape, shape),
        in_specs=[VMEM] * (2 + len(left) + len(right)),
        out_specs=(VMEM, VMEM),
        name="residual_norm",
    )(x, gain.reshape(1, -1), *left, *right)


def total_kernel(count, *refs):
    out_ref = refs[-1]
    half = out_ref.shape[1] // 2
    out_ref[:, :half] = total_of(refs[:count]).astype(BF16)
    out_ref[:, half:] = total_of(refs[count:-1]).astype(BF16)


def total_rows(left, right):
    rows, half = left[0].shape
    return pl.pallas_call(
        functools.partial(total_kernel, len(left)),
        out_shape=jax.ShapeDtypeStruct((rows, 2 * half), BF16),
        in_specs=[VMEM] * (len(left) + len(right)),
        out_specs=VMEM,
        name="total_rows",
    )(*left, *right)


def hold_kernel(source_ref, out_ref, sem):
    copy = pltpu.make_async_copy(source_ref, out_ref, sem)
    copy.start()
    copy.wait()


def hold(rows):
    return pl.pallas_call(
        hold_kernel,
        out_shape=pltpu.VMEM(rows.shape, BF16),
        in_specs=[HBM],
        out_specs=VMEM,
        scratch_shapes=[pltpu.SemaphoreType.DMA],
        compiler_params=pltpu.CompilerParams(vmem_limit_bytes=4 * MIB),
        name="hold",
    )(pltpu.with_memory_space_constraint(rows, pltpu.HBM))


def pair_kernel(a_ref, b_ref, *outs):
    rows, half = outs[0].shape
    for i in range(len(outs) // 2):
        here = slice(i * rows, (i + 1) * rows)
        total = (a_ref[here, :].astype(F32) + b_ref[here, :].astype(F32)).astype(BF16)
        outs[2 * i][...] = total[:, :half]
        outs[2 * i + 1][...] = total[:, half:]


def pair_sum(a, b, count):
    shape = jax.ShapeDtypeStruct((a.shape[0] // count, a.shape[1] // 2), BF16)
    return pl.pallas_call(
        pair_kernel,
        out_shape=(shape,) * (2 * count),
        in_specs=[VMEM, VMEM],
        out_specs=(VMEM,) * (2 * count),
        compiler_params=pltpu.CompilerParams(vmem_limit_bytes=24 * MIB),
        name="pair_sum",
    )(a, b)


def attention_kernel(
    token_blocks,
    factor_blocks,
    head_blocks,
    spot_ref,
    gain_ref,
    row_ref,
    cos_ref,
    sin_ref,
    qg_ref,
    kg_ref,
    sho_ref,
    *refs,
):
    (wq_source, up_source, wo_source, exo_source), refs = refs[:4], refs[4:]
    tokens, refs = refs[:token_blocks], refs[token_blocks:]
    pieces, refs = refs[:factor_blocks], refs[factor_blocks:]
    parts, refs = refs[:head_blocks], refs[head_blocks:]
    own_ref, part_ref, kv_ref = refs[:3]
    wq_ref, up_ref, wo_ref, exo_ref, x_ref, s_ref, w_ref, qf_ref, kvf_ref, q_ref = refs[3:13]
    meta_ref, x_sems, s_sems, w_sems = refs[13:]
    meta_ref[...] = row_ref[...].T
    rows, width = x_ref.shape
    query_cols = wq_ref.shape[1]
    head = qg_ref.shape[1]
    heads = query_cols // head
    block = min(256, rows // 2)
    blocks = rows // block
    scale = head**-0.5
    devices, cols, _ = w_ref.shape
    chips = devices // 2
    own_rows = rows // devices
    chip, core = spot_ref[0], spot_ref[1]
    token_copies, factor_copies, head_copies = [], [], []
    for i, piece in enumerate(tokens):
        target = x_ref.at[pl.ds(i * own_rows, own_rows)]
        token_copies.append(pltpu.make_async_copy(piece, target, x_sems.at[i]))
        token_copies[-1].start()
    for q in range(2):
        for j in range(chips):
            device = (chip ^ j) * 2 + (core ^ q)
            head_copies.append(
                pltpu.make_async_copy(
                    parts[q].at[j], w_ref.at[device], w_sems.at[q * chips + j]
                )
            )
            head_copies[-1].start()
    token_copies.append(pltpu.make_async_copy(wq_source, wq_ref, x_sems.at[devices]))
    token_copies[-1].start()
    factor_copies.append(pltpu.make_async_copy(up_source, up_ref, x_sems.at[devices + 1]))
    factor_copies[-1].start()
    for i, piece in enumerate(pieces):
        target = s_ref.at[pl.ds(spot_ref[2 + i], piece.shape[0])]
        factor_copies.append(pltpu.make_async_copy(piece, target, s_sems.at[i]))
        factor_copies[-1].start()
    last_copies = [
        pltpu.make_async_copy(wo_source, wo_ref, x_sems.at[devices + 2]),
        pltpu.make_async_copy(exo_source, exo_ref, x_sems.at[devices + 3]),
    ]
    for copy in last_copies:
        copy.start()
    adapters, ranks = s_ref.shape[:2]
    factors = adapters * ranks

    def own_slot(low, slot):
        count = low.shape[1] // adapters
        column = lax.broadcasted_iota(jnp.int32, (1, low.shape[1]), 1).astype(F32)
        keep = (column >= slot * count) & (column < slot * count + count)
        return jnp.where(keep, low, 0.0).astype(BF16)

    gain = gain_ref[...].astype(F32)
    qg = qg_ref[...].astype(F32)
    kg = kg_ref[...].astype(F32)

    for copy in token_copies + head_copies:
        copy.wait()

    def project(i, carry):
        here = pl.ds(pl.multiple_of(i * block, block), block)
        x = rms(x_ref[here, :].astype(F32), gain).astype(BF16)
        x_ref[here, :] = x
        qf_ref[here, :] = dot(x, wq_ref[...])
        kvf_ref[here, :] = dot_nt(x, w_ref[...].reshape(devices * cols, width))
        return carry

    loop(blocks, project, 0)

    for copy in factor_copies:
        copy.wait()

    def turned(v, gain, here):
        v = rms(v, gain)
        return v * cos_ref[here, :] + pltpu.roll(v, head // 2, 1) * sin_ref[here, :]

    def adapt(i, carry):
        here = pl.ds(pl.multiple_of(i * block, block), block)
        low = dot_nt(x_ref[here, :], s_ref[...].reshape(factors, width))
        low = own_slot(low, meta_ref[here, 0:1])
        delta = ADAPTER_FACTOR * dot(low, up_ref[...])
        q = qf_ref[here, :] + delta[:, :query_cols]
        kv = (kvf_ref[here, :] + delta[:, query_cols:]).astype(BF16)
        for h in range(heads):
            cut = slice(h * head, (h + 1) * head)
            q_ref[here, cut] = turned(q[:, cut], qg, here).astype(BF16)
        kv_ref[here, :head] = turned(kv[:, :head].astype(F32), kg, here).astype(BF16)
        kv_ref[here, head:] = kv[:, head:]
        return carry

    loop(blocks, adapt, 0)

    for copy in last_copies:
        copy.wait()

    def attend(target, offset):
        def one(i, carry):
            there = pl.ds(pl.multiple_of(i * block, block), block)
            here = pl.ds(pl.multiple_of(offset + i * block, block), block)
            allowed = (row_ref[2:3, :] <= meta_ref[here, 2:3]) & (
                row_ref[1:2, :] == meta_ref[here, 1:2]
            )
            heads_mixed = []
            for h in range(heads):
                cut = slice(h * head, (h + 1) * head)
                s = dot_nt(q_ref[here, cut], kv_ref[:, :head]) * scale
                raised = jnp.where(allowed, jnp.exp(s), 0.0)
                mixed = dot(raised.astype(BF16), kv_ref[:, head:])
                mixed = mixed / jnp.sum(raised, axis=1, keepdims=True)
                heads_mixed.append(mixed.astype(BF16))
            mixed = jnp.concatenate(heads_mixed, axis=1)
            low = dot_nt(mixed, sho_ref[...])
            low = own_slot(low, meta_ref[here, 0:1])
            step = min(512, width)
            for c in range(0, width, step):
                cut = slice(c, c + step)
                term = dot(mixed, wo_ref[:, cut]) + ADAPTER_FACTOR * dot(low, exo_ref[:, cut])
                target[there, cut] = term.astype(BF16)
            return carry

        loop(blocks // 2, one, 0)

    attend(part_ref, rows // 2)
    attend(own_ref, 0)


def attention(spots, tokens, weights, meta, pieces, parts, adapters):
    gain, wq, up, qg, kg, sho, wo, exo = weights
    own_rows, width = tokens[0].shape
    rows = own_rows * len(tokens)
    chips, cols, _ = parts[0].shape
    query_cols = wq.shape[1]
    head = qg.shape[1]
    ranks = pieces[0].shape[1]
    half = jax.ShapeDtypeStruct((rows // 2, width), BF16)
    flops = 2 * rows * (width * (adapters * ranks + 2 * query_cols + 2 * head) + rows * query_cols)
    return pl.pallas_call(
        functools.partial(attention_kernel, len(tokens), len(pieces), len(parts)),
        out_shape=(half, half, jax.ShapeDtypeStruct((rows, 2 * head), BF16)),
        in_specs=[SMEM] + [VMEM] * 7 + [ANY] * (4 + len(tokens) + len(pieces) + len(parts)),
        out_specs=(VMEM, VMEM, VMEM),
        scratch_shapes=[
            pltpu.VMEM(wq.shape, BF16),
            pltpu.VMEM(up.shape, BF16),
            pltpu.VMEM(wo.shape, BF16),
            pltpu.VMEM(exo.shape, BF16),
            pltpu.VMEM((rows, width), BF16),
            pltpu.VMEM((adapters, ranks, width), BF16),
            pltpu.VMEM((2 * chips, cols, width), BF16),
            pltpu.VMEM((rows, query_cols), F32),
            pltpu.VMEM((rows, 2 * head), F32),
            pltpu.VMEM((rows, query_cols), BF16),
            pltpu.VMEM((rows, meta[0].shape[0]), F32),
            pltpu.SemaphoreType.DMA((2 * chips + 4,)),
            pltpu.SemaphoreType.DMA((len(pieces),)),
            pltpu.SemaphoreType.DMA((2 * chips,)),
        ],
        compiler_params=pltpu.CompilerParams(vmem_limit_bytes=60 * MIB),
        cost_estimate=pl.CostEstimate(
            flops=flops, bytes_accessed=16 * MIB, transcendentals=rows * rows
        ),
        name="attention",
    )(spots, gain, *meta, qg, kg, sho, wq, up, wo, exo, *tokens, *pieces, *parts)


def pages_kernel(first_ref, length_ref, page_ref, entries_ref, out_ref):
    columns, extent = entries_ref.shape
    rows = extent - PAGE
    window = 2 * PAGE
    gap = lax.broadcasted_iota(jnp.int32, (window, PAGE), 0) - lax.broadcasted_iota(
        jnp.int32, (window, PAGE), 1
    )
    lane = lax.broadcasted_iota(jnp.int32, (columns, PAGE), 1)

    def one(n, carry):
        length = length_ref[n]
        page = page_ref[n]

        @pl.when(length > 0)
        def _():
            first = jnp.minimum(first_ref[n], rows - 1)
            base = pl.multiple_of(first // PAGE * PAGE, PAGE)
            pick = (gap == first - base).astype(F32).astype(BF16)
            moved = dot(entries_ref[:, pl.ds(base, window)], pick)
            out_ref[page] = jnp.where(lane < length, moved, 0.0).astype(BF16)

        @pl.when(length <= 0)
        def _():
            out_ref[page] = jnp.zeros((columns, PAGE), BF16)

        return carry

    lax.fori_loop(0, page_ref.shape[0], one, 0)


def fill_pages(first, length, page, entries):
    rows, columns = entries.shape
    count = page.shape[0]
    turned = jnp.pad(entries.T, ((0, 0), (0, PAGE)))
    return pl.pallas_call(
        pages_kernel,
        out_shape=jax.ShapeDtypeStruct((count, columns, PAGE), BF16),
        in_specs=[SMEM, SMEM, SMEM, VMEM],
        out_specs=VMEM,
        compiler_params=pltpu.CompilerParams(vmem_limit_bytes=32 * MIB),
        cost_estimate=pl.CostEstimate(
            flops=count * columns * PAGE * PAGE * 16, bytes_accessed=4 * MIB, transcendentals=0
        ),
        name="fill_pages",
    )(first, length, page, turned)


def start_all(copies):
    for copy in copies:
        copy.start()
    return copies


def wait_all(copies):
    for copy in copies:
        copy.wait()


def token_copies(pieces, x_ref, sems):
    rows = pieces[0].shape[0]
    return [
        pltpu.make_async_copy(piece, x_ref.at[pl.ds(i * rows, rows)], sems.at[i])
        for i, piece in enumerate(pieces)
    ]


def pick_rows(route_ref, x_ref, rows_ref, experts, pair, room, capacity):
    total, width = x_ref.shape
    step = min(512, width)
    line = lax.broadcasted_iota(jnp.int32, (room, pair), 0).astype(F32)
    for b in range(total // pair):
        there = slice(b * pair, (b + 1) * pair)
        pick = jnp.concatenate(
            [
                (route_ref[n : n + 1, there] == line + b * room).astype(F32).astype(BF16)
                for n in range(experts)
            ],
            axis=0,
        )
        for c in range(0, width, step):
            cut = slice(c, c + step)
            got = dot(pick, x_ref[there, cut]).astype(BF16)
            for n in range(experts):
                begin = n * capacity + b * room
                rows_ref[begin : begin + room, cut] = got[n * room : (n + 1) * room]


def combine(turned_ref, y_ref, own_ref, part_ref, experts, pair, room, capacity):
    total, width = turned_ref.shape[0], y_ref.shape[1]
    step = min(512, width)
    half = total // 2
    line = lax.broadcasted_iota(jnp.int32, (pair, experts * room), 1).astype(F32)
    for b in range(total // pair):
        here = slice(b * pair, (b + 1) * pair)
        spread = jnp.zeros((pair, experts * room), F32)
        for n in range(experts):
            place = turned_ref[here, n : n + 1] + (n - b) * room
            share = turned_ref[here, experts + n : experts + n + 1]
            spread = jnp.where(place == line, share, spread)
        spread = spread.astype(BF16)
        target, first = (own_ref, b * pair) if b * pair < half else (part_ref, b * pair - half)
        for c in range(0, width, step):
            cut = slice(c, c + step)
            begins = [n * capacity + b * room for n in range(experts)]
            y = jnp.concatenate([y_ref[begin : begin + room, cut] for begin in begins], axis=0)
            target[first : first + pair, cut] = dot(spread, y).astype(BF16)


def experts_kernel(blocks, capacity, route_ref, *refs):
    pieces, refs = refs[:blocks], refs[blocks:]
    gate_ref, up_ref, down_ref, own_ref, part_ref = refs[:5]
    x_ref, rows_ref, y_ref, turned_ref, sum_ref, gate_buf, up_buf, down_buf = refs[5:13]
    x_sems, w_sems = refs[13:]
    experts = rows_ref.shape[0] // capacity
    slots = gate_buf.shape[0]
    streams = ((gate_ref, gate_buf), (up_ref, up_buf), (down_ref, down_buf))

    def copy(k, e, s):
        source, buffer = streams[k]
        return pltpu.make_async_copy(source.at[e], buffer.at[s], w_sems.at[k, s])

    tokens = start_all(token_copies(pieces, x_ref, x_sems))
    for e in range(min(slots, experts)):
        for k in range(3):
            copy(k, e, e).start()
    turned_ref[...] = route_ref[...].T
    wait_all(tokens)
    pair = 2 * x_ref.shape[0] // blocks
    pick_rows(route_ref, x_ref, rows_ref, experts, pair, 2 * CAP_DEV, capacity)

    def rows_of(e):
        return pl.ds(pl.multiple_of(e * capacity, capacity), capacity)

    def gate_of(e):
        s = lax.rem(e, slots)
        copy(0, e, s).wait()
        return dot_nt(rows_ref[rows_of(e), :], gate_buf[s])

    def finish(e, next_gate):
        s = lax.rem(e, slots)
        copy(1, e, s).wait()
        up = dot_nt(rows_ref[rows_of(e), :], up_buf[s])
        gate = sum_ref[...]
        if next_gate:
            following = gate_of(e + 1)
        hidden = (gate / (1.0 + jnp.exp(-gate)) * up).astype(BF16)
        if next_gate:
            sum_ref[...] = following
        copy(2, e, s).wait()
        y_ref[rows_of(e), :] = dot(hidden, down_buf[s]).astype(BF16)

    def one(e, carry):
        finish(e, True)

        @pl.when(e + slots < experts)
        def _():
            for k in range(3):
                copy(k, e + slots, lax.rem(e, slots)).start()

        return carry

    sum_ref[...] = gate_of(0)
    lax.fori_loop(0, experts - 1, one, 0)
    finish(experts - 1, False)
    combine(turned_ref, y_ref, own_ref, part_ref, experts, pair, 2 * CAP_DEV, capacity)


def expert_layer(routes, pieces, gate, up, down, capacity):
    experts, hidden, width = gate.shape
    own_rows = pieces[0].shape[0]
    total = own_rows * len(pieces)
    slots = min(3 if total <= 512 else 2, experts)
    half = jax.ShapeDtypeStruct((total // 2, width), BF16)
    return pl.pallas_call(
        functools.partial(experts_kernel, len(pieces), capacity),
        out_shape=(half, half),
        in_specs=[VMEM] + [ANY] * (3 + len(pieces)),
        out_specs=(VMEM, VMEM),
        scratch_shapes=[
            pltpu.VMEM((total, width), BF16),
            pltpu.VMEM((experts * capacity, width), BF16),
            pltpu.VMEM((experts * capacity, width), BF16),
            pltpu.VMEM(routes.shape[::-1], F32),
            pltpu.VMEM((capacity, hidden), F32),
            pltpu.VMEM((slots, hidden, width), BF16),
            pltpu.VMEM((slots, hidden, width), BF16),
            pltpu.VMEM((slots, hidden, width), BF16),
            pltpu.SemaphoreType.DMA((len(pieces),)),
            pltpu.SemaphoreType.DMA((3, slots)),
        ],
        compiler_params=pltpu.CompilerParams(vmem_limit_bytes=60 * MIB),
        cost_estimate=pl.CostEstimate(
            flops=6 * experts * capacity * hidden * width,
            bytes_accessed=6 * experts * hidden * width,
            transcendentals=experts * capacity * hidden,
        ),
        name="experts",
    )(routes, *pieces, gate, up, down)


def other_core(value, parts):
    return lax.ppermute(value, "tensor", [(i, i ^ 1) for i in range(parts)])


def swap_chips(value, parts, by):
    return lax.ppermute(value, "tensor", [(i, i ^ (2 * by)) for i in range(parts)])


def swap_holder(value, holders, by):
    return lax.ppermute(value, "dp", [(i, i ^ by) for i in range(holders)])


def gather_blocks(own, parts, between=lambda blocks: blocks):
    chips = parts // 2
    blocks = {0: own}
    bit = chips // 2
    while bit:
        for i, block in list(blocks.items()):
            if i ^ bit not in blocks:
                blocks[i ^ bit] = swap_chips(block, parts, bit)
        if bit == chips // 2:
            if 1 not in blocks:
                blocks[1] = swap_chips(own, parts, 1)
            blocks = between(blocks)
        bit //= 2
    mine = [blocks[i] for i in range(chips)]
    return mine + [other_core(block, parts) for block in mine]


def scatter_terms(own, part, parts):
    chips = parts // 2
    sums = pair_sum(hold(own), other_core(part, parts), chips)
    halves = []
    for k in range(2):
        terms = {j: [sums[2 * j + k]] for j in range(chips)}
        late, last, bit = [], None, 1
        while bit < chips:
            for j in sorted((j for j in terms if j & bit), reverse=True):
                sent = terms.pop(j)
                if len(sent) > 1:
                    sent = [sum(term.astype(F32) for term in sent).astype(BF16)]
                if j == bit and 2 * bit < chips:
                    late.append((bit, sent[0]))
                    continue
                last = sent[0]
                terms[j ^ bit].append(swap_chips(last, parts, bit))
            bit *= 2
        for bit, sent in late:
            sent, last = lax.optimization_barrier((sent, last))
            terms[0].append(swap_chips(sent, parts, bit))
        halves.append(terms[0])
    return halves


def from_here(rows, chip, core, chips):
    split = rows.reshape((chips, 2, -1) + rows.shape[1:])
    split = jnp.where(core == 0, split, split[:, ::-1])
    bit = 1
    while bit < chips:
        pairs = split.reshape((chips // (2 * bit), 2, bit) + split.shape[1:])
        split = jnp.where((chip & bit) == 0, pairs, pairs[:, ::-1]).reshape(split.shape)
        bit *= 2
    return split


def to_device(rows, chip, core, chips):
    return jnp.swapaxes(from_here(rows, chip, core, chips), 0, 1).reshape(rows.shape)


def to_group(rows, chip, core, chips):
    split = jnp.swapaxes(rows.reshape((2, chips, -1) + rows.shape[1:]), 0, 1)
    return from_here(split.reshape(rows.shape), chip, core, chips).reshape(rows.shape)


def local(
    tokens,
    attn_gain,
    moe_gain,
    q_gain,
    k_gain,
    query_weight,
    w_kv,
    w_o,
    w_gate,
    w_up,
    w_down,
    shrink_qkv,
    shrink_o,
    query_up_factors,
    key_value_up_factors,
    expand_o,
    lengths,
    groups,
    adapter_of_request,
    adapter_slot,
    page_table,
    expert_ids,
    expert_gates,
):
    parts = lax.axis_size("tensor")
    place = lax.axis_index("tensor")
    holders = lax.axis_size("dp")
    holder = lax.axis_index("dp")
    chips, chip, core = parts // 2, place // 2, place % 2
    own_rows, width = tokens.shape
    total = own_rows * parts
    head_length = q_gain.shape[0]
    adapters, rank, kv_width = key_value_up_factors.shape
    kv_heads = kv_width // (2 * head_length)
    held, ranks = shrink_qkv.shape[:2]
    head = place * kv_heads // parts
    query_cols = query_weight.shape[1]
    experts = w_gate.shape[0]

    line = jnp.arange(total, dtype=jnp.int32)
    side, number = line // (total // 2), line // own_rows % chips
    position = ((number ^ chip) * 2 + (side ^ core)) * own_rows + line % own_rows
    length_row, group_row, adapter_row = lengths[0], groups[0], adapter_of_request[0]
    ends = jnp.cumsum(length_row)
    starts = ends - length_row
    request = jnp.sum((ends[None, :] <= position[:, None]).astype(jnp.int32), axis=1)
    same = group_row[:, None] == group_row[None, :]
    group_first = jnp.min(jnp.where(same, starts[None, :], total), axis=1)
    slot_of_request = lookup(adapter_row, adapter_slot)
    group = lookup(request, group_row)
    rope_pos = position - lookup(request, group_first)
    slot = lookup(request, slot_of_request)
    meta_row = jnp.stack([slot, group, position] + [position] * 5, axis=0).astype(F32)
    freq = jnp.exp(
        -jnp.arange(head_length // 2, dtype=F32) * (2.0 * math.log(ROPE_BASE) / head_length)
    )
    angle = rope_pos.astype(F32)[:, None] * freq[None, :]
    cosine, sine = jnp.cos(angle), jnp.sin(angle)
    cosine = jnp.concatenate([cosine, cosine], axis=1)
    sine = jnp.concatenate([-sine, sine], axis=1)

    up_kv = lax.dynamic_index_in_dim(
        key_value_up_factors.reshape(adapters, rank, kv_heads, 2, head_length), head, 2, keepdims=False
    )
    up = jnp.concatenate(
        [
            jnp.pad(query_up_factors, ((0, 0), (0, 2 * rank), (0, 0))),
            jnp.pad(up_kv[:, :, 0], ((0, 0), (rank, rank), (0, 0))),
            jnp.pad(up_kv[:, :, 1], ((0, 0), (2 * rank, 0), (0, 0))),
        ],
        axis=2,
    ).reshape(adapters * ranks, query_cols + 2 * head_length)

    weights = (
        attn_gain.reshape(1, -1),
        query_weight,
        up,
        q_gain.reshape(1, -1),
        k_gain.reshape(1, -1),
        shrink_o.reshape(adapters * rank, query_cols),
        w_o,
        expand_o.reshape(adapters * rank, width),
    )
    meta = (meta_row, cosine, sine)
    half = held // 2
    half_own = lax.dynamic_slice_in_dim(shrink_qkv, core * half, half, 0)
    halves = []
    for r in range(1, holders):
        top = 1 << (r.bit_length() - 1)
        halves.append(swap_holder(half_own if r == top else halves[r - top - 1], holders, top))
    spots = [chip, core, holder * held]
    for r in range(1, holders):
        begin = (holder ^ r) * held
        spots += [begin + core * half, begin + (1 - core) * half]
    spots = jnp.stack(spots).astype(jnp.int32)
    cuts = [
        lax.dynamic_index_in_dim(w_kv, 2 * (chip ^ j) * kv_heads // parts, 1, keepdims=False)
        for j in range(chips)
    ]

    def between(blocks):
        nonlocal cuts, meta
        blocks, halves[:2], cuts, meta = lax.optimization_barrier(
            (blocks, halves[:2], cuts, meta)
        )
        return blocks

    gathered = gather_blocks(tokens, parts, between)
    mine = [cuts[0]] + [swap_chips(cuts[j], parts, j) for j in range(1, chips)]
    mine = jnp.stack(mine)
    mine, weights, spots = lax.optimization_barrier((mine, weights, spots))
    head_parts = [mine, other_core(mine, parts)]
    pieces = [shrink_qkv]
    for got in halves:
        pieces += [got, other_core(got, parts)]
    own, part, entries = attention(
        spots,
        gathered,
        weights,
        meta,
        pieces,
        head_parts,
        adapters,
    )
    left, right = scatter_terms(own, part, parts)

    attn_own, moe_own = residual_norm(tokens, moe_gain, left, right)

    moe_own, entries, starts, length_row, page_table, expert_ids, expert_gates = (
        lax.optimization_barrier(
            (moe_own, entries, starts, length_row, page_table, expert_ids, expert_gates)
        )
    )

    local_cols = kv_width // parts
    kept = lax.dynamic_slice_in_dim(
        entries, place * local_cols - head * 2 * head_length, local_cols, 1
    )
    page_row = page_table[0]
    per_request = page_row.shape[0] // length_row.shape[0]
    offset = PAGE * jnp.arange(per_request, dtype=jnp.int32)[None, :]
    page_first = (starts[:, None] + offset).reshape(-1)
    page_length = jnp.clip(length_row[:, None] - offset, 0, PAGE).reshape(-1)
    kv_pages = fill_pages(page_first, page_length, page_row, to_group(kept, chip, core, chips))

    capacity = CAP_DEV * parts
    ids = to_device(expert_ids, chip, core, chips)
    gates = to_device(expert_gates, chip, core, chips)
    share = gates / jnp.sum(gates, axis=1, keepdims=True)
    own_experts = place * experts + jnp.arange(experts, dtype=jnp.int32)
    chosen = ids[:, :, None] == own_experts[None, None, :]
    hit = jnp.any(chosen, axis=1)
    weight = jnp.sum(jnp.where(chosen, share[:, :, None], 0.0), axis=1)
    block = line // own_rows
    earlier = (line[:, None] > line[None, :]) & (block[:, None] == block[None, :])
    before = dot(earlier.astype(BF16), hit.astype(BF16)).astype(jnp.int32)
    slot_in = jnp.where(hit, block[:, None] * CAP_DEV + before, -(1 << 20))

    routes = jnp.concatenate([slot_in.astype(F32).T, weight.T], axis=0)
    routes = jnp.pad(routes, ((0, -routes.shape[0] % 8), (0, 0)))

    def tables_first(blocks):
        nonlocal routes, kv_pages
        blocks, routes, kv_pages = lax.optimization_barrier((blocks, routes, kv_pages))
        return blocks

    gathered = gather_blocks(moe_own, parts, tables_first)
    own, part = expert_layer(routes, gathered, w_gate, w_up, w_down, capacity)
    left, right = scatter_terms(own, part, parts)

    moe_total = total_rows(left, right)
    return (attn_own, moe_total, kv_pages)


def solution(mesh):
    placed = (
        P(("dp", "tensor"), None),
        P(),
        P(),
        P(),
        P(),
        P(None, "tensor"),
        P("tensor", None, None),
        P("tensor", None),
        P("tensor", None, None),
        P("tensor", None, None),
        P("tensor", None, None),
        P("dp", None, None),
        P(None, None, "tensor"),
        P(None, None, "tensor"),
        P(),
        P(),
        P("dp", None),
        P("dp", None),
        P("dp", None),
        P(),
        P("dp", None),
        P("dp", None),
        P("dp", None),
    )
    return jax.shard_map(
        local,
        mesh=mesh,
        in_specs=placed,
        out_specs=(P(("dp", "tensor"), None), P(("dp", "tensor"), None), P("dp", "tensor", None)),
        check_vma=False,
    )
```

```python
import functools
import math

import jax
import jax.numpy as jnp
from jax import lax
from jax.experimental import pallas as pl
from jax.experimental.pallas import tpu as pltpu
from jax.sharding import PartitionSpec as P

PAGE = 128
CAP_DEV = 16
NORM_EPS = 1e-06
ROPE_BASE = 1000000.0
ADAPTER_FACTOR = 0.5
MIB = 1 << 20
BF16 = jnp.bfloat16
F32 = jnp.float32
VMEM = pl.BlockSpec(memory_space=pltpu.VMEM)
SMEM = pl.BlockSpec(memory_space=pltpu.SMEM)
ANY = pl.BlockSpec(memory_space=pl.ANY)
HBM = pl.BlockSpec(memory_space=pltpu.HBM)


def dot(a, b):
    return jnp.dot(a, b, preferred_element_type=F32)


def dot_nt(a, b):
    return lax.dot_general(a, b, (((1,), (1,)), ((), ())), preferred_element_type=F32)


def lookup(index_value, table):
    match = index_value[:, None] == jnp.arange(table.shape[0], dtype=jnp.int32)[None, :]
    return jnp.sum(jnp.where(match, table[None, :], 0), axis=1)


def loop(count, body, carry):
    if count <= 2:
        for i in range(count):
            carry = body(i, carry)
        return carry
    return lax.fori_loop(0, count, body, carry)


def rms(v, gain):
    return v * lax.rsqrt(jnp.mean(v * v, axis=-1, keepdims=True) + NORM_EPS) * gain


def total_of(parts):
    total = parts[0][...].astype(F32)
    for part in parts[1:]:
        total = total + part[...].astype(F32)
    return total


def residual_kernel(count, x_ref, gain_ref, *refs):
    attn_ref, out_ref = refs[-2:]
    total = jnp.concatenate([total_of(refs[:count]), total_of(refs[count:-2])], axis=1)
    attn_ref[...] = total.astype(BF16)
    out_ref[...] = rms(x_ref[...].astype(F32) + total, gain_ref[...].astype(F32)).astype(BF16)


def residual_norm(x, gain, left, right):
    shape = jax.ShapeDtypeStruct(x.shape, BF16)
    return pl.pallas_call(
        functools.partial(residual_kernel, len(left)),
        out_shape=(shape, shape),
        in_specs=[VMEM] * (2 + len(left) + len(right)),
        out_specs=(VMEM, VMEM),
        name="residual_norm",
    )(x, gain.reshape(1, -1), *left, *right)


def total_kernel(count, *refs):
    out_ref = refs[-1]
    half = out_ref.shape[1] // 2
    out_ref[:, :half] = total_of(refs[:count]).astype(BF16)
    out_ref[:, half:] = total_of(refs[count:-1]).astype(BF16)


def total_rows(left, right):
    rows, half = left[0].shape
    return pl.pallas_call(
        functools.partial(total_kernel, len(left)),
        out_shape=jax.ShapeDtypeStruct((rows, 2 * half), BF16),
        in_specs=[VMEM] * (len(left) + len(right)),
        out_specs=VMEM,
        name="total_rows",
    )(*left, *right)


def hold_kernel(source_ref, out_ref, sem):
    copy = pltpu.make_async_copy(source_ref, out_ref, sem)
    copy.start()
    copy.wait()


def hold(rows):
    return pl.pallas_call(
        hold_kernel,
        out_shape=pltpu.VMEM(rows.shape, BF16),
        in_specs=[HBM],
        out_specs=VMEM,
        scratch_shapes=[pltpu.SemaphoreType.DMA],
        compiler_params=pltpu.CompilerParams(vmem_limit_bytes=4 * MIB),
        name="hold",
    )(pltpu.with_memory_space_constraint(rows, pltpu.HBM))


def pair_kernel(a_ref, b_ref, *outs):
    rows, half = outs[0].shape
    for i in range(len(outs) // 2):
        here = slice(i * rows, (i + 1) * rows)
        total = (a_ref[here, :].astype(F32) + b_ref[here, :].astype(F32)).astype(BF16)
        outs[2 * i][...] = total[:, :half]
        outs[2 * i + 1][...] = total[:, half:]


def pair_sum(a, b, count):
    shape = jax.ShapeDtypeStruct((a.shape[0] // count, a.shape[1] // 2), BF16)
    return pl.pallas_call(
        pair_kernel,
        out_shape=(shape,) * (2 * count),
        in_specs=[VMEM, VMEM],
        out_specs=(VMEM,) * (2 * count),
        compiler_params=pltpu.CompilerParams(vmem_limit_bytes=24 * MIB),
        name="pair_sum",
    )(a, b)


def attention_kernel(
    token_blocks,
    factor_blocks,
    head_blocks,
    spot_ref,
    gain_ref,
    row_ref,
    cos_ref,
    sin_ref,
    qg_ref,
    kg_ref,
    sho_ref,
    *refs,
):
    (wq_source, up_source, wo_source, exo_source), refs = refs[:4], refs[4:]
    tokens, refs = refs[:token_blocks], refs[token_blocks:]
    pieces, refs = refs[:factor_blocks], refs[factor_blocks:]
    parts, refs = refs[:head_blocks], refs[head_blocks:]
    own_ref, part_ref, kv_ref = refs[:3]
    wq_ref, up_ref, wo_ref, exo_ref, x_ref, s_ref, w_ref, qf_ref, kvf_ref, q_ref = refs[3:13]
    meta_ref, x_sems, s_sems, w_sems = refs[13:]
    meta_ref[...] = row_ref[...].T
    rows, width = x_ref.shape
    query_cols = wq_ref.shape[1]
    head = qg_ref.shape[1]
    heads = query_cols // head
    block = min(256, rows // 2)
    blocks = rows // block
    scale = head**-0.5
    devices, cols, _ = w_ref.shape
    chips = devices // 2
    own_rows = rows // devices
    chip, core = spot_ref[0], spot_ref[1]
    token_copies, factor_copies, head_copies = [], [], []
    for i, piece in enumerate(tokens):
        target = x_ref.at[pl.ds(i * own_rows, own_rows)]
        token_copies.append(pltpu.make_async_copy(piece, target, x_sems.at[i]))
        token_copies[-1].start()
    for q in range(2):
        for j in range(chips):
            device = (chip ^ j) * 2 + (core ^ q)
            head_copies.append(
                pltpu.make_async_copy(
                    parts[q].at[j], w_ref.at[device], w_sems.at[q * chips + j]
                )
            )
            head_copies[-1].start()
    token_copies.append(pltpu.make_async_copy(wq_source, wq_ref, x_sems.at[devices]))
    token_copies[-1].start()
    factor_copies.append(pltpu.make_async_copy(up_source, up_ref, x_sems.at[devices + 1]))
    factor_copies[-1].start()
    for i, piece in enumerate(pieces):
        target = s_ref.at[pl.ds(spot_ref[2 + i], piece.shape[0])]
        factor_copies.append(pltpu.make_async_copy(piece, target, s_sems.at[i]))
        factor_copies[-1].start()
    last_copies = [
        pltpu.make_async_copy(wo_source, wo_ref, x_sems.at[devices + 2]),
        pltpu.make_async_copy(exo_source, exo_ref, x_sems.at[devices + 3]),
    ]
    for copy in last_copies:
        copy.start()
    adapters, ranks = s_ref.shape[:2]
    factors = adapters * ranks

    def own_slot(low, slot):
        count = low.shape[1] // adapters
        column = lax.broadcasted_iota(jnp.int32, (1, low.shape[1]), 1).astype(F32)
        keep = (column >= slot * count) & (column < slot * count + count)
        return jnp.where(keep, low, 0.0).astype(BF16)

    gain = gain_ref[...].astype(F32)
    qg = qg_ref[...].astype(F32)
    kg = kg_ref[...].astype(F32)

    for copy in token_copies + head_copies:
        copy.wait()

    def project(i, carry):
        here = pl.ds(pl.multiple_of(i * block, block), block)
        x = rms(x_ref[here, :].astype(F32), gain).astype(BF16)
        x_ref[here, :] = x
        qf_ref[here, :] = dot(x, wq_ref[...])
        kvf_ref[here, :] = dot_nt(x, w_ref[...].reshape(devices * cols, width))
        return carry

    loop(blocks, project, 0)

    for copy in factor_copies:
        copy.wait()

    def turned(v, gain, here):
        v = rms(v, gain)
        return v * cos_ref[here, :] + pltpu.roll(v, head // 2, 1) * sin_ref[here, :]

    def adapt(i, carry):
        here = pl.ds(pl.multiple_of(i * block, block), block)
        low = dot_nt(x_ref[here, :], s_ref[...].reshape(factors, width))
        low = own_slot(low, meta_ref[here, 0:1])
        delta = ADAPTER_FACTOR * dot(low, up_ref[...])
        q = qf_ref[here, :] + delta[:, :query_cols]
        kv = (kvf_ref[here, :] + delta[:, query_cols:]).astype(BF16)
        for h in range(heads):
            cut = slice(h * head, (h + 1) * head)
            q_ref[here, cut] = turned(q[:, cut], qg, here).astype(BF16)
        kv_ref[here, :head] = turned(kv[:, :head].astype(F32), kg, here).astype(BF16)
        kv_ref[here, head:] = kv[:, head:]
        return carry

    loop(blocks, adapt, 0)

    for copy in last_copies:
        copy.wait()

    def attend(target, offset):
        def one(i, carry):
            there = pl.ds(pl.multiple_of(i * block, block), block)
            here = pl.ds(pl.multiple_of(offset + i * block, block), block)
            allowed = (row_ref[2:3, :] <= meta_ref[here, 2:3]) & (
                row_ref[1:2, :] == meta_ref[here, 1:2]
            )
            heads_mixed = []
            for h in range(heads):
                cut = slice(h * head, (h + 1) * head)
                s = dot_nt(q_ref[here, cut], kv_ref[:, :head]) * scale
                raised = jnp.where(allowed, jnp.exp(s), 0.0)
                mixed = dot(raised.astype(BF16), kv_ref[:, head:])
                mixed = mixed / jnp.sum(raised, axis=1, keepdims=True)
                heads_mixed.append(mixed.astype(BF16))
            mixed = jnp.concatenate(heads_mixed, axis=1)
            low = dot_nt(mixed, sho_ref[...])
            low = own_slot(low, meta_ref[here, 0:1])
            step = min(512, width)
            for c in range(0, width, step):
                cut = slice(c, c + step)
                term = dot(mixed, wo_ref[:, cut]) + ADAPTER_FACTOR * dot(low, exo_ref[:, cut])
                target[there, cut] = term.astype(BF16)
            return carry

        loop(blocks // 2, one, 0)

    attend(part_ref, rows // 2)
    attend(own_ref, 0)


def attention(spots, tokens, weights, meta, pieces, parts, adapters):
    gain, wq, up, qg, kg, sho, wo, exo = weights
    own_rows, width = tokens[0].shape
    rows = own_rows * len(tokens)
    chips, cols, _ = parts[0].shape
    query_cols = wq.shape[1]
    head = qg.shape[1]
    ranks = pieces[0].shape[1]
    half = jax.ShapeDtypeStruct((rows // 2, width), BF16)
    flops = 2 * rows * (width * (adapters * ranks + 2 * query_cols + 2 * head) + rows * query_cols)
    return pl.pallas_call(
        functools.partial(attention_kernel, len(tokens), len(pieces), len(parts)),
        out_shape=(half, half, jax.ShapeDtypeStruct((rows, 2 * head), BF16)),
        in_specs=[SMEM] + [VMEM] * 7 + [ANY] * (4 + len(tokens) + len(pieces) + len(parts)),
        out_specs=(VMEM, VMEM, VMEM),
        scratch_shapes=[
            pltpu.VMEM(wq.shape, BF16),
            pltpu.VMEM(up.shape, BF16),
            pltpu.VMEM(wo.shape, BF16),
            pltpu.VMEM(exo.shape, BF16),
            pltpu.VMEM((rows, width), BF16),
            pltpu.VMEM((adapters, ranks, width), BF16),
            pltpu.VMEM((2 * chips, cols, width), BF16),
            pltpu.VMEM((rows, query_cols), F32),
            pltpu.VMEM((rows, 2 * head), F32),
            pltpu.VMEM((rows, query_cols), BF16),
            pltpu.VMEM((rows, meta[0].shape[0]), F32),
            pltpu.SemaphoreType.DMA((2 * chips + 4,)),
            pltpu.SemaphoreType.DMA((len(pieces),)),
            pltpu.SemaphoreType.DMA((2 * chips,)),
        ],
        compiler_params=pltpu.CompilerParams(vmem_limit_bytes=60 * MIB),
        cost_estimate=pl.CostEstimate(
            flops=flops, bytes_accessed=16 * MIB, transcendentals=rows * rows
        ),
        name="attention",
    )(spots, gain, *meta, qg, kg, sho, wq, up, wo, exo, *tokens, *pieces, *parts)


def pages_kernel(first_ref, length_ref, page_ref, entries_ref, out_ref):
    columns, extent = entries_ref.shape
    rows = extent - PAGE
    window = 2 * PAGE
    gap = lax.broadcasted_iota(jnp.int32, (window, PAGE), 0) - lax.broadcasted_iota(
        jnp.int32, (window, PAGE), 1
    )
    lane = lax.broadcasted_iota(jnp.int32, (columns, PAGE), 1)

    def one(n, carry):
        length = length_ref[n]
        page = page_ref[n]

        @pl.when(length > 0)
        def _():
            first = jnp.minimum(first_ref[n], rows - 1)
            base = pl.multiple_of(first // PAGE * PAGE, PAGE)
            pick = (gap == first - base).astype(F32).astype(BF16)
            moved = dot(entries_ref[:, pl.ds(base, window)], pick)
            out_ref[page] = jnp.where(lane < length, moved, 0.0).astype(BF16)

        @pl.when(length <= 0)
        def _():
            out_ref[page] = jnp.zeros((columns, PAGE), BF16)

        return carry

    lax.fori_loop(0, page_ref.shape[0], one, 0)


def fill_pages(first, length, page, entries):
    rows, columns = entries.shape
    count = page.shape[0]
    turned = jnp.pad(entries.T, ((0, 0), (0, PAGE)))
    return pl.pallas_call(
        pages_kernel,
        out_shape=jax.ShapeDtypeStruct((count, columns, PAGE), BF16),
        in_specs=[SMEM, SMEM, SMEM, VMEM],
        out_specs=VMEM,
        compiler_params=pltpu.CompilerParams(vmem_limit_bytes=32 * MIB),
        cost_estimate=pl.CostEstimate(
            flops=count * columns * PAGE * PAGE * 16, bytes_accessed=4 * MIB, transcendentals=0
        ),
        name="fill_pages",
    )(first, length, page, turned)


def start_all(copies):
    for copy in copies:
        copy.start()
    return copies


def wait_all(copies):
    for copy in copies:
        copy.wait()


def token_copies(pieces, x_ref, sems):
    rows = pieces[0].shape[0]
    return [
        pltpu.make_async_copy(piece, x_ref.at[pl.ds(i * rows, rows)], sems.at[i])
        for i, piece in enumerate(pieces)
    ]


def pick_rows(route_ref, x_ref, rows_ref, experts, pair, room, capacity):
    total, width = x_ref.shape
    step = min(512, width)
    line = lax.broadcasted_iota(jnp.int32, (room, pair), 0).astype(F32)
    for b in range(total // pair):
        there = slice(b * pair, (b + 1) * pair)
        pick = jnp.concatenate(
            [
                (route_ref[n : n + 1, there] == line + b * room).astype(F32).astype(BF16)
                for n in range(experts)
            ],
            axis=0,
        )
        for c in range(0, width, step):
            cut = slice(c, c + step)
            got = dot(pick, x_ref[there, cut]).astype(BF16)
            for n in range(experts):
                begin = n * capacity + b * room
                rows_ref[begin : begin + room, cut] = got[n * room : (n + 1) * room]


def combine(turned_ref, y_ref, own_ref, part_ref, experts, pair, room, capacity):
    total, width = turned_ref.shape[0], y_ref.shape[1]
    step = min(512, width)
    half = total // 2
    line = lax.broadcasted_iota(jnp.int32, (pair, experts * room), 1).astype(F32)
    for b in range(total // pair):
        here = slice(b * pair, (b + 1) * pair)
        spread = jnp.zeros((pair, experts * room), F32)
        for n in range(experts):
            place = turned_ref[here, n : n + 1] + (n - b) * room
            share = turned_ref[here, experts + n : experts + n + 1]
            spread = jnp.where(place == line, share, spread)
        spread = spread.astype(BF16)
        target, first = (own_ref, b * pair) if b * pair < half else (part_ref, b * pair - half)
        for c in range(0, width, step):
            cut = slice(c, c + step)
            begins = [n * capacity + b * room for n in range(experts)]
            y = jnp.concatenate([y_ref[begin : begin + room, cut] for begin in begins], axis=0)
            target[first : first + pair, cut] = dot(spread, y).astype(BF16)


def experts_kernel(blocks, capacity, route_ref, *refs):
    pieces, refs = refs[:blocks], refs[blocks:]
    gate_ref, up_ref, down_ref, own_ref, part_ref = refs[:5]
    x_ref, rows_ref, y_ref, turned_ref, gate_buf, up_buf, down_buf, x_sems, w_sems = refs[5:]
    experts = rows_ref.shape[0] // capacity
    slots = gate_buf.shape[0]
    streams = ((gate_ref, gate_buf), (up_ref, up_buf), (down_ref, down_buf))

    def copy(k, e, s):
        source, buffer = streams[k]
        return pltpu.make_async_copy(source.at[e], buffer.at[s], w_sems.at[k, s])

    tokens = start_all(token_copies(pieces, x_ref, x_sems))
    for e in range(min(slots, experts)):
        for k in range(3):
            copy(k, e, e).start()
    turned_ref[...] = route_ref[...].T
    wait_all(tokens)
    pair = 2 * x_ref.shape[0] // blocks
    pick_rows(route_ref, x_ref, rows_ref, experts, pair, 2 * CAP_DEV, capacity)

    def one(e, carry):
        s = lax.rem(e, slots)
        here = pl.ds(pl.multiple_of(e * capacity, capacity), capacity)
        x = rows_ref[here, :]
        copy(0, e, s).wait()
        gate = dot_nt(x, gate_buf[s])
        copy(1, e, s).wait()
        up = dot_nt(x, up_buf[s])
        hidden = (gate / (1.0 + jnp.exp(-gate)) * up).astype(BF16)
        copy(2, e, s).wait()
        y_ref[here, :] = dot(hidden, down_buf[s]).astype(BF16)

        @pl.when(e + slots < experts)
        def _():
            for k in range(3):
                copy(k, e + slots, s).start()

        return carry

    lax.fori_loop(0, experts, one, 0)
    combine(turned_ref, y_ref, own_ref, part_ref, experts, pair, 2 * CAP_DEV, capacity)


def expert_layer(routes, pieces, gate, up, down, capacity):
    experts, hidden, width = gate.shape
    own_rows = pieces[0].shape[0]
    total = own_rows * len(pieces)
    slots = min(3 if total <= 512 else 2, experts)
    half = jax.ShapeDtypeStruct((total // 2, width), BF16)
    return pl.pallas_call(
        functools.partial(experts_kernel, len(pieces), capacity),
        out_shape=(half, half),
        in_specs=[VMEM] + [ANY] * (3 + len(pieces)),
        out_specs=(VMEM, VMEM),
        scratch_shapes=[
            pltpu.VMEM((total, width), BF16),
            pltpu.VMEM((experts * capacity, width), BF16),
            pltpu.VMEM((experts * capacity, width), BF16),
            pltpu.VMEM(routes.shape[::-1], F32),
            pltpu.VMEM((slots, hidden, width), BF16),
            pltpu.VMEM((slots, hidden, width), BF16),
            pltpu.VMEM((slots, hidden, width), BF16),
            pltpu.SemaphoreType.DMA((len(pieces),)),
            pltpu.SemaphoreType.DMA((3, slots)),
        ],
        compiler_params=pltpu.CompilerParams(vmem_limit_bytes=60 * MIB),
        cost_estimate=pl.CostEstimate(
            flops=6 * experts * capacity * hidden * width,
            bytes_accessed=6 * experts * hidden * width,
            transcendentals=experts * capacity * hidden,
        ),
        name="experts",
    )(routes, *pieces, gate, up, down)


def other_core(value, parts):
    return lax.ppermute(value, "tensor", [(i, i ^ 1) for i in range(parts)])


def swap_chips(value, parts, by):
    return lax.ppermute(value, "tensor", [(i, i ^ (2 * by)) for i in range(parts)])


def swap_holder(value, holders, by):
    return lax.ppermute(value, "dp", [(i, i ^ by) for i in range(holders)])


def gather_blocks(own, parts, between=lambda blocks: blocks):
    chips = parts // 2
    blocks = {0: own}
    bit = chips // 2
    while bit:
        for i, block in list(blocks.items()):
            if i ^ bit not in blocks:
                blocks[i ^ bit] = swap_chips(block, parts, bit)
        if bit == chips // 2:
            if 1 not in blocks:
                blocks[1] = swap_chips(own, parts, 1)
            blocks = between(blocks)
        bit //= 2
    mine = [blocks[i] for i in range(chips)]
    return mine + [other_core(block, parts) for block in mine]


def scatter_terms(own, part, parts):
    chips = parts // 2
    sums = pair_sum(hold(own), other_core(part, parts), chips)
    halves = []
    for k in range(2):
        terms = {j: [sums[2 * j + k]] for j in range(chips)}
        late, last, bit = [], None, 1
        while bit < chips:
            for j in sorted((j for j in terms if j & bit), reverse=True):
                sent = terms.pop(j)
                if len(sent) > 1:
                    sent = [sum(term.astype(F32) for term in sent).astype(BF16)]
                if j == bit and 2 * bit < chips:
                    late.append((bit, sent[0]))
                    continue
                last = sent[0]
                terms[j ^ bit].append(swap_chips(last, parts, bit))
            bit *= 2
        for bit, sent in late:
            sent, last = lax.optimization_barrier((sent, last))
            terms[0].append(swap_chips(sent, parts, bit))
        halves.append(terms[0])
    return halves


def from_here(rows, chip, core, chips):
    split = rows.reshape((chips, 2, -1) + rows.shape[1:])
    split = jnp.where(core == 0, split, split[:, ::-1])
    bit = 1
    while bit < chips:
        pairs = split.reshape((chips // (2 * bit), 2, bit) + split.shape[1:])
        split = jnp.where((chip & bit) == 0, pairs, pairs[:, ::-1]).reshape(split.shape)
        bit *= 2
    return split


def to_device(rows, chip, core, chips):
    return jnp.swapaxes(from_here(rows, chip, core, chips), 0, 1).reshape(rows.shape)


def to_group(rows, chip, core, chips):
    split = jnp.swapaxes(rows.reshape((2, chips, -1) + rows.shape[1:]), 0, 1)
    return from_here(split.reshape(rows.shape), chip, core, chips).reshape(rows.shape)


def local(
    tokens,
    attn_gain,
    moe_gain,
    q_gain,
    k_gain,
    query_weight,
    w_kv,
    w_o,
    w_gate,
    w_up,
    w_down,
    shrink_qkv,
    shrink_o,
    query_up_factors,
    key_value_up_factors,
    expand_o,
    lengths,
    groups,
    adapter_of_request,
    adapter_slot,
    page_table,
    expert_ids,
    expert_gates,
):
    parts = lax.axis_size("tensor")
    place = lax.axis_index("tensor")
    holders = lax.axis_size("dp")
    holder = lax.axis_index("dp")
    chips, chip, core = parts // 2, place // 2, place % 2
    own_rows, width = tokens.shape
    total = own_rows * parts
    head_length = q_gain.shape[0]
    adapters, rank, kv_width = key_value_up_factors.shape
    kv_heads = kv_width // (2 * head_length)
    held, ranks = shrink_qkv.shape[:2]
    head = place * kv_heads // parts
    query_cols = query_weight.shape[1]
    experts = w_gate.shape[0]

    line = jnp.arange(total, dtype=jnp.int32)
    side, number = line // (total // 2), line // own_rows % chips
    position = ((number ^ chip) * 2 + (side ^ core)) * own_rows + line % own_rows
    length_row, group_row, adapter_row = lengths[0], groups[0], adapter_of_request[0]
    ends = jnp.cumsum(length_row)
    starts = ends - length_row
    request = jnp.sum((ends[None, :] <= position[:, None]).astype(jnp.int32), axis=1)
    same = group_row[:, None] == group_row[None, :]
    group_first = jnp.min(jnp.where(same, starts[None, :], total), axis=1)
    slot_of_request = lookup(adapter_row, adapter_slot)
    group = lookup(request, group_row)
    rope_pos = position - lookup(request, group_first)
    slot = lookup(request, slot_of_request)
    meta_row = jnp.stack([slot, group, position] + [position] * 5, axis=0).astype(F32)
    freq = jnp.exp(
        -jnp.arange(head_length // 2, dtype=F32) * (2.0 * math.log(ROPE_BASE) / head_length)
    )
    angle = rope_pos.astype(F32)[:, None] * freq[None, :]
    cosine, sine = jnp.cos(angle), jnp.sin(angle)
    cosine = jnp.concatenate([cosine, cosine], axis=1)
    sine = jnp.concatenate([-sine, sine], axis=1)

    up_kv = lax.dynamic_index_in_dim(
        key_value_up_factors.reshape(adapters, rank, kv_heads, 2, head_length), head, 2, keepdims=False
    )
    up = jnp.concatenate(
        [
            jnp.pad(query_up_factors, ((0, 0), (0, 2 * rank), (0, 0))),
            jnp.pad(up_kv[:, :, 0], ((0, 0), (rank, rank), (0, 0))),
            jnp.pad(up_kv[:, :, 1], ((0, 0), (2 * rank, 0), (0, 0))),
        ],
        axis=2,
    ).reshape(adapters * ranks, query_cols + 2 * head_length)

    weights = (
        attn_gain.reshape(1, -1),
        query_weight,
        up,
        q_gain.reshape(1, -1),
        k_gain.reshape(1, -1),
        shrink_o.reshape(adapters * rank, query_cols),
        w_o,
        expand_o.reshape(adapters * rank, width),
    )
    meta = (meta_row, cosine, sine)
    half = held // 2
    half_own = lax.dynamic_slice_in_dim(shrink_qkv, core * half, half, 0)
    halves = []
    for r in range(1, holders):
        top = 1 << (r.bit_length() - 1)
        halves.append(swap_holder(half_own if r == top else halves[r - top - 1], holders, top))
    spots = [chip, core, holder * held]
    for r in range(1, holders):
        begin = (holder ^ r) * held
        spots += [begin + core * half, begin + (1 - core) * half]
    spots = jnp.stack(spots).astype(jnp.int32)
    cuts = [
        lax.dynamic_index_in_dim(w_kv, 2 * (chip ^ j) * kv_heads // parts, 1, keepdims=False)
        for j in range(chips)
    ]

    def between(blocks):
        nonlocal cuts, meta
        blocks, halves[:2], cuts, meta = lax.optimization_barrier(
            (blocks, halves[:2], cuts, meta)
        )
        return blocks

    gathered = gather_blocks(tokens, parts, between)
    mine = [cuts[0]] + [swap_chips(cuts[j], parts, j) for j in range(1, chips)]
    mine = jnp.stack(mine)
    mine, weights, spots = lax.optimization_barrier((mine, weights, spots))
    head_parts = [mine, other_core(mine, parts)]
    pieces = [shrink_qkv]
    for got in halves:
        pieces += [got, other_core(got, parts)]
    own, part, entries = attention(
        spots,
        gathered,
        weights,
        meta,
        pieces,
        head_parts,
        adapters,
    )
    left, right = scatter_terms(own, part, parts)

    attn_own, moe_own = residual_norm(tokens, moe_gain, left, right)

    moe_own, entries, starts, length_row, page_table, expert_ids, expert_gates = (
        lax.optimization_barrier(
            (moe_own, entries, starts, length_row, page_table, expert_ids, expert_gates)
        )
    )

    local_cols = kv_width // parts
    kept = lax.dynamic_slice_in_dim(
        entries, place * local_cols - head * 2 * head_length, local_cols, 1
    )
    page_row = page_table[0]
    per_request = page_row.shape[0] // length_row.shape[0]
    offset = PAGE * jnp.arange(per_request, dtype=jnp.int32)[None, :]
    page_first = (starts[:, None] + offset).reshape(-1)
    page_length = jnp.clip(length_row[:, None] - offset, 0, PAGE).reshape(-1)
    kv_pages = fill_pages(page_first, page_length, page_row, to_group(kept, chip, core, chips))

    capacity = CAP_DEV * parts
    ids = to_device(expert_ids, chip, core, chips)
    gates = to_device(expert_gates, chip, core, chips)
    share = gates / jnp.sum(gates, axis=1, keepdims=True)
    own_experts = place * experts + jnp.arange(experts, dtype=jnp.int32)
    chosen = ids[:, :, None] == own_experts[None, None, :]
    hit = jnp.any(chosen, axis=1)
    weight = jnp.sum(jnp.where(chosen, share[:, :, None], 0.0), axis=1)
    block = line // own_rows
    earlier = (line[:, None] > line[None, :]) & (block[:, None] == block[None, :])
    before = dot(earlier.astype(BF16), hit.astype(BF16)).astype(jnp.int32)
    slot_in = jnp.where(hit, block[:, None] * CAP_DEV + before, -(1 << 20))

    routes = jnp.concatenate([slot_in.astype(F32).T, weight.T], axis=0)
    routes = jnp.pad(routes, ((0, -routes.shape[0] % 8), (0, 0)))

    def tables_first(blocks):
        nonlocal routes, kv_pages
        blocks, routes, kv_pages = lax.optimization_barrier((blocks, routes, kv_pages))
        return blocks

    gathered = gather_blocks(moe_own, parts, tables_first)
    own, part = expert_layer(routes, gathered, w_gate, w_up, w_down, capacity)
    left, right = scatter_terms(own, part, parts)

    moe_total = total_rows(left, right)
    return (attn_own, moe_total, kv_pages)


def solution(mesh):
    placed = (
        P(("dp", "tensor"), None),
        P(),
        P(),
        P(),
        P(),
        P(None, "tensor"),
        P("tensor", None, None),
        P("tensor", None),
        P("tensor", None, None),
        P("tensor", None, None),
        P("tensor", None, None),
        P("dp", None, None),
        P(None, None, "tensor"),
        P(None, None, "tensor"),
        P(),
        P(),
        P("dp", None),
        P("dp", None),
        P("dp", None),
        P(),
        P("dp", None),
        P("dp", None),
        P("dp", None),
    )
    return jax.shard_map(
        local,
        mesh=mesh,
        in_specs=placed,
        out_specs=(P(("dp", "tensor"), None), P(("dp", "tensor"), None), P("dp", "tensor", None)),
        check_vma=False,
    )
```
